32 devices in a mesh: seq: 8 (over y, x, core), fsdp: 4 (over z).
Axes of the slice: x: 2, y: 2, z: 4, core: 2. Of those that a mesh axis runs over, the one named last changes fastest.
Arguments:
- tokens: bfloat16 [4, 1024, 2048], P('fsdp', 'seq'), may hold values from -6 to 6
- positions: int32 [4, 1024], P('fsdp', 'seq'), may hold values from 0 to 511, as said below
- w_query: bfloat16 [2048, 2048], P('fsdp'), may hold values from -0.125 to 0.125
- w_key: bfloat16 [2048, 256], P('fsdp'), may hold values from -0.125 to 0.125
- w_value: bfloat16 [2048, 256], P('fsdp'), may hold values from -0.125 to 0.125
- w_out: bfloat16 [2048, 2048], P('fsdp'), may hold values from -2 to 2
- gain_attn: bfloat16 [2048], P('fsdp'), may hold values from 0.099609375 to 1.8984375
- w_gate: bfloat16 [2048, 5632], P('fsdp'), may hold values from -0.125 to 0.125
- w_up: bfloat16 [2048, 5632], P('fsdp'), may hold values from -0.125 to 0.125
- w_down: bfloat16 [5632, 2048], P('fsdp'), may hold values from -0.078125 to 0.078125
- gain_mlp: bfloat16 [2048], P('fsdp'), may hold values from 0.099609375 to 1.8984375
- cotangent: bfloat16 [4, 1024, 2048], P('fsdp', 'seq'), may hold values from -6 to 6
Outputs:
- layer_out: bfloat16 [4, 1024, 2048], P('fsdp', 'seq')
- grad_tokens: float32 [4, 1024, 2048], P('fsdp', 'seq')
- grad_query: float32 [2048, 2048], P('fsdp')
- grad_key: float32 [2048, 256], P('fsdp')
- grad_value: float32 [2048, 256], P('fsdp')
- grad_out: float32 [2048, 2048], P('fsdp')
- grad_gain_attn: float32 [2048], P('fsdp')
- grad_gate: float32 [2048, 5632], P('fsdp')
- grad_up: float32 [2048, 5632], P('fsdp')
- grad_down: float32 [5632, 2048], P('fsdp')
- grad_gain_mlp: float32 [2048], P('fsdp')
The draws below stay inside these ranges and needn't reach their ends.
Inputs may be any that keep to these rules, and one draw needn't show every extreme that they name: `positions`: within each sequence a position is 0 where a document starts and rises by one from token to token inside a document; documents start at the first token, at token 512 and at some later tokens, and the first document spans tokens 0 to 511.
All inputs are finite; a program needn't handle non-finite values.
Results may differ from the reference program's by a relative error of at most 0.018.
Values may be sent and summed in bfloat16 or wider, within the bound.
No kernel may reach another device: no remote copies, remote signals or barrier semaphores. Data moves between devices by JAX's collectives and lax.ppermute only.
A program may use at most 640 MiB of HBM per device.

```python
import math
import jax
import jax.numpy as jnp
from jax import lax

D = 2048
HEADS = 32
KV_HEADS = 4
HEAD_DIM = 64
FF = 5632
LEN = 1024
SEQS = 4
N_SEQ = 8


def draw_positions(key, part):
    key = jax.random.fold_in(key, 11)
    index = jnp.broadcast_to(jnp.arange(LEN, dtype=jnp.int32)[None, :], (SEQS, LEN))
    marks = jax.random.randint(key, (SEQS, LEN), 0, 256) == 0
    marks = marks & (index > LEN // 2) | (index == 0) | (index == LEN // 2)
    starts = jnp.where(marks, index, 0)
    starts = lax.cummax(starts, axis=1)
    return (index - starts).astype(jnp.int32)


def steps_of(own_key, shape, shards, least, top_value):
    loudness, own = 1.0, jax.random.fold_in(own_key, 6)
    for axis_at, parts in shards:
        draws = jnp.exp(jax.random.uniform(jax.random.fold_in(own, axis_at), (parts,), jnp.float32, least / len(shards), top_value / len(shards)))
        loudness = loudness * jnp.repeat(draws, shape[axis_at] // parts).reshape([-1 if axis == axis_at else 1 for axis in range(len(shape))])
    return loudness


def normal_values(own_key, dims, deviation, limit, split=(), kind=jnp.bfloat16):
    factor_of = steps_of(own_key, dims, split, -0.22, 0.18) if split else 1.0
    result = jax.random.normal(own_key, dims, jnp.float32) * deviation * factor_of
    return jnp.minimum(jnp.maximum(result, -limit), limit).astype(kind)


def setup_inputs(seed: int = 0) -> dict:
    arg_keys = jax.random.split(jax.random.key(seed), 13)
    tokens = normal_values(arg_keys[0], (SEQS, LEN, D), 1.0, 6.0, ((0, 4), (1, 8)))
    positions = draw_positions(jax.random.fold_in(arg_keys[12], 71), 0)
    w_query = normal_values(arg_keys[2], (D, HEADS * HEAD_DIM), D ** -0.5, 0.125, ((0, 4),))
    w_key = normal_values(arg_keys[3], (D, KV_HEADS * HEAD_DIM), D ** -0.5, 0.125, ((0, 4),))
    w_value = normal_values(arg_keys[4], (D, KV_HEADS * HEAD_DIM), D ** -0.5, 0.125, ((0, 4),))
    w_out = normal_values(arg_keys[5], (HEADS * HEAD_DIM, D), (max(D // 256, 1)) ** -0.5, 2.0, ((0, 4),))
    gain_attn = jnp.clip(1.0 + 0.18 * jax.random.normal(arg_keys[6], (D,), jnp.float32), 0.099609375, 1.8984375).astype(jnp.bfloat16)
    w_gate = normal_values(arg_keys[7], (D, FF), D ** -0.5, 0.125, ((0, 4),))
    w_up = normal_values(arg_keys[8], (D, FF), D ** -0.5, 0.125, ((0, 4),))
    w_down = normal_values(arg_keys[9], (FF, D), FF ** -0.5, 0.078125, ((0, 4),))
    gain_mlp = jnp.clip(1.0 + 0.18 * jax.random.normal(arg_keys[10], (D,), jnp.float32), 0.099609375, 1.8984375).astype(jnp.bfloat16)
    cotangent = normal_values(arg_keys[11], (SEQS, LEN, D), 1.0, 6.0, ((0, 4), (1, 8)))
    return dict(tokens=tokens, positions=positions, w_query=w_query, w_key=w_key, w_value=w_value, w_out=w_out, gain_attn=gain_attn, w_gate=w_gate, w_up=w_up, w_down=w_down, gain_mlp=gain_mlp, cotangent=cotangent)


EPS = 1e-05
ROPE_BASE = 10000.0

@jax.custom_vjp
def low(v):
    return lax.optimization_barrier(v.astype(jnp.bfloat16)).astype(jnp.float32)

@jax.custom_vjp
def low_back(v):
    return v

def low_keep(v):
    return (low(v), None)

def low_pass(kept, grad):
    return (grad,)

def back_keep(v):
    return (v, None)

def back_low(kept, grad):
    return (low(grad),)
low.defvjp(low_keep, low_pass)
low_back.defvjp(back_keep, back_low)

def matmul(left_rows, right_rows):
    return jnp.dot(left_rows, right_rows, precision=lax.Precision.HIGHEST, preferred_element_type=jnp.float32)

def rope_tables(positions, head_size):
    half_dim = head_size // 2
    freqs_base = jnp.exp(jnp.arange(half_dim, dtype=jnp.float32) * (-2.0 * math.log(ROPE_BASE) / head_size))
    angles = positions.astype(jnp.float32)[..., None] * freqs_base
    return (jnp.cos(angles), jnp.sin(angles))

def rotate(values, cosine, sine_table):
    half_dim = values.shape[-1] // 2
    lower_half = values[..., :half_dim]
    upper_half = values[..., half_dim:]
    cos_part = cosine[:, None, :]
    sin_part = sine_table[:, None, :]
    return jnp.concatenate([lower_half * cos_part - upper_half * sin_part, upper_half * cos_part + lower_half * sin_part], axis=-1)

def rms_norm(values, gain):
    inverse = lax.rsqrt(lax.optimization_barrier(jnp.mean(values * values, axis=-1, keepdims=True)) + EPS)
    return values * inverse * gain

def attend_block(query_block, start, key_copies, value_copies):
    key_heads = jnp.repeat(key_copies, HEADS // N_SEQ, axis=1)
    value_heads = jnp.repeat(value_copies, HEADS // N_SEQ, axis=1)
    scores = jnp.einsum('qhd,khd->hqk', query_block, key_heads, precision=lax.Precision.HIGHEST) * HEAD_DIM ** (-0.5)
    scores = low_back(scores)
    block_rows = query_block.shape[0]
    causal = jnp.arange(LEN, dtype=jnp.int32)[None, :] <= (start + jnp.arange(block_rows, dtype=jnp.int32))[:, None]
    scores = jnp.where(causal[None], scores, -jnp.inf)
    row_max = lax.optimization_barrier(jnp.max(scores, axis=-1, keepdims=True))
    unnormed = jnp.exp(scores - row_max)
    row_sum = lax.optimization_barrier(jnp.sum(unnormed, axis=-1))
    accum = jnp.einsum('hqk,khd->qhd', low(unnormed), value_heads, precision=lax.Precision.HIGHEST)
    accum = low_back(accum)
    return accum / jnp.transpose(row_sum)[:, :, None]

def layer(sequence, cosine, sine_table, w_query, w_key, w_value, w_out, gain_attn, w_gate, w_up, w_down, gain_mlp):
    normed_in = low(rms_norm(sequence, gain_attn))
    query_pre = low_back(matmul(normed_in, w_query)).reshape(LEN, HEADS, HEAD_DIM)
    query = low(low_back(rotate(query_pre, cosine, sine_table)))
    key_pre = low_back(matmul(normed_in, w_key)).reshape(LEN, KV_HEADS, HEAD_DIM)
    keys = low(rotate(key_pre, cosine, sine_table))
    key_copies = low_back(jnp.repeat(keys, N_SEQ // KV_HEADS, axis=1))
    values = low(low_back(matmul(normed_in, w_value))).reshape(LEN, KV_HEADS, HEAD_DIM)
    value_copies = low_back(jnp.repeat(values, N_SEQ // KV_HEADS, axis=1))
    block = 512 if LEN % 512 == 0 else LEN

    def one_block(block_args):
        return attend_block(block_args[0], block_args[1], key_copies, value_copies)
    starts = jnp.arange(LEN // block, dtype=jnp.int32) * block
    attended = lax.map(jax.checkpoint(one_block), (query.reshape(LEN // block, block, HEADS, HEAD_DIM), starts))
    attended = low(low_back(attended.reshape(LEN, HEADS * HEAD_DIM)))
    middle = sequence + low_back(matmul(attended, w_out))
    normed_mid = low(rms_norm(middle, gain_mlp))
    gate = low_back(matmul(normed_mid, w_gate))
    upper = low_back(matmul(normed_mid, w_up))
    hidden = low(jax.nn.silu(gate) * upper)
    return middle + matmul(hidden, w_down)

def reference(tokens, positions, w_query, w_key, w_value, w_out, gain_attn, w_gate, w_up, w_down, gain_mlp, cotangent):
    cosine, sine_table = rope_tables(positions, HEAD_DIM)
    weights = [w.astype(jnp.float32) for w in (w_query, w_key, w_value, w_out, gain_attn, w_gate, w_up, w_down, gain_mlp)]

    def forward(stream, *params):

        def step(carried, inputs):
            return (carried, layer(inputs[0], inputs[1], inputs[2], *params))
        _, outputs = lax.scan(step, jnp.zeros((), jnp.float32), (stream, cosine, sine_table))
        return outputs
    outputs, pullback = jax.vjp(forward, tokens.astype(jnp.float32), *weights)
    grads = pullback(cotangent.astype(jnp.float32))
    return (outputs.astype(jnp.bfloat16), grads[0], grads[1], grads[2], grads[3], grads[4], grads[5], grads[6], grads[7], grads[8], grads[9])
```

```python
import math

import jax
import jax.numpy as jnp
from jax import lax
from jax.sharding import PartitionSpec as P

HEADS = 32
KV_HEADS = 4
HEAD_DIM = 64


EPS = 1e-05
ROPE_BASE = 10000.0


def rope_tables(positions, head_size):
    half_dim = head_size // 2
    freqs_base = jnp.exp(
        jnp.arange(half_dim, dtype=jnp.float32) * (-2.0 * math.log(ROPE_BASE) / head_size)
    )
    angles = positions.astype(jnp.float32)[..., None] * freqs_base
    return (jnp.cos(angles), jnp.sin(angles))


def rotate(values, cosine, sine_table):
    half_dim = values.shape[-1] // 2
    lower_half = values[..., :half_dim]
    upper_half = values[..., half_dim:]
    cos_part = cosine[:, None, :]
    sin_part = sine_table[:, None, :]
    return jnp.concatenate(
        [
            lower_half * cos_part - upper_half * sin_part,
            upper_half * cos_part + lower_half * sin_part,
        ],
        axis=-1,
    )


def unrotate(values, cosine, sine_table):
    return rotate(values, cosine, -sine_table)


def norm_back(grad_normed, normed, inverse):
    return inverse * (grad_normed - normed * jnp.mean(grad_normed * normed, axis=-1, keepdims=True))


def dot(left, right, dims):
    return lax.dot_general(left, right, ((dims[0], dims[1]), ((), ())), preferred_element_type=jnp.float32)


def swap(value, mask):
    return lax.ppermute(value, "seq", [(i, i ^ mask) for i in range(lax.axis_size("seq"))])


def seq_gather(part):
    n = lax.axis_size("seq")
    if n == 8:
        half = part.shape[0] // 2
        by_x, by_y = swap(part, 2), swap(part, 4)
        far = jnp.concatenate([swap(by_x[:half], 4), swap(by_y[half:], 2)])
        mine = jnp.stack([part, by_x, by_y, far])
    else:
        mine, mask = part[None], 2
        while mask < n:
            mine = jnp.concatenate([mine, swap(mine, mask)])
            mask *= 2
    return jnp.concatenate([mine, swap(mine, 1)])


def seq_scatter(parts):
    n = lax.axis_size("seq")

    def add(own, other):
        return own.astype(jnp.float32) + other.astype(jnp.float32)

    low = jnp.bfloat16
    mine = add(parts[: n // 2], swap(parts[n // 2 :], 1))
    if n == 8:
        half = parts.shape[1] // 2
        far = mine[3].astype(low)
        from_x, from_y = swap(far[:half], 2), swap(far[half:], 4)
        to_y = jnp.concatenate([add(mine[2][:half], from_x), mine[2][half:]]).astype(low)
        to_x = jnp.concatenate([mine[1][:half], add(mine[1][half:], from_y)]).astype(low)
        return mine[0] + swap(to_x, 2).astype(jnp.float32) + swap(to_y, 4).astype(jnp.float32)
    mask = n // 2
    while mask > 1:
        count = mine.shape[0] // 2
        mine = add(mine[:count], swap(mine[count:].astype(low), mask))
        mask //= 2
    return mine[0]


def flips(stacked, axis):
    shape, n, bit = stacked.shape, stacked.shape[axis], 1
    place = lax.axis_index("seq")
    while bit < n:
        split = stacked.reshape(shape[:axis] + (n // (2 * bit), 2, bit) + shape[axis + 1 :])
        stacked = jnp.where((place & bit) != 0, jnp.flip(split, axis + 1), split).reshape(shape)
        bit *= 2
    return stacked


def to_absolute(slots, axis=0):
    shape, n = slots.shape, slots.shape[axis]
    split = slots.reshape(shape[:axis] + (2, n // 2) + shape[axis + 1 :])
    return flips(jnp.swapaxes(split, axis, axis + 1).reshape(shape), axis)


def to_slots(absolute, axis=0):
    shape, n = absolute.shape, absolute.shape[axis]
    split = flips(absolute, axis).reshape(shape[:axis] + (n // 2, 2) + shape[axis + 1 :])
    return jnp.swapaxes(split, axis, axis + 1).reshape(shape)


def seq_exchange(slots):
    n = lax.axis_size("seq")
    masks = [((k << 1) & (n - 1)) | (k // (n // 2)) for k in range(n)]
    return jnp.stack([slots[k] if mask == 0 else swap(slots[k], mask) for k, mask in enumerate(masks)])


def columns_of(weight, place, groups, shards):
    width = weight.shape[1] // (groups * shards)
    return jnp.concatenate(
        [
            lax.dynamic_slice_in_dim(weight, (f * groups + place) * width, width, 1)
            for f in range(shards)
        ],
        axis=1,
    )


def on_device(
    tokens,
    positions,
    w_query,
    w_key,
    w_value,
    w_out,
    gain_attn,
    w_gate,
    w_up,
    w_down,
    gain_mlp,
    cotangent,
):
    low, wide = jnp.bfloat16, jnp.float32
    groups = lax.axis_size("seq")
    shards = lax.axis_size("fsdp")
    place = lax.axis_index("seq")
    shard = lax.axis_index("fsdp")
    tok_rows, width = tokens.shape[1:]
    shard_rows = w_query.shape[0]
    heads_dev = HEADS // groups
    kv_copies = groups // KV_HEADS
    seq_len = tok_rows * groups
    q_cols = heads_dev * HEAD_DIM
    out_cols = width // groups
    ff = w_gate.shape[1]
    ff_dev = ff // groups
    scale = HEAD_DIM ** (-0.5)

    def z_gather(part):
        return lax.all_gather(part, "fsdp", axis=0, tiled=True)

    def z_scatter(part):
        return lax.psum_scatter(part, "fsdp", scatter_dimension=0, tiled=True)

    def columns(weight, start, count):
        return lax.dynamic_slice_in_dim(weight, start, count, 1)

    kv_head = place // kv_copies
    attn_full = z_gather(
        jnp.concatenate(
            [
                columns(w_query, place * q_cols, q_cols),
                columns(w_key, kv_head * HEAD_DIM, HEAD_DIM),
                columns(w_value, kv_head * HEAD_DIM, HEAD_DIM),
            ],
            axis=1,
        )
    )
    out_part = z_gather(columns(w_out, place * out_cols, out_cols))
    gate_full = z_gather(columns_of(w_gate, place, groups, shards))
    up_full = z_gather(columns_of(w_up, place, groups, shards))
    down_rows = w_down.shape[0] // groups
    down_full = z_gather(lax.dynamic_slice_in_dim(w_down, place * down_rows, down_rows, 0))
    gains = lax.all_gather(jnp.stack([gain_attn, gain_mlp]), "fsdp", axis=1, tiled=True)
    gain_in, gain_mid = gains[0].astype(wide), gains[1].astype(wide)

    own = tokens[0]
    stream = seq_gather(own).reshape(seq_len, width).astype(wide)
    dy = seq_gather(cotangent[0]).reshape(seq_len, width)
    where = seq_gather(positions).reshape(seq_len)
    cosine, sine_table = rope_tables(where, HEAD_DIM)
    inverse_all = lax.rsqrt(jnp.mean(stream * stream, axis=-1, keepdims=True) + EPS)
    normed_in = (stream * inverse_all * gain_in).astype(low)
    qkv = jnp.dot(normed_in, attn_full, preferred_element_type=wide)
    query_rot = rotate(qkv[:, :q_cols].reshape(seq_len, heads_dev, HEAD_DIM), cosine, sine_table)
    key_rot = rotate(qkv[:, None, q_cols : q_cols + HEAD_DIM], cosine, sine_table)
    qkv_rot = jnp.concatenate(
        [query_rot.reshape(seq_len, q_cols), key_rot[:, 0], qkv[:, q_cols + HEAD_DIM :]], axis=1
    ).astype(low)
    qkv_all = to_absolute(qkv_rot.reshape(groups, tok_rows, -1)).reshape(seq_len, -1)
    query_all = qkv_all[:, :q_cols].reshape(seq_len, heads_dev, HEAD_DIM)
    key_all = qkv_all[:, q_cols : q_cols + HEAD_DIM]
    value_all = qkv_all[:, q_cols + HEAD_DIM :]

    block = 512
    blocks = seq_len // block
    key_index = jnp.arange(seq_len, dtype=jnp.int32)
    starts = jnp.arange(blocks, dtype=jnp.int32) * block
    query_blocks = query_all.reshape(blocks, block, heads_dev, HEAD_DIM)

    def block_scores(query_block, start):
        scores = (
            jnp.einsum("qhd,kd->hqk", query_block, key_all, preferred_element_type=jnp.float32)
            * scale
        )
        causal = key_index[None, :] <= (start + jnp.arange(block, dtype=jnp.int32))[:, None]
        return jnp.where(causal[None], scores, -jnp.inf)

    def attend(block_args):
        query_block, start = block_args
        scores = block_scores(query_block, start)
        row_max = jnp.max(scores, axis=-1)
        unnormed = jnp.exp(scores - row_max[..., None])
        row_sum = jnp.sum(unnormed, axis=-1)
        accum = jnp.einsum(
            "hqk,kd->qhd",
            unnormed.astype(jnp.bfloat16),
            value_all,
            preferred_element_type=jnp.float32,
        )
        return (accum / jnp.transpose(row_sum)[:, :, None], row_max, row_sum)

    out_blocks, max_blocks, sum_blocks = lax.map(attend, (query_blocks, starts))
    attended_send = out_blocks.astype(low).reshape(groups, tok_rows, q_cols)
    attended_tok = (
        to_absolute(seq_exchange(to_slots(attended_send))).transpose(1, 0, 2).reshape(tok_rows, -1)
    )

    out_slots = seq_gather(out_part)
    stream_own = own.astype(wide)
    projected = jnp.einsum("to,soc->tsc", attended_tok, out_slots, preferred_element_type=wide)
    middle = stream_own + to_absolute(projected, 1).reshape(tok_rows, width)
    inverse_mid = lax.rsqrt(jnp.mean(middle * middle, axis=-1, keepdims=True) + EPS)
    unit_mid = middle * inverse_mid
    normed_mid = seq_gather((unit_mid * gain_mid).astype(low)).reshape(seq_len, width)

    gate_pre = jnp.dot(normed_mid, gate_full, preferred_element_type=wide)
    upper_pre = jnp.dot(normed_mid, up_full, preferred_element_type=wide)
    sigmoid_gate = jax.nn.sigmoid(gate_pre)
    activated = gate_pre * sigmoid_gate
    hidden = (activated * upper_pre).astype(low)
    down_term = jnp.dot(hidden, down_full, preferred_element_type=wide).astype(low)
    layer_out = (middle + seq_scatter(down_term.reshape(groups, tok_rows, width))).astype(low)

    grad_hidden = dot(dy, down_full, ((1,), (1,)))
    grad_gate_pre = (
        grad_hidden * upper_pre * (sigmoid_gate * (1.0 + gate_pre * (1.0 - sigmoid_gate)))
    ).astype(low)
    grad_upper = (grad_hidden * activated).astype(low)
    grad_normed_mid = (
        dot(grad_gate_pre, gate_full, ((1,), (1,))) + dot(grad_upper, up_full, ((1,), (1,)))
    ).astype(low)
    grad_normed_mid = seq_scatter(grad_normed_mid.reshape(groups, tok_rows, width))
    grad_layer = cotangent[0].astype(wide)
    grad_gain_mid = jnp.sum(grad_normed_mid * unit_mid, axis=0)
    grad_middle = norm_back(grad_normed_mid * gain_mid, unit_mid, inverse_mid) + grad_layer
    down_sum = z_scatter(dot(hidden, dy, ((0,), (0,))).astype(low))
    gate_sum = z_scatter(dot(normed_mid, grad_gate_pre, ((0,), (0,))).astype(low))
    up_sum = z_scatter(dot(normed_mid, grad_upper, ((0,), (0,))).astype(low))

    grad_proj = to_slots(grad_middle.astype(low).reshape(tok_rows, groups, out_cols), 1)
    grad_attended = jnp.einsum("tsc,soc->to", grad_proj, out_slots, preferred_element_type=wide)
    grad_attended = to_slots(grad_attended.astype(low).reshape(tok_rows, groups, q_cols), 1)
    grad_heads = to_absolute(seq_exchange(grad_attended.transpose(1, 0, 2)))
    grad_blocks = grad_heads.reshape(blocks, block, heads_dev, HEAD_DIM)

    def retrace(carried, block_args):
        query_block, grad_block, out_block, row_max, row_sum, start = block_args
        scores = block_scores(query_block, start)
        unnormed = jnp.exp(scores - row_max[..., None])
        grad_out_f = grad_block.astype(jnp.float32)
        grad_accum = (grad_out_f / jnp.transpose(row_sum)[:, :, None]).astype(jnp.bfloat16)
        grad_probs = jnp.einsum(
            "qhd,kd->hqk", grad_accum, value_all, preferred_element_type=jnp.float32
        )
        shift = jnp.transpose(jnp.sum(grad_out_f * out_block, axis=-1)) / row_sum
        grad_scores = (unnormed * (grad_probs - shift[..., None])).astype(jnp.bfloat16)
        grad_query_block = (
            jnp.einsum("hqk,kd->qhd", grad_scores, key_all, preferred_element_type=jnp.float32)
            * scale
        )
        grad_keys = (
            carried[0]
            + jnp.einsum(
                "hqk,qhd->kd", grad_scores, query_block, preferred_element_type=jnp.float32
            )
            * scale
        )
        grad_values = carried[1] + jnp.einsum(
            "hqk,qhd->kd",
            unnormed.astype(jnp.bfloat16),
            grad_accum,
            preferred_element_type=jnp.float32,
        )
        return ((grad_keys, grad_values), grad_query_block.astype(jnp.bfloat16))

    zeros_kv = jnp.zeros((seq_len, HEAD_DIM), jnp.float32)
    (grad_keys, grad_values), grad_query_blocks = lax.scan(
        retrace,
        (zeros_kv, zeros_kv),
        (query_blocks, grad_blocks, out_blocks, max_blocks, sum_blocks, starts),
    )
    grad_all = jnp.concatenate(
        [
            grad_query_blocks.reshape(seq_len, q_cols),
            grad_keys.astype(low),
            grad_values.astype(low),
        ],
        axis=1,
    )
    grad_all = to_slots(grad_all.reshape(groups, tok_rows, -1)).reshape(seq_len, -1).astype(wide)
    grad_q = unrotate(
        grad_all[:, :q_cols].reshape(seq_len, heads_dev, HEAD_DIM), cosine, sine_table
    )
    grad_k = unrotate(grad_all[:, None, q_cols : q_cols + HEAD_DIM], cosine, sine_table)
    grad_qkv = jnp.concatenate(
        [grad_q.reshape(seq_len, q_cols), grad_k[:, 0], grad_all[:, q_cols + HEAD_DIM :]], axis=1
    ).astype(low)
    grad_normed_in = dot(grad_qkv, attn_full, ((1,), (1,))).astype(low)
    grad_normed_in = seq_scatter(grad_normed_in.reshape(groups, tok_rows, width))
    inverse_in = lax.rsqrt(jnp.mean(stream_own * stream_own, axis=-1, keepdims=True) + EPS)
    unit_in = stream_own * inverse_in
    grad_gain_in = jnp.sum(grad_normed_in * unit_in, axis=0)
    grad_stream = norm_back(grad_normed_in * gain_in, unit_in, inverse_in) + grad_middle

    attended_all = seq_gather(attended_tok).reshape(seq_len, -1)
    grad_proj_cols = seq_exchange(grad_proj.transpose(1, 0, 2)).reshape(seq_len, out_cols)
    attn_sum = z_scatter(
        jnp.concatenate(
            [
                dot(normed_in, grad_qkv, ((0,), (0,))).astype(low),
                dot(attended_all, grad_proj_cols, ((0,), (0,))).astype(low),
            ],
            axis=1,
        )
    )

    def spread_columns(part, pieces):
        slots = to_absolute(seq_gather(part)).astype(wide)
        split = slots.reshape(groups, part.shape[0], pieces, -1)
        return split.transpose(1, 2, 0, 3).reshape(part.shape[0], -1)

    grad_down = to_absolute(seq_gather(down_sum)).reshape(w_down.shape).astype(wide)
    grad_gate = spread_columns(gate_sum, shards)
    grad_up = spread_columns(up_sum, shards)
    attn_slots = to_absolute(seq_gather(attn_sum)).astype(wide)

    def flat(part):
        return part.transpose(1, 0, 2).reshape(shard_rows, -1)

    grad_query = flat(attn_slots[:, :, :q_cols])
    grad_kv = attn_slots[:, :, q_cols : q_cols + 2 * HEAD_DIM].reshape(
        KV_HEADS, kv_copies, shard_rows, 2 * HEAD_DIM
    )
    grad_kv = jnp.sum(grad_kv, axis=1)
    grad_key = flat(grad_kv[:, :, :HEAD_DIM])
    grad_value = flat(grad_kv[:, :, HEAD_DIM:])
    grad_out = flat(attn_slots[:, :, q_cols + 2 * HEAD_DIM :])
    gain_sums = lax.psum(jnp.stack([grad_gain_in, grad_gain_mid]), ("seq", "fsdp"))
    gain_sums = lax.dynamic_slice_in_dim(gain_sums, shard * shard_rows, shard_rows, 1)
    return (
        layer_out[None],
        grad_stream[None],
        grad_query,
        grad_key,
        grad_value,
        grad_out,
        gain_sums[0],
        grad_gate,
        grad_up,
        grad_down,
        gain_sums[1],
    )


def solution(mesh):
    placed = (
        P("fsdp", "seq", None),
        P("fsdp", "seq"),
        P("fsdp", None),
        P("fsdp", None),
        P("fsdp", None),
        P("fsdp", None),
        P("fsdp"),
        P("fsdp", None),
        P("fsdp", None),
        P("fsdp", None),
        P("fsdp"),
        P("fsdp", "seq", None),
    )
    return jax.shard_map(
        on_device,
        mesh=mesh,
        in_specs=placed,
        out_specs=(
            P("fsdp", "seq", None),
            P("fsdp", "seq", None),
            P("fsdp", None),
            P("fsdp", None),
            P("fsdp", None),
            P("fsdp", None),
            P("fsdp"),
            P("fsdp", None),
            P("fsdp", None),
            P("fsdp", None),
            P("fsdp"),
        ),
        check_vma=False,
    )
```

```python
import math

import jax
import jax.numpy as jnp
from jax import lax
from jax.experimental import pallas as pl
from jax.experimental.pallas import tpu as pltpu
from jax.sharding import PartitionSpec as P

HEADS = 32
KV_HEADS = 4
HEAD_DIM = 64


EPS = 1e-05
ROPE_BASE = 10000.0


def rope_tables(positions, head_size):
    half_dim = head_size // 2
    lane = jnp.arange(128)
    freqs = jnp.exp(
        (lane % half_dim).astype(jnp.float32) * (-2.0 * math.log(ROPE_BASE) / head_size)
    )
    angles = positions.astype(jnp.float32)[..., None] * freqs
    sign = jnp.where(lane % head_size < half_dim, -1.0, 1.0)
    return jnp.cos(angles), jnp.sin(angles) * sign


def norm_back(grad_normed, normed, inverse):
    return inverse * (grad_normed - normed * jnp.mean(grad_normed * normed, axis=-1, keepdims=True))


def dot(left, right, dims):
    return lax.dot_general(left, right, ((dims[0], dims[1]), ((), ())), preferred_element_type=jnp.float32)


def swap(value, mask):
    return lax.ppermute(value, "seq", [(i, i ^ mask) for i in range(lax.axis_size("seq"))])


def place_pieces(pieces, places, shape):
    cols = shape[2]
    tile = 512 if cols % 512 == 0 else cols

    def kernel(*refs):
        for piece, (slot, row), ref in zip(pieces, places, refs):
            refs[-1][slot, row : row + piece.shape[0]] = ref[...]

    return pl.pallas_call(
        kernel,
        grid=(cols // tile,),
        out_shape=jax.ShapeDtypeStruct(shape, pieces[0].dtype),
        in_specs=[pl.BlockSpec((piece.shape[0], tile), lambda i: (0, i)) for piece in pieces],
        out_specs=pl.BlockSpec(shape[:2] + (tile,), lambda i: (0, 0, i)),
        compiler_params=pltpu.CompilerParams(vmem_limit_bytes=48 * 2**20),
        cost_estimate=pl.CostEstimate(flops=0, bytes_accessed=math.prod(shape) * 4, transcendentals=0),
    )(*pieces)


def even_pieces(part, *meanwhile):
    half = part.shape[0] // 32 * 16
    by_x, by_y = lax.optimization_barrier((swap(part, 2), swap(part, 4), meanwhile))[:2]
    far = lax.optimization_barrier((swap(by_x[:half], 4), swap(by_y[half:], 2)))
    return (part, by_x, by_y, *far), ((0, 0), (1, 0), (2, 0), (3, 0), (3, half))


def doubled(part):
    mine, mask = part[None], 2
    while mask < lax.axis_size("seq"):
        mine = jnp.concatenate([mine, swap(mine, mask)])
        mask *= 2
    return mine


def seq_halves(part, *meanwhile):
    if lax.axis_size("seq") == 8 and part.shape[0] % 16 == 0:
        pieces, places = even_pieces(part, *meanwhile)
        mine = place_pieces(pieces, places, (4,) + part.shape)
    else:
        mine = doubled(part)
    return mine, swap(mine, 1)


def after(value, *earlier):
    return lax.optimization_barrier((value, *earlier))[0]


def seq_gather(part, *meanwhile):
    mine, other = seq_halves(part, *meanwhile)
    if part.shape[0] % 16:
        return jnp.concatenate([mine, other])
    half, rows, cols = mine.shape
    tile = 512 if cols % 512 == 0 else cols

    def kernel(mine_ref, other_ref, out_ref):
        out_ref[:half] = mine_ref[...]
        out_ref[half:] = other_ref[...]

    return pl.pallas_call(
        kernel,
        grid=(cols // tile,),
        out_shape=jax.ShapeDtypeStruct((2 * half, rows, cols), part.dtype),
        in_specs=[pl.BlockSpec((half, rows, tile), lambda i: (0, 0, i))] * 2,
        out_specs=pl.BlockSpec((2 * half, rows, tile), lambda i: (0, 0, i)),
        cost_estimate=pl.CostEstimate(flops=0, bytes_accessed=mine.size * 8, transcendentals=0),
    )(mine, other)


def ring_sum(value):
    n = lax.axis_size("fsdp")
    moving = value
    for _ in range(n - 1):
        moving = lax.ppermute(moving, "fsdp", [(i, (i + 1) % n) for i in range(n)])
        value = value + moving
    return value


def ordered(place, even, odd, body):
    core = place & 1
    pl.when(core == 0)(lambda: body(even, odd))
    pl.when(core == 1)(lambda: body(odd, even))


def put_columns(even, odd, place, pieces, w_gate, w_up):
    half, rows, cols = even.shape
    n, w = 2 * half, cols // (2 * pieces)
    tile = 64

    def kernel(place_ref, even_ref, odd_ref, w_gate_ref, w_up_ref, gate_ref, up_ref, sums_ref):
        chip = place_ref[0] // 2

        def body(first, second):
            blocks = [(second if t % 2 else first)[(t // 2) ^ chip] for t in range(n)]
            sums = jnp.zeros((tile, 1), jnp.float32)
            for target, weight, start in ((gate_ref, w_gate_ref, 0), (up_ref, w_up_ref, cols // 2)):
                for f in range(pieces):
                    at, to = start + f * w, slice(f * n * w, (f + 1) * n * w)
                    row = jnp.concatenate([block[:, at : at + w] for block in blocks], axis=1)
                    row = row.astype(jnp.float32)
                    target[:, to] = row
                    sums += jnp.sum(row * weight[:, to].astype(jnp.float32), axis=1, keepdims=True)
            sums_ref[...] = sums

        ordered(place_ref[0], even_ref, odd_ref, body)

    spec = pl.BlockSpec((half, tile, cols), lambda i: (0, i, 0))
    wide = jax.ShapeDtypeStruct((rows, pieces * n * w), jnp.float32)
    return pl.pallas_call(
        kernel,
        grid=(rows // tile,),
        out_shape=(wide, wide, jax.ShapeDtypeStruct((rows, 1), jnp.float32)),
        in_specs=[pl.BlockSpec(memory_space=pltpu.SMEM), spec, spec]
        + [pl.BlockSpec((tile, pieces * n * w), lambda i: (i, 0))] * 2,
        out_specs=[pl.BlockSpec((tile, pieces * n * w), lambda i: (i, 0))] * 2
        + [pl.BlockSpec((tile, 1), lambda i: (i, 0))],
        compiler_params=pltpu.CompilerParams(vmem_limit_bytes=48 * 2**20),
        cost_estimate=pl.CostEstimate(flops=0, bytes_accessed=even.size * 12, transcendentals=0),
    )(place, even, odd, w_gate, w_up)


def put_rows(even, odd, place):
    half, rows, cols = even.shape
    tile = 256

    def kernel(place_ref, even_ref, odd_ref, out_ref):
        chip = place_ref[0] // 2

        def body(first, second):
            for t in range(2 * half):
                block = (second if t % 2 else first)[(t // 2) ^ chip]
                out_ref[t * rows : (t + 1) * rows, :] = block.astype(jnp.float32)

        ordered(place_ref[0], even_ref, odd_ref, body)

    spec = pl.BlockSpec((half, rows, tile), lambda i: (0, 0, i))
    return pl.pallas_call(
        kernel,
        grid=(cols // tile,),
        out_shape=jax.ShapeDtypeStruct((2 * half * rows, cols), jnp.float32),
        in_specs=[pl.BlockSpec(memory_space=pltpu.SMEM), spec, spec],
        out_specs=pl.BlockSpec((2 * half * rows, tile), lambda i: (0, i)),
        compiler_params=pltpu.CompilerParams(vmem_limit_bytes=48 * 2**20),
        cost_estimate=pl.CostEstimate(flops=0, bytes_accessed=even.size * 12, transcendentals=0),
    )(place, even, odd)


def put_attention(even, odd, place, weights, q_cols, out_cols):
    half, rows, cols = even.shape
    n, tile = 2 * half, 128
    copies = n // KV_HEADS
    sizes = (n * q_cols, KV_HEADS * HEAD_DIM, KV_HEADS * HEAD_DIM, n * out_cols)

    def kernel(place_ref, even_ref, odd_ref, wq_ref, wk_ref, wv_ref, *refs):
        query_ref, key_ref, value_ref, out_ref, sums_ref = refs
        chip = place_ref[0] // 2

        def body(first, second):
            blocks = [
                (second if t % 2 else first)[(t // 2) ^ chip].astype(jnp.float32) for t in range(n)
            ]
            for t, block in enumerate(blocks):
                query_ref[:, t * q_cols : (t + 1) * q_cols] = block[:, :q_cols]
                out_ref[:, t * out_cols : (t + 1) * out_cols] = block[:, cols - out_cols :]
            sums = [
                sum(block[:, q_cols : q_cols + 2 * HEAD_DIM] for block in blocks[h * copies : (h + 1) * copies])
                for h in range(KV_HEADS)
            ]
            key_ref[...] = jnp.concatenate([part[:, :HEAD_DIM] for part in sums], axis=1)
            value_ref[...] = jnp.concatenate([part[:, HEAD_DIM:] for part in sums], axis=1)
            sums_ref[...] = sum(
                jnp.sum(ref[...] * weight[...].astype(jnp.float32), axis=1, keepdims=True)
                for ref, weight in ((query_ref, wq_ref), (key_ref, wk_ref), (value_ref, wv_ref))
            )

        ordered(place_ref[0], even_ref, odd_ref, body)

    spec = pl.BlockSpec((half, tile, cols), lambda i: (0, i, 0))
    return pl.pallas_call(
        kernel,
        grid=(rows // tile,),
        out_shape=[jax.ShapeDtypeStruct((rows, size), jnp.float32) for size in (*sizes, 1)],
        in_specs=[pl.BlockSpec(memory_space=pltpu.SMEM), spec, spec]
        + [pl.BlockSpec((tile, size), lambda i: (i, 0)) for size in sizes[:3]],
        out_specs=[pl.BlockSpec((tile, size), lambda i: (i, 0)) for size in (*sizes, 1)],
        compiler_params=pltpu.CompilerParams(vmem_limit_bytes=48 * 2**20),
        cost_estimate=pl.CostEstimate(flops=0, bytes_accessed=even.size * 12, transcendentals=0),
    )(place, even, odd, *weights)


def seq_scatter(even, odd):
    n = lax.axis_size("seq")

    def add(own, other):
        return own.astype(jnp.float32) + other.astype(jnp.float32)

    low = jnp.bfloat16
    mine = add(even, swap(odd, 1))
    if n == 8:
        half = even.shape[1] // 2
        far = mine[3].astype(low)
        from_x, from_y = swap(far[:half], 2), swap(far[half:], 4)
        to_y = jnp.concatenate([add(mine[2][:half], from_x), mine[2][half:]]).astype(low)
        to_x = jnp.concatenate([mine[1][:half], add(mine[1][half:], from_y)]).astype(low)
        return mine[0] + swap(to_x, 2).astype(jnp.float32) + swap(to_y, 4).astype(jnp.float32)
    mask = n // 2
    while mask > 1:
        count = mine.shape[0] // 2
        mine = add(mine[:count], swap(mine[count:].astype(low), mask))
        mask //= 2
    return mine[0]


def slot_of(mask, n):
    return (mask >> 1) + (mask & 1) * (n // 2)


def split_columns(parts, place, n):
    rows = parts[0].shape[0]
    sizes = [part.shape[1] // n for part in parts]
    half, cols = n // 2, sum(sizes)

    def kernel(place_ref, *refs):
        for core, ref in enumerate(refs[-2:]):
            for k in range(half):
                block, at = place_ref[0] ^ (2 * k + core), 0
                for size, part_ref in zip(sizes, refs):
                    start = pl.multiple_of(block * size, size)
                    ref[k, :, at : at + size] = part_ref[:, pl.ds(start, size)]
                    at += size

    vmem = pl.BlockSpec(memory_space=pltpu.VMEM)
    return pl.pallas_call(
        kernel,
        out_shape=[jax.ShapeDtypeStruct((half, rows, cols), parts[0].dtype)] * 2,
        in_specs=[pl.BlockSpec(memory_space=pltpu.SMEM)] + [vmem] * len(parts),
        out_specs=[vmem] * 2,
    )(place, *parts)


def seq_exchange(even, odd):
    half, rows, cols = even.shape
    other = swap(odd, 1)

    def kernel(even_ref, other_ref, *refs):
        for k, ref in enumerate(refs):
            ref[0] = even_ref[k]
            ref[1] = other_ref[k]

    vmem = pl.BlockSpec(memory_space=pltpu.VMEM)
    pairs = pl.pallas_call(
        kernel,
        out_shape=[jax.ShapeDtypeStruct((2, rows, cols), even.dtype)] * half,
        in_specs=[vmem] * 2,
        out_specs=[vmem] * half,
    )(even, other)
    return [pair if k == 0 else swap(pair, 2 * k) for k, pair in enumerate(pairs)]


def join_columns(pairs, place):
    n, (_, rows, cols) = 2 * len(pairs), pairs[0].shape

    def kernel(place_ref, *refs):
        for k, ref in enumerate(refs[:-1]):
            for core in range(2):
                start = pl.multiple_of((place_ref[0] ^ (2 * k + core)) * cols, cols)
                refs[-1][:, pl.ds(start, cols)] = ref[core]

    vmem = pl.BlockSpec(memory_space=pltpu.VMEM)
    return pl.pallas_call(
        kernel,
        out_shape=jax.ShapeDtypeStruct((rows, n * cols), pairs[0].dtype),
        in_specs=[pl.BlockSpec(memory_space=pltpu.SMEM)] + [vmem] * len(pairs),
        out_specs=vmem,
    )(place, *pairs)


def join_weight(even, odd, place):
    half, rows, cols = even.shape
    n, tile = 2 * half, 512

    def kernel(place_ref, even_ref, odd_ref, out_ref):
        for ref, core in ((even_ref, 0), (odd_ref, 1)):
            for k in range(half):
                start = pl.multiple_of((place_ref[0] ^ (2 * k + core)) * cols, cols)
                out_ref[:, pl.ds(start, cols)] = ref[k]

    spec = pl.BlockSpec((half, tile, cols), lambda i: (0, i, 0))
    return pl.pallas_call(
        kernel,
        grid=(rows // tile,),
        out_shape=jax.ShapeDtypeStruct((rows, n * cols), even.dtype),
        in_specs=[pl.BlockSpec(memory_space=pltpu.SMEM), spec, spec],
        out_specs=pl.BlockSpec((tile, n * cols), lambda i: (i, 0)),
        compiler_params=pltpu.CompilerParams(vmem_limit_bytes=48 * 2**20),
        cost_estimate=pl.CostEstimate(flops=0, bytes_accessed=even.size * 8, transcendentals=0),
    )(place, even, odd)


def lanes(shape):
    return lax.broadcasted_iota(jnp.int32, shape, 1)


def halves_swapped(value):
    first = lanes(value.shape) % HEAD_DIM < HEAD_DIM // 2
    size = value.shape[1]
    left, right = pltpu.roll(value, size - HEAD_DIM // 2, 1), pltpu.roll(value, HEAD_DIM // 2, 1)
    return jnp.where(first, left, right)


def turned(value, cosine, sine):
    parts = [
        value[:, i : i + 128] * cosine + halves_swapped(value[:, i : i + 128]) * sine
        for i in range(0, value.shape[1], 128)
    ]
    return jnp.concatenate(parts, axis=1)


def key_copies(key_value):
    first = lanes(key_value.shape) < HEAD_DIM
    turned_over = pltpu.roll(key_value, HEAD_DIM, 1)
    keys = jnp.where(first, key_value, turned_over)
    values = jnp.where(first, turned_over, key_value)
    return keys, values, first


def only(value, head):
    first = lanes(value.shape) < HEAD_DIM
    return jnp.where(first if head == 0 else ~first, value, jnp.zeros_like(value))


def matmul(left, right, dims):
    return lax.dot_general(left, right, (dims, ((), ())), preferred_element_type=jnp.float32)


ROWS_OF = ((1,), (1,))
PLAIN = ((1,), (0,))
COLUMNS_OF = ((0,), (0,))
MASKED = -1e30


def attention(qkv, cosine, sine, place, heads_dev):
    n, rows, cols = qkv.shape
    length, q_cols = n * rows, heads_dev * HEAD_DIM
    block = 256
    low, wide = jnp.bfloat16, jnp.float32

    def kernel(place_ref, qkv_ref, cos_ref, sin_ref, *refs):
        even_ref, odd_ref, out_ref, rot_ref, top_ref, sum_ref = refs
        for t in range(n):
            slot = slot_of(place_ref[0] ^ t, n)
            value = qkv_ref[slot]
            moved = turned(value[:, : q_cols + 128], cos_ref[slot], sin_ref[slot])
            key_value = jnp.where(
                lanes((rows, 128)) < HEAD_DIM, moved[:, q_cols:], value[:, q_cols:]
            )
            at = slice(t * rows, (t + 1) * rows)
            rot_ref[at, :q_cols] = moved[:, :q_cols].astype(low)
            rot_ref[at, q_cols:] = key_value.astype(low)
        for i in range(length // block):
            span = (i + 1) * block
            key_value = rot_ref[:span, q_cols:]
            keys, values, _ = key_copies(key_value)
            held = [only(values, 0), only(values, 1)]
            shape = (block, span)
            seen = lax.broadcasted_iota(jnp.int32, shape, 1) <= i * block + (
                lax.broadcasted_iota(jnp.int32, shape, 0)
            )
            at = slice(i * block, (i + 1) * block)
            for pair in range(q_cols // 128):
                query = rot_ref[at, pair * 128 : (pair + 1) * 128] * jnp.asarray(0.125, low)
                total = None
                for head in range(2):
                    scores = matmul(only(query, head), keys, ROWS_OF)
                    scores = jnp.where(seen, scores, MASKED)
                    top = jnp.max(scores, axis=1, keepdims=True)
                    unnormed = jnp.exp(scores - top)
                    row_sum = jnp.sum(unnormed, axis=1, keepdims=True)
                    part = matmul(unnormed.astype(low), held[head], PLAIN) / row_sum
                    top_ref[2 * pair + head, at, :] = top
                    sum_ref[2 * pair + head, at, :] = row_sum
                    total = part if total is None else total + part
                out_ref[at, pair * 128 : (pair + 1) * 128] = total
        for core, ref in ((0, even_ref), (1, odd_ref)):
            for k in range(n // 2):
                start = pl.multiple_of((place_ref[0] ^ (2 * k + core)) * rows, rows)
                ref[k] = out_ref[pl.ds(start, rows), :].astype(low)

    vmem = pl.BlockSpec(memory_space=pltpu.VMEM)
    results = pl.pallas_call(
        kernel,
        out_shape=[jax.ShapeDtypeStruct((n // 2, rows, q_cols), low)] * 2
        + [
            jax.ShapeDtypeStruct((length, q_cols), wide),
            jax.ShapeDtypeStruct((length, q_cols + 2 * HEAD_DIM), low),
            jax.ShapeDtypeStruct((heads_dev, length, 1), wide),
            jax.ShapeDtypeStruct((heads_dev, length, 1), wide),
        ],
        in_specs=[pl.BlockSpec(memory_space=pltpu.SMEM)] + [vmem] * 3,
        out_specs=[vmem] * 6,
        compiler_params=pltpu.CompilerParams(vmem_limit_bytes=48 * 2**20),
        cost_estimate=pl.CostEstimate(
            flops=2 * length * length * 128 * heads_dev,
            bytes_accessed=qkv.size * 8,
            transcendentals=length * length * heads_dev // 2,
        ),
    )(place, qkv, cosine, sine)
    return results[:2], *results[2:]


def attention_back(grads, rotated, out, tops, sums, cosine, sine, place):
    n, (_, rows, all_cols) = 2 * len(grads), grads[0].shape
    length, cols = rotated.shape
    q_cols = cols - 2 * HEAD_DIM
    heads_dev = q_cols // HEAD_DIM
    block = 256
    low, wide = jnp.bfloat16, jnp.float32

    def kernel(place_ref, rot_ref, out_ref, top_ref, sum_ref, cos_ref, sin_ref, *refs):
        grad_refs = refs[: n // 2]
        result_ref, others_ref, grad_ref, dq_ref, dk_ref, dv_ref = refs[n // 2 :]
        for k, ref in enumerate(grad_refs):
            for core in range(2):
                start = pl.multiple_of((place_ref[0] ^ (2 * k + core)) * rows, rows)
                grad_ref[pl.ds(start, rows), :] = ref[core, :, :q_cols]
                others_ref[core * (n // 2) + k] = ref[core, :, q_cols:]
        dk_ref[...] = jnp.zeros_like(dk_ref)
        dv_ref[...] = jnp.zeros_like(dv_ref)
        for i in range(length // block):
            span = (i + 1) * block
            keys, values, _ = key_copies(rot_ref[:span, q_cols:])
            held = [only(keys, 0), only(keys, 1)]
            shape = (block, span)
            seen = lax.broadcasted_iota(jnp.int32, shape, 1) <= i * block + (
                lax.broadcasted_iota(jnp.int32, shape, 0)
            )
            at = slice(i * block, (i + 1) * block)
            dk = dv = None
            for pair in range(q_cols // 128):
                pair_at = slice(pair * 128, (pair + 1) * 128)
                query = rot_ref[at, pair_at] * jnp.asarray(0.125, low)
                grad = grad_ref[at, pair_at].astype(wide)
                product = grad * out_ref[at, pair_at]
                dq = None
                for head in range(2):
                    row_sum = sum_ref[2 * pair + head, at, :]
                    own_query = only(query, head)
                    own_grad = only((grad / row_sum).astype(low), head)
                    scores = jnp.where(seen, matmul(own_query, keys, ROWS_OF), MASKED)
                    unnormed = jnp.exp(scores - top_ref[2 * pair + head, at, :])
                    shift = jnp.sum(only(product, head), axis=1, keepdims=True) / row_sum
                    grad_probs = matmul(own_grad, values, ROWS_OF)
                    grad_scores = (unnormed * (grad_probs - shift)).astype(low)
                    dq_part = matmul(grad_scores, held[head], PLAIN)
                    dk_part = matmul(grad_scores, own_query, COLUMNS_OF)
                    dv_part = matmul(unnormed.astype(low), own_grad, COLUMNS_OF)
                    dq = dq_part if dq is None else dq + dq_part
                    dk = dk_part if dk is None else dk + dk_part
                    dv = dv_part if dv is None else dv + dv_part
                dq_ref[at, pair_at] = dq * 0.125
            dk_ref[:span, :] += dk
            dv_ref[:span, :] += dv
        for t in range(n):
            slot = slot_of(place_ref[0] ^ t, n)
            at = slice(t * rows, (t + 1) * rows)
            dk, dv = dk_ref[at, :], dv_ref[at, :]
            first = lanes(dk.shape) < HEAD_DIM
            dk, dv = dk + pltpu.roll(dk, HEAD_DIM, 1), dv + pltpu.roll(dv, HEAD_DIM, 1)
            moved = turned(
                jnp.concatenate([dq_ref[at, :], dk], axis=1), cos_ref[slot], -sin_ref[slot]
            )
            result_ref[slot, :, :q_cols] = moved[:, :q_cols].astype(low)
            result_ref[slot, :, q_cols:] = jnp.where(first, moved[:, q_cols:], dv).astype(low)

    vmem = pl.BlockSpec(memory_space=pltpu.VMEM)
    return pl.pallas_call(
        kernel,
        out_shape=[
            jax.ShapeDtypeStruct((n, rows, cols), low),
            jax.ShapeDtypeStruct((n, rows, all_cols - q_cols), low),
        ],
        in_specs=[pl.BlockSpec(memory_space=pltpu.SMEM)] + [vmem] * (6 + n // 2),
        out_specs=[vmem] * 2,
        scratch_shapes=[
            pltpu.VMEM((length, q_cols), low),
            pltpu.VMEM((length, q_cols), wide),
            pltpu.VMEM((length, 128), wide),
            pltpu.VMEM((length, 128), wide),
        ],
        compiler_params=pltpu.CompilerParams(vmem_limit_bytes=48 * 2**20),
        cost_estimate=pl.CostEstimate(
            flops=5 * length * length * 128 * heads_dev,
            bytes_accessed=rotated.size * 8,
            transcendentals=length * length * heads_dev // 2,
        ),
    )(place, rotated, out, tops, sums, cosine, sine, *grads)


def silu_parts(gate):
    sigmoid_gate = 1.0 / (1.0 + jnp.exp(-gate))
    return sigmoid_gate, gate * sigmoid_gate


def hidden_units(normed, weights):
    rows, width = normed.shape
    cols = weights.shape[1]
    tile, ff_dev = 256, cols // 2

    def kernel(normed_ref, weights_ref, pre_ref, hidden_ref):
        pre = matmul(normed_ref[...], weights_ref[...], PLAIN)
        pre_ref[...] = pre
        hidden_ref[...] = (silu_parts(pre[:, :ff_dev])[1] * pre[:, ff_dev:]).astype(jnp.bfloat16)

    return pl.pallas_call(
        kernel,
        grid=(rows // tile,),
        out_shape=[
            jax.ShapeDtypeStruct((rows, cols), jnp.float32),
            jax.ShapeDtypeStruct((rows, ff_dev), jnp.bfloat16),
        ],
        in_specs=[
            pl.BlockSpec((tile, width), lambda i: (i, 0)),
            pl.BlockSpec((width, cols), lambda i: (0, 0)),
        ],
        out_specs=[
            pl.BlockSpec((tile, cols), lambda i: (i, 0)),
            pl.BlockSpec((tile, ff_dev), lambda i: (i, 0)),
        ],
        compiler_params=pltpu.CompilerParams(vmem_limit_bytes=48 * 2**20),
        cost_estimate=pl.CostEstimate(
            flops=2 * rows * width * cols, bytes_accessed=rows * cols * 8, transcendentals=rows * ff_dev
        ),
    )(normed, weights)


def hidden_back(dy, down, pre):
    rows, width = dy.shape
    ff_dev = down.shape[0]
    tile = 256

    def kernel(dy_ref, down_ref, pre_ref, out_ref):
        grad_hidden = matmul(dy_ref[...], down_ref[...], ROWS_OF)
        gate, upper = pre_ref[:, :ff_dev], pre_ref[:, ff_dev:]
        sigmoid_gate, activated = silu_parts(gate)
        grad_gate = grad_hidden * upper * (sigmoid_gate * (1.0 + gate * (1.0 - sigmoid_gate)))
        both = jnp.concatenate([grad_gate, grad_hidden * activated], axis=1)
        out_ref[...] = both.astype(jnp.bfloat16)

    return pl.pallas_call(
        kernel,
        grid=(rows // tile,),
        out_shape=jax.ShapeDtypeStruct((rows, 2 * ff_dev), jnp.bfloat16),
        in_specs=[
            pl.BlockSpec((tile, width), lambda i: (i, 0)),
            pl.BlockSpec((ff_dev, width), lambda i: (0, 0)),
            pl.BlockSpec((tile, 2 * ff_dev), lambda i: (i, 0)),
        ],
        out_specs=pl.BlockSpec((tile, 2 * ff_dev), lambda i: (i, 0)),
        compiler_params=pltpu.CompilerParams(vmem_limit_bytes=48 * 2**20),
        cost_estimate=pl.CostEstimate(
            flops=2 * rows * width * ff_dev, bytes_accessed=rows * ff_dev * 16, transcendentals=rows * ff_dev
        ),
    )(dy, down, pre)


def attention_terms(normed, grad_qkv, attended, grad_proj):
    rows, width = normed.shape
    sizes = grad_qkv.shape[1], grad_proj.shape[1]
    tile = 512

    def kernel(normed_ref, grad_qkv_ref, attended_ref, grad_proj_ref, out_ref):
        low = jnp.bfloat16
        out_ref[:, : sizes[0]] = matmul(normed_ref[...], grad_qkv_ref[...], COLUMNS_OF).astype(low)
        out_ref[:, sizes[0] :] = matmul(attended_ref[...], grad_proj_ref[...], COLUMNS_OF).astype(low)

    return pl.pallas_call(
        kernel,
        grid=(width // tile,),
        out_shape=jax.ShapeDtypeStruct((width, sum(sizes)), jnp.bfloat16),
        in_specs=[
            pl.BlockSpec((rows, tile), lambda i: (0, i)),
            pl.BlockSpec((rows, sizes[0]), lambda i: (0, 0)),
            pl.BlockSpec((rows, tile), lambda i: (0, i)),
            pl.BlockSpec((rows, sizes[1]), lambda i: (0, 0)),
        ],
        out_specs=pl.BlockSpec((tile, sum(sizes)), lambda i: (i, 0)),
        compiler_params=pltpu.CompilerParams(vmem_limit_bytes=48 * 2**20),
        cost_estimate=pl.CostEstimate(
            flops=2 * rows * width * sum(sizes), bytes_accessed=rows * width * 4, transcendentals=0
        ),
    )(normed, grad_qkv, attended, grad_proj)


def stage(sure, body, *args):
    shapes = jax.eval_shape(body, *args)

    def nothing(*_):
        return jax.tree.map(lambda leaf: jnp.zeros(leaf.shape, leaf.dtype), shapes)

    return lax.cond(sure, body, nothing, *args)


def columns_of(weight, place, groups, shards):
    width = weight.shape[1] // (groups * shards)
    return jnp.concatenate(
        [
            lax.dynamic_slice_in_dim(weight, (f * groups + place) * width, width, 1)
            for f in range(shards)
        ],
        axis=1,
    )


def on_device(
    tokens,
    positions,
    w_query,
    w_key,
    w_value,
    w_out,
    gain_attn,
    w_gate,
    w_up,
    w_down,
    gain_mlp,
    cotangent,
):
    low, wide = jnp.bfloat16, jnp.float32
    groups = lax.axis_size("seq")
    shards = lax.axis_size("fsdp")
    place = lax.axis_index("seq")
    shard = lax.axis_index("fsdp")
    tok_rows, width = tokens.shape[1:]
    shard_rows = w_query.shape[0]
    heads_dev = HEADS // groups
    kv_copies = groups // KV_HEADS
    seq_len = tok_rows * groups
    q_cols = heads_dev * HEAD_DIM
    out_cols = width // groups
    ff = w_gate.shape[1]
    ff_dev = ff // groups
    scale = HEAD_DIM ** (-0.5)

    def z_gather(part):
        return lax.all_gather(part, "fsdp", axis=0, tiled=True)

    def z_scatter(part):
        return lax.psum_scatter(part, "fsdp", scatter_dimension=0, tiled=True)

    def columns(weight, start, count):
        return lax.dynamic_slice_in_dim(weight, start, count, 1)

    place_arg = place.reshape(1).astype(jnp.int32)
    kv_head = place // kv_copies
    attn_full = z_gather(
        jnp.concatenate(
            [
                columns(w_query, place * q_cols, q_cols),
                columns(w_key, kv_head * HEAD_DIM, HEAD_DIM),
                columns(w_value, kv_head * HEAD_DIM, HEAD_DIM),
                columns(w_out, place * out_cols, out_cols),
            ],
            axis=1,
        )
    )
    attn_full, out_part = attn_full[:, :-out_cols], attn_full[:, -out_cols:]
    mlp_full = z_gather(
        jnp.concatenate(
            [columns_of(w_gate, place, groups, shards), columns_of(w_up, place, groups, shards)],
            axis=1,
        )
    )
    down_rows = w_down.shape[0] // groups
    down_full = z_gather(lax.dynamic_slice_in_dim(w_down, place * down_rows, down_rows, 0))
    sure = positions[0, 0] >= 0
    own = tokens[0]
    gains_own = jnp.stack([gain_attn, gain_mlp]).astype(wide)

    def inputs_stage(own, positions, gains_own):
        gains = lax.dynamic_update_slice(
            jnp.zeros((2, width), wide), gains_own, (0, shard * shard_rows)
        )
        gains = ring_sum(gains)
        where = seq_gather(positions).reshape(seq_len)
        stream = seq_gather(own, gains, where).reshape(seq_len, width).astype(wide)
        cosine, sine = rope_tables(where, HEAD_DIM)
        cosine, sine = cosine.reshape(groups, tok_rows, 128), sine.reshape(groups, tok_rows, 128)
        inverse_all = lax.rsqrt(jnp.mean(stream * stream, axis=-1, keepdims=True) + EPS)
        normed_in = (stream * inverse_all * gains[0]).astype(low)
        return gains, cosine, sine, normed_in

    gains, cosine, sine, normed_in = stage(sure, inputs_stage, own, positions, gains_own)
    gain_in, gain_mid = gains

    def attention_stage(own, cotangent, normed_in, attn_full, out_part, cosine, sine, gain_mid):
        qkv = jnp.dot(normed_in, attn_full, preferred_element_type=wide)
        attended_send, *kept = attention(
            qkv.reshape(groups, tok_rows, -1), cosine, sine, place_arg, heads_dev
        )
        attended_tok = join_columns(seq_exchange(*attended_send), place_arg)
        out_even, out_odd = seq_halves(out_part, attended_send[0])
        out_full = join_weight(out_even, out_odd, place_arg)
        dy = seq_gather(after(cotangent, out_even)).reshape(seq_len, width)
        middle = own.astype(wide) + jnp.dot(attended_tok, out_full, preferred_element_type=wide)
        inverse_mid = lax.rsqrt(jnp.mean(middle * middle, axis=-1, keepdims=True) + EPS)
        unit_mid = middle * inverse_mid
        normed_mid = seq_gather((unit_mid * gain_mid).astype(low)).reshape(seq_len, width)
        return attended_tok, out_full, middle, normed_mid, dy, kept

    attended_tok, out_full, middle, normed_mid, dy, kept = stage(
        sure, attention_stage, own, cotangent[0], normed_in, attn_full, out_part, cosine, sine, gain_mid
    )

    def hidden_stage(normed_mid, mlp_full, dy, attended_tok):
        mlp_pre, hidden = hidden_units(normed_mid, mlp_full)
        attended_all = seq_gather(attended_tok, hidden).reshape(seq_len, -1)
        return attended_all, mlp_pre, hidden, dot(hidden, dy, ((0,), (0,))).astype(low)

    attended_all, mlp_pre, hidden, down_grad = stage(
        sure, hidden_stage, normed_mid, mlp_full, dy, attended_tok
    )
    down_sum = z_scatter(down_grad)
    grad_mlp = hidden_back(after(dy, down_grad), down_full, mlp_pre)
    halves = (slice(0, seq_len // 2), slice(seq_len // 2, None))

    def by_halves(product):
        return [product(at).astype(low).reshape(groups // 2, tok_rows, width) for at in halves]

    mlp_grad = dot(normed_mid, grad_mlp, ((0,), (0,))).astype(low)
    mlp_sum = z_scatter(mlp_grad)

    def middle_stage(
        grad_mlp, mlp_full, hidden, down_full, middle, dy_own, gain_mid, out_full, mlp_grad
    ):
        inverse_mid = lax.rsqrt(jnp.mean(middle * middle, axis=-1, keepdims=True) + EPS)
        unit_mid = middle * inverse_mid
        terms = by_halves(lambda at: dot(grad_mlp[at], mlp_full, ((1,), (1,))))
        grad_normed_mid = seq_scatter(*terms)
        grad_middle = norm_back(grad_normed_mid * gain_mid, unit_mid, inverse_mid)
        grad_middle = grad_middle + dy_own.astype(wide)
        grad_proj = grad_middle.astype(low)
        grad_attended = dot(grad_proj, out_full, ((1,), (1,))).astype(low)
        grad_even, grad_odd = split_columns((grad_attended, grad_proj), place_arg, groups)
        later = after(hidden, tuple(terms))
        down_terms = by_halves(
            lambda at: jnp.dot(later[at], down_full, preferred_element_type=wide)
        )
        layer_out = (middle + seq_scatter(*down_terms)).astype(low)
        return grad_middle, layer_out, grad_even, grad_odd

    grad_middle, layer_out, grad_even, grad_odd = stage(
        sure, middle_stage, grad_mlp, mlp_full, hidden, down_full, middle, cotangent[0], gain_mid, out_full,
        mlp_grad[:16],
    )

    def back_stage(
        grad_even, grad_odd, attended_all, normed_in, attn_full, cosine, sine, kept, down_sum
    ):
        wide_out, rotated, tops, sums = kept
        grad_pairs = seq_exchange(grad_even, grad_odd)
        grad_qkv, grad_proj_cols = attention_back(
            grad_pairs, rotated, wide_out, tops, sums, cosine, sine, place_arg
        )
        grad_qkv = grad_qkv.reshape(seq_len, -1)
        grad_proj_cols = grad_proj_cols.reshape(seq_len, out_cols)
        attn_terms = attention_terms(normed_in, grad_qkv, attended_all, grad_proj_cols)
        terms_in = by_halves(lambda at: dot(grad_qkv[at], attn_full, ((1,), (1,))))
        down_even, down_odd = seq_halves(after(down_sum, tuple(grad_pairs)), attn_terms)
        return attn_terms, terms_in, down_even, down_odd

    attn_terms, terms_in, down_even, down_odd = stage(
        sure, back_stage, grad_even, grad_odd, attended_all, normed_in, attn_full, cosine, sine, kept,
        after(down_sum, grad_even),
    )

    attn_sum = z_scatter(attn_terms)

    def tokens_stage(own, even, odd, gain_in, grad_middle, down_even, down_odd, mlp_sum):
        grad_normed_in = seq_scatter(even, odd)
        stream_own = own.astype(wide)
        inverse_in = lax.rsqrt(jnp.mean(stream_own * stream_own, axis=-1, keepdims=True) + EPS)
        unit_in = stream_own * inverse_in
        grad_stream = norm_back(grad_normed_in * gain_in, unit_in, inverse_in) + grad_middle
        grad_down = put_rows(down_even, down_odd, place_arg)
        return grad_stream, grad_down, *seq_halves(mlp_sum, grad_down)

    grad_stream, grad_down, mlp_even, mlp_odd = stage(
        sure, tokens_stage, own, *terms_in, gain_in, grad_middle, down_even, down_odd,
        after(mlp_sum, attn_terms),
    )

    def last_stage(mlp_even, mlp_odd, w_gate, w_up, attn_sum):
        grads = put_columns(mlp_even, mlp_odd, place_arg, shards, w_gate, w_up)
        return grads, seq_halves(attn_sum, grads)

    (grad_gate, grad_up, rows_mid), attn_halves = stage(
        sure, last_stage, mlp_even, mlp_odd, w_gate, w_up, attn_sum
    )
    grad_query, grad_key, grad_value, grad_out, rows_in = put_attention(
        *attn_halves,
        place_arg,
        (w_query, w_key, w_value),
        q_cols,
        out_cols,
    )
    return (
        layer_out[None],
        grad_stream[None],
        grad_query,
        grad_key,
        grad_value,
        grad_out,
        rows_in[:, 0] / gain_attn.astype(wide),
        grad_gate,
        grad_up,
        grad_down,
        rows_mid[:, 0] / gain_mlp.astype(wide),
    )


def solution(mesh):
    placed = (
        P("fsdp", "seq", None),
        P("fsdp", "seq"),
        P("fsdp", None),
        P("fsdp", None),
        P("fsdp", None),
        P("fsdp", None),
        P("fsdp"),
        P("fsdp", None),
        P("fsdp", None),
        P("fsdp", None),
        P("fsdp"),
        P("fsdp", "seq", None),
    )
    return jax.shard_map(
        on_device,
        mesh=mesh,
        in_specs=placed,
        out_specs=(
            P("fsdp", "seq", None),
            P("fsdp", "seq", None),
            P("fsdp", None),
            P("fsdp", None),
            P("fsdp", None),
            P("fsdp", None),
            P("fsdp"),
            P("fsdp", None),
            P("fsdp", None),
            P("fsdp", None),
            P("fsdp"),
        ),
        check_vma=False,
    )
```

```python
import math

import jax
import jax.numpy as jnp
from jax import lax
from jax.experimental import pallas as pl
from jax.experimental.pallas import tpu as pltpu
from jax.sharding import PartitionSpec as P

HEADS = 32
KV_HEADS = 4
HEAD_DIM = 64


EPS = 1e-05
ROPE_BASE = 10000.0


def rope_tables(positions, head_size):
    half_dim = head_size // 2
    lane = jnp.arange(128)
    freqs = jnp.exp(
        (lane % half_dim).astype(jnp.float32) * (-2.0 * math.log(ROPE_BASE) / head_size)
    )
    angles = positions.astype(jnp.float32)[..., None] * freqs
    sign = jnp.where(lane % head_size < half_dim, -1.0, 1.0)
    return jnp.cos(angles), jnp.sin(angles) * sign


def norm_back(grad_normed, normed, inverse):
    return inverse * (grad_normed - normed * jnp.mean(grad_normed * normed, axis=-1, keepdims=True))


def dot(left, right, dims):
    return lax.dot_general(left, right, ((dims[0], dims[1]), ((), ())), preferred_element_type=jnp.float32)


def swap(value, mask):
    return lax.ppermute(value, "seq", [(i, i ^ mask) for i in range(lax.axis_size("seq"))])


def place_pieces(pieces, places, shape):
    cols = shape[2]
    tile = 512 if cols % 512 == 0 else cols

    def kernel(*refs):
        for piece, (slot, row), ref in zip(pieces, places, refs):
            refs[-1][slot, row : row + piece.shape[0]] = ref[...]

    return pl.pallas_call(
        kernel,
        grid=(cols // tile,),
        out_shape=jax.ShapeDtypeStruct(shape, pieces[0].dtype),
        in_specs=[pl.BlockSpec((piece.shape[0], tile), lambda i: (0, i)) for piece in pieces],
        out_specs=pl.BlockSpec(shape[:2] + (tile,), lambda i: (0, 0, i)),
        compiler_params=pltpu.CompilerParams(vmem_limit_bytes=48 * 2**20),
        cost_estimate=pl.CostEstimate(flops=0, bytes_accessed=math.prod(shape) * 4, transcendentals=0),
    )(*pieces)


def after(value, *earlier):
    return lax.optimization_barrier((value, *earlier))[0]


def together(*chains):
    results, values, live = [None] * len(chains), [None] * len(chains), list(range(len(chains)))
    while live:
        sent = {}
        for i in live:
            try:
                sent[i] = chains[i].send(values[i])
            except StopIteration as stop:
                results[i] = stop.value
        live = list(sent)
        for i, value in lax.optimization_barrier(sent).items():
            values[i] = value
    return results


def work(*parts):
    results = []
    for part in parts:
        results.append((yield () if part is None else part()))
    return results


def held(value, steps):
    for _ in range(steps):
        value = yield value
    return value


def in_turn(*makers):
    result = None
    for maker in makers:
        result = yield from maker(result)
    return result


def near_chain(part):
    n = lax.axis_size("seq")
    if n == 8 and part.shape[0] % 16 == 0:
        half = part.shape[0] // 32 * 16
        by_x, by_y = yield swap(part, 2), swap(part, 4)
        far = yield swap(by_x[:half], 4), swap(by_y[half:], 2)
        places = ((0, 0), (1, 0), (2, 0), (3, 0), (3, half))
        return place_pieces((part, by_x, by_y, *far), places, (4,) + part.shape)
    mine, mask = part[None], 2
    while mask < n:
        mine = jnp.concatenate([mine, (yield swap(mine, mask))])
        mask *= 2
    return mine


def core_chain(mine):
    return (yield mine, swap(mine, 1))


def halves_chain(part):
    return in_turn(lambda _: near_chain(part), core_chain)


def gather_chain(part):
    mine, other = yield from halves_chain(part)
    if part.shape[0] % 16:
        return jnp.concatenate([mine, other])
    half, rows, cols = mine.shape
    tile = 512 if cols % 512 == 0 else cols

    def kernel(mine_ref, other_ref, out_ref):
        out_ref[:half] = mine_ref[...]
        out_ref[half:] = other_ref[...]

    return pl.pallas_call(
        kernel,
        grid=(cols // tile,),
        out_shape=jax.ShapeDtypeStruct((2 * half, rows, cols), part.dtype),
        in_specs=[pl.BlockSpec((half, rows, tile), lambda i: (0, 0, i))] * 2,
        out_specs=pl.BlockSpec((2 * half, rows, tile), lambda i: (0, 0, i)),
        cost_estimate=pl.CostEstimate(flops=0, bytes_accessed=mine.size * 8, transcendentals=0),
    )(mine, other)


def ring_chain(value):
    n = lax.axis_size("fsdp")
    moving = value
    for _ in range(n - 1):
        moving = yield lax.ppermute(moving, "fsdp", [(i, (i + 1) % n) for i in range(n)])
        value = value + moving
    return value


def scatter_chain(make_odd, make_even):
    n = lax.axis_size("seq")

    def add(own, other):
        return own.astype(jnp.float32) + other.astype(jnp.float32)

    low = jnp.bfloat16
    odd = make_odd()
    even, other = yield make_even(), swap(odd, 1)
    mine = add(even, other)
    if n == 8:
        half = even.shape[1] // 2
        far = mine[3].astype(low)
        from_x, from_y = yield swap(far[:half], 2), swap(far[half:], 4)
        to_y = jnp.concatenate([add(mine[2][:half], from_x), mine[2][half:]]).astype(low)
        to_x = jnp.concatenate([mine[1][:half], add(mine[1][half:], from_y)]).astype(low)
        by_x, by_y = yield swap(to_x, 2), swap(to_y, 4)
        return add(mine[0], by_x) + by_y.astype(jnp.float32)
    mask = n // 2
    while mask > 1:
        count = mine.shape[0] // 2
        mine = add(mine[:count], (yield swap(mine[count:].astype(low), mask)))
        mask //= 2
    return mine[0]


def ordered(place, even, odd, body):
    core = place & 1
    pl.when(core == 0)(lambda: body(even, odd))
    pl.when(core == 1)(lambda: body(odd, even))


def put_columns(even, odd, place, pieces, second):
    half, rows, cols = even.shape
    n, w = 2 * half, cols // (2 * pieces)
    tile = 64

    def kernel(place_ref, even_ref, odd_ref, out_ref):
        chip = place_ref[0] // 2

        def body(first, other):
            blocks = [(other if t % 2 else first)[(t // 2) ^ chip] for t in range(n)]
            for f in range(pieces):
                at = (second * pieces + f) * w
                row = jnp.concatenate([block[:, at : at + w] for block in blocks], axis=1)
                out_ref[:, f * n * w : (f + 1) * n * w] = row.astype(jnp.float32)

        ordered(place_ref[0], even_ref, odd_ref, body)

    spec = pl.BlockSpec((half, tile, cols), lambda i: (0, i, 0))
    return pl.pallas_call(
        kernel,
        grid=(rows // tile,),
        out_shape=jax.ShapeDtypeStruct((rows, pieces * n * w), jnp.float32),
        in_specs=[pl.BlockSpec(memory_space=pltpu.SMEM), spec, spec],
        out_specs=pl.BlockSpec((tile, pieces * n * w), lambda i: (i, 0)),
        compiler_params=pltpu.CompilerParams(vmem_limit_bytes=48 * 2**20),
        cost_estimate=pl.CostEstimate(flops=0, bytes_accessed=even.size * 8, transcendentals=0),
    )(place, even, odd)


def put_rows(even, odd, place):
    half, rows, cols = even.shape
    tile = 256

    def kernel(place_ref, even_ref, odd_ref, out_ref):
        chip = place_ref[0] // 2

        def body(first, second):
            for t in range(2 * half):
                block = (second if t % 2 else first)[(t // 2) ^ chip]
                out_ref[t * rows : (t + 1) * rows, :] = block.astype(jnp.float32)

        ordered(place_ref[0], even_ref, odd_ref, body)

    spec = pl.BlockSpec((half, rows, tile), lambda i: (0, 0, i))
    return pl.pallas_call(
        kernel,
        grid=(cols // tile,),
        out_shape=jax.ShapeDtypeStruct((2 * half * rows, cols), jnp.float32),
        in_specs=[pl.BlockSpec(memory_space=pltpu.SMEM), spec, spec],
        out_specs=pl.BlockSpec((2 * half * rows, tile), lambda i: (0, i)),
        compiler_params=pltpu.CompilerParams(vmem_limit_bytes=48 * 2**20),
        cost_estimate=pl.CostEstimate(flops=0, bytes_accessed=even.size * 12, transcendentals=0),
    )(place, even, odd)


def put_attention(even, odd, place, q_cols, out_cols):
    half, rows, cols = even.shape
    n, tile = 2 * half, 64
    copies = n // KV_HEADS
    sizes = (n * q_cols, KV_HEADS * HEAD_DIM, KV_HEADS * HEAD_DIM, n * out_cols)

    def kernel(place_ref, even_ref, odd_ref, query_ref, key_ref, value_ref, out_ref):
        chip = place_ref[0] // 2

        def body(first, second):
            blocks = [
                (second if t % 2 else first)[(t // 2) ^ chip].astype(jnp.float32) for t in range(n)
            ]
            for t, block in enumerate(blocks):
                query_ref[:, t * q_cols : (t + 1) * q_cols] = block[:, :q_cols]
                out_ref[:, t * out_cols : (t + 1) * out_cols] = block[:, cols - out_cols :]
            sums = [
                sum(block[:, q_cols : q_cols + 2 * HEAD_DIM] for block in blocks[h * copies : (h + 1) * copies])
                for h in range(KV_HEADS)
            ]
            key_ref[...] = jnp.concatenate([part[:, :HEAD_DIM] for part in sums], axis=1)
            value_ref[...] = jnp.concatenate([part[:, HEAD_DIM:] for part in sums], axis=1)

        ordered(place_ref[0], even_ref, odd_ref, body)

    spec = pl.BlockSpec((half, tile, cols), lambda i: (0, i, 0))
    return pl.pallas_call(
        kernel,
        grid=(rows // tile,),
        out_shape=[jax.ShapeDtypeStruct((rows, size), jnp.float32) for size in sizes],
        in_specs=[pl.BlockSpec(memory_space=pltpu.SMEM), spec, spec],
        out_specs=[pl.BlockSpec((tile, size), lambda i: (i, 0)) for size in sizes],
        compiler_params=pltpu.CompilerParams(vmem_limit_bytes=48 * 2**20),
        cost_estimate=pl.CostEstimate(flops=0, bytes_accessed=even.size * 12, transcendentals=0),
    )(place, even, odd)


def slot_of(mask, n):
    return (mask >> 1) + (mask & 1) * (n // 2)


def split_columns(parts, place, n):
    rows = parts[0].shape[0]
    sizes = [part.shape[1] // n for part in parts]
    half, cols = n // 2, sum(sizes)

    def kernel(place_ref, *refs):
        for core, ref in enumerate(refs[-2:]):
            for k in range(half):
                block, at = place_ref[0] ^ (2 * k + core), 0
                for size, part_ref in zip(sizes, refs):
                    start = pl.multiple_of(block * size, size)
                    ref[k, :, at : at + size] = part_ref[:, pl.ds(start, size)]
                    at += size

    vmem = pl.BlockSpec(memory_space=pltpu.VMEM)
    return pl.pallas_call(
        kernel,
        out_shape=[jax.ShapeDtypeStruct((half, rows, cols), parts[0].dtype)] * 2,
        in_specs=[pl.BlockSpec(memory_space=pltpu.SMEM)] + [vmem] * len(parts),
        out_specs=[vmem] * 2,
    )(place, *parts)


def exchange_chain(even, odd):
    half, rows, cols = even.shape
    other = yield swap(odd, 1)

    def kernel(even_ref, other_ref, *refs):
        for k, ref in enumerate(refs):
            ref[0] = even_ref[k]
            ref[1] = other_ref[k]

    vmem = pl.BlockSpec(memory_space=pltpu.VMEM)
    pairs = pl.pallas_call(
        kernel,
        out_shape=[jax.ShapeDtypeStruct((2, rows, cols), even.dtype)] * half,
        in_specs=[vmem] * 2,
        out_specs=[vmem] * half,
    )(even, other)
    return (yield [pair if k == 0 else swap(pair, 2 * k) for k, pair in enumerate(pairs)])


def join_columns(pairs, place):
    n, (_, rows, cols) = 2 * len(pairs), pairs[0].shape

    def kernel(place_ref, *refs):
        for k, ref in enumerate(refs[:-1]):
            for core in range(2):
                start = pl.multiple_of((place_ref[0] ^ (2 * k + core)) * cols, cols)
                refs[-1][:, pl.ds(start, cols)] = ref[core]

    vmem = pl.BlockSpec(memory_space=pltpu.VMEM)
    return pl.pallas_call(
        kernel,
        out_shape=jax.ShapeDtypeStruct((rows, n * cols), pairs[0].dtype),
        in_specs=[pl.BlockSpec(memory_space=pltpu.SMEM)] + [vmem] * len(pairs),
        out_specs=vmem,
    )(place, *pairs)


def join_weight(even, odd, place):
    half, rows, cols = even.shape
    n, tile = 2 * half, 512

    def kernel(place_ref, even_ref, odd_ref, out_ref):
        for ref, core in ((even_ref, 0), (odd_ref, 1)):
            for k in range(half):
                start = pl.multiple_of((place_ref[0] ^ (2 * k + core)) * cols, cols)
                out_ref[:, pl.ds(start, cols)] = ref[k]

    spec = pl.BlockSpec((half, tile, cols), lambda i: (0, i, 0))
    return pl.pallas_call(
        kernel,
        grid=(rows // tile,),
        out_shape=jax.ShapeDtypeStruct((rows, n * cols), even.dtype),
        in_specs=[pl.BlockSpec(memory_space=pltpu.SMEM), spec, spec],
        out_specs=pl.BlockSpec((tile, n * cols), lambda i: (i, 0)),
        compiler_params=pltpu.CompilerParams(vmem_limit_bytes=48 * 2**20),
        cost_estimate=pl.CostEstimate(flops=0, bytes_accessed=even.size * 8, transcendentals=0),
    )(place, even, odd)


def lanes(shape):
    return lax.broadcasted_iota(jnp.int32, shape, 1)


def halves_swapped(value):
    first = lanes(value.shape) % HEAD_DIM < HEAD_DIM // 2
    size = value.shape[1]
    left, right = pltpu.roll(value, size - HEAD_DIM // 2, 1), pltpu.roll(value, HEAD_DIM // 2, 1)
    return jnp.where(first, left, right)


def turned(value, cosine, sine):
    parts = [
        value[:, i : i + 128] * cosine + halves_swapped(value[:, i : i + 128]) * sine
        for i in range(0, value.shape[1], 128)
    ]
    return jnp.concatenate(parts, axis=1)


def key_copies(key_value):
    first = lanes(key_value.shape) < HEAD_DIM
    turned_over = pltpu.roll(key_value, HEAD_DIM, 1)
    keys = jnp.where(first, key_value, turned_over)
    values = jnp.where(first, turned_over, key_value)
    return keys, values, first


def only(value, head):
    first = lanes(value.shape) < HEAD_DIM
    return jnp.where(first if head == 0 else ~first, value, jnp.zeros_like(value))


def matmul(left, right, dims):
    return lax.dot_general(left, right, (dims, ((), ())), preferred_element_type=jnp.float32)


ROWS_OF = ((1,), (1,))
PLAIN = ((1,), (0,))
COLUMNS_OF = ((0,), (0,))
MASKED = -1e30


def attention(qkv, cosine, sine, place, heads_dev):
    n, rows, cols = qkv.shape
    length, q_cols = n * rows, heads_dev * HEAD_DIM
    block = 256
    low, wide = jnp.bfloat16, jnp.float32

    def kernel(place_ref, qkv_ref, cos_ref, sin_ref, *refs):
        even_ref, odd_ref, out_ref, rot_ref, top_ref, sum_ref = refs
        for t in range(n):
            slot = slot_of(place_ref[0] ^ t, n)
            value = qkv_ref[slot]
            moved = turned(value[:, : q_cols + 128], cos_ref[slot], sin_ref[slot])
            key_value = jnp.where(
                lanes((rows, 128)) < HEAD_DIM, moved[:, q_cols:], value[:, q_cols:]
            )
            at = slice(t * rows, (t + 1) * rows)
            rot_ref[at, :q_cols] = moved[:, :q_cols].astype(low)
            rot_ref[at, q_cols:] = key_value.astype(low)
        for i in range(length // block):
            span = (i + 1) * block
            key_value = rot_ref[:span, q_cols:]
            keys, values, _ = key_copies(key_value)
            held = [only(values, 0), only(values, 1)]
            shape = (block, span)
            seen = lax.broadcasted_iota(jnp.int32, shape, 1) <= i * block + (
                lax.broadcasted_iota(jnp.int32, shape, 0)
            )
            at = slice(i * block, (i + 1) * block)
            for pair in range(q_cols // 128):
                query = rot_ref[at, pair * 128 : (pair + 1) * 128] * jnp.asarray(0.125, low)
                total = None
                for head in range(2):
                    scores = matmul(only(query, head), keys, ROWS_OF)
                    scores = jnp.where(seen, scores, MASKED)
                    top = jnp.max(scores, axis=1, keepdims=True)
                    unnormed = jnp.exp(scores - top)
                    row_sum = jnp.sum(unnormed, axis=1, keepdims=True)
                    part = matmul(unnormed.astype(low), held[head], PLAIN) / row_sum
                    top_ref[2 * pair + head, at, :] = top
                    sum_ref[2 * pair + head, at, :] = row_sum
                    total = part if total is None else total + part
                out_ref[at, pair * 128 : (pair + 1) * 128] = total
        for core, ref in ((0, even_ref), (1, odd_ref)):
            for k in range(n // 2):
                start = pl.multiple_of((place_ref[0] ^ (2 * k + core)) * rows, rows)
                ref[k] = out_ref[pl.ds(start, rows), :].astype(low)

    vmem = pl.BlockSpec(memory_space=pltpu.VMEM)
    results = pl.pallas_call(
        kernel,
        out_shape=[jax.ShapeDtypeStruct((n // 2, rows, q_cols), low)] * 2
        + [
            jax.ShapeDtypeStruct((length, q_cols), wide),
            jax.ShapeDtypeStruct((length, q_cols + 2 * HEAD_DIM), low),
            jax.ShapeDtypeStruct((heads_dev, length, 1), wide),
            jax.ShapeDtypeStruct((heads_dev, length, 1), wide),
        ],
        in_specs=[pl.BlockSpec(memory_space=pltpu.SMEM)] + [vmem] * 3,
        out_specs=[vmem] * 6,
        compiler_params=pltpu.CompilerParams(vmem_limit_bytes=48 * 2**20),
        cost_estimate=pl.CostEstimate(
            flops=2 * length * length * 128 * heads_dev,
            bytes_accessed=qkv.size * 8,
            transcendentals=length * length * heads_dev // 2,
        ),
    )(place, qkv, cosine, sine)
    return results[:2], *results[2:]


def attention_back(grads, rotated, out, tops, sums, cosine, sine, place):
    n, (_, rows, all_cols) = 2 * len(grads), grads[0].shape
    length, cols = rotated.shape
    q_cols = cols - 2 * HEAD_DIM
    heads_dev = q_cols // HEAD_DIM
    block = 256
    low, wide = jnp.bfloat16, jnp.float32

    def kernel(place_ref, rot_ref, out_ref, top_ref, sum_ref, cos_ref, sin_ref, *refs):
        grad_refs = refs[: n // 2]
        result_ref, others_ref, grad_ref, dq_ref, dk_ref, dv_ref = refs[n // 2 :]
        for k, ref in enumerate(grad_refs):
            for core in range(2):
                start = pl.multiple_of((place_ref[0] ^ (2 * k + core)) * rows, rows)
                grad_ref[pl.ds(start, rows), :] = ref[core, :, :q_cols]
                others_ref[core * (n // 2) + k] = ref[core, :, q_cols:]
        dk_ref[...] = jnp.zeros_like(dk_ref)
        dv_ref[...] = jnp.zeros_like(dv_ref)
        for i in range(length // block):
            span = (i + 1) * block
            keys, values, _ = key_copies(rot_ref[:span, q_cols:])
            held = [only(keys, 0), only(keys, 1)]
            shape = (block, span)
            seen = lax.broadcasted_iota(jnp.int32, shape, 1) <= i * block + (
                lax.broadcasted_iota(jnp.int32, shape, 0)
            )
            at = slice(i * block, (i + 1) * block)
            dk = dv = None
            for pair in range(q_cols // 128):
                pair_at = slice(pair * 128, (pair + 1) * 128)
                query = rot_ref[at, pair_at] * jnp.asarray(0.125, low)
                grad = grad_ref[at, pair_at].astype(wide)
                product = grad * out_ref[at, pair_at]
                dq = None
                for head in range(2):
                    row_sum = sum_ref[2 * pair + head, at, :]
                    own_query = only(query, head)
                    own_grad = only((grad / row_sum).astype(low), head)
                    scores = jnp.where(seen, matmul(own_query, keys, ROWS_OF), MASKED)
                    unnormed = jnp.exp(scores - top_ref[2 * pair + head, at, :])
                    shift = jnp.sum(only(product, head), axis=1, keepdims=True) / row_sum
                    grad_probs = matmul(own_grad, values, ROWS_OF)
                    grad_scores = (unnormed * (grad_probs - shift)).astype(low)
                    dq_part = matmul(grad_scores, held[head], PLAIN)
                    dk_part = matmul(grad_scores, own_query, COLUMNS_OF)
                    dv_part = matmul(unnormed.astype(low), own_grad, COLUMNS_OF)
                    dq = dq_part if dq is None else dq + dq_part
                    dk = dk_part if dk is None else dk + dk_part
                    dv = dv_part if dv is None else dv + dv_part
                dq_ref[at, pair_at] = dq * 0.125
            dk_ref[:span, :] += dk
            dv_ref[:span, :] += dv
        for t in range(n):
            slot = slot_of(place_ref[0] ^ t, n)
            at = slice(t * rows, (t + 1) * rows)
            dk, dv = dk_ref[at, :], dv_ref[at, :]
            first = lanes(dk.shape) < HEAD_DIM
            dk, dv = dk + pltpu.roll(dk, HEAD_DIM, 1), dv + pltpu.roll(dv, HEAD_DIM, 1)
            moved = turned(
                jnp.concatenate([dq_ref[at, :], dk], axis=1), cos_ref[slot], -sin_ref[slot]
            )
            result_ref[slot, :, :q_cols] = moved[:, :q_cols].astype(low)
            result_ref[slot, :, q_cols:] = jnp.where(first, moved[:, q_cols:], dv).astype(low)

    vmem = pl.BlockSpec(memory_space=pltpu.VMEM)
    return pl.pallas_call(
        kernel,
        out_shape=[
            jax.ShapeDtypeStruct((n, rows, cols), low),
            jax.ShapeDtypeStruct((n, rows, all_cols - q_cols), low),
        ],
        in_specs=[pl.BlockSpec(memory_space=pltpu.SMEM)] + [vmem] * (6 + n // 2),
        out_specs=[vmem] * 2,
        scratch_shapes=[
            pltpu.VMEM((length, q_cols), low),
            pltpu.VMEM((length, q_cols), wide),
            pltpu.VMEM((length, 128), wide),
            pltpu.VMEM((length, 128), wide),
        ],
        compiler_params=pltpu.CompilerParams(vmem_limit_bytes=48 * 2**20),
        cost_estimate=pl.CostEstimate(
            flops=5 * length * length * 128 * heads_dev,
            bytes_accessed=rotated.size * 8,
            transcendentals=length * length * heads_dev // 2,
        ),
    )(place, rotated, out, tops, sums, cosine, sine, *grads)


def silu_parts(gate):
    sigmoid_gate = 1.0 / (1.0 + jnp.exp(-gate))
    return sigmoid_gate, gate * sigmoid_gate


def hidden_units(normed, weights):
    rows, width = normed.shape
    cols = weights.shape[1]
    tile, ff_dev = 256, cols // 2

    def kernel(normed_ref, weights_ref, pre_ref, hidden_ref):
        pre = matmul(normed_ref[...], weights_ref[...], PLAIN)
        pre_ref[...] = pre
        hidden_ref[...] = (silu_parts(pre[:, :ff_dev])[1] * pre[:, ff_dev:]).astype(jnp.bfloat16)

    return pl.pallas_call(
        kernel,
        grid=(rows // tile,),
        out_shape=[
            jax.ShapeDtypeStruct((rows, cols), jnp.float32),
            jax.ShapeDtypeStruct((rows, ff_dev), jnp.bfloat16),
        ],
        in_specs=[
            pl.BlockSpec((tile, width), lambda i: (i, 0)),
            pl.BlockSpec((width, cols), lambda i: (0, 0)),
        ],
        out_specs=[
            pl.BlockSpec((tile, cols), lambda i: (i, 0)),
            pl.BlockSpec((tile, ff_dev), lambda i: (i, 0)),
        ],
        compiler_params=pltpu.CompilerParams(vmem_limit_bytes=48 * 2**20),
        cost_estimate=pl.CostEstimate(
            flops=2 * rows * width * cols, bytes_accessed=rows * cols * 8, transcendentals=rows * ff_dev
        ),
    )(normed, weights)


def hidden_back(dy, down, pre):
    rows, width = dy.shape
    ff_dev = down.shape[0]
    tile = 256

    def kernel(dy_ref, down_ref, pre_ref, out_ref):
        grad_hidden = matmul(dy_ref[...], down_ref[...], ROWS_OF)
        gate, upper = pre_ref[:, :ff_dev], pre_ref[:, ff_dev:]
        sigmoid_gate, activated = silu_parts(gate)
        grad_gate = grad_hidden * upper * (sigmoid_gate * (1.0 + gate * (1.0 - sigmoid_gate)))
        both = jnp.concatenate([grad_gate, grad_hidden * activated], axis=1)
        out_ref[...] = both.astype(jnp.bfloat16)

    return pl.pallas_call(
        kernel,
        grid=(rows // tile,),
        out_shape=jax.ShapeDtypeStruct((rows, 2 * ff_dev), jnp.bfloat16),
        in_specs=[
            pl.BlockSpec((tile, width), lambda i: (i, 0)),
            pl.BlockSpec((ff_dev, width), lambda i: (0, 0)),
            pl.BlockSpec((tile, 2 * ff_dev), lambda i: (i, 0)),
        ],
        out_specs=pl.BlockSpec((tile, 2 * ff_dev), lambda i: (i, 0)),
        compiler_params=pltpu.CompilerParams(vmem_limit_bytes=48 * 2**20),
        cost_estimate=pl.CostEstimate(
            flops=2 * rows * width * ff_dev, bytes_accessed=rows * ff_dev * 16, transcendentals=rows * ff_dev
        ),
    )(dy, down, pre)


def row_products(*pairs):
    rows, width = pairs[0][0].shape
    sizes = [right.shape[1] for _, right in pairs]
    tile = 512

    def kernel(*refs):
        at = 0
        for i, size in enumerate(sizes):
            product = matmul(refs[2 * i][...], refs[2 * i + 1][...], COLUMNS_OF)
            refs[-1][:, at : at + size] = product.astype(jnp.bfloat16)
            at += size

    return pl.pallas_call(
        kernel,
        grid=(width // tile,),
        out_shape=jax.ShapeDtypeStruct((width, sum(sizes)), jnp.bfloat16),
        in_specs=[
            spec
            for size in sizes
            for spec in (
                pl.BlockSpec((rows, tile), lambda i: (0, i)),
                pl.BlockSpec((rows, size), lambda i: (0, 0)),
            )
        ],
        out_specs=pl.BlockSpec((tile, sum(sizes)), lambda i: (i, 0)),
        compiler_params=pltpu.CompilerParams(vmem_limit_bytes=48 * 2**20),
        cost_estimate=pl.CostEstimate(
            flops=2 * rows * width * sum(sizes), bytes_accessed=rows * width * 4, transcendentals=0
        ),
    )(*[array for pair in pairs for array in pair])


def stage(sure, body, *args):
    shapes = jax.eval_shape(body, *args)

    def nothing(*_):
        return jax.tree.map(lambda leaf: jnp.zeros(leaf.shape, leaf.dtype), shapes)

    return lax.cond(sure, body, nothing, *args)


def columns_of(weight, place, groups, shards):
    width = weight.shape[1] // (groups * shards)
    return jnp.concatenate(
        [
            lax.dynamic_slice_in_dim(weight, (f * groups + place) * width, width, 1)
            for f in range(shards)
        ],
        axis=1,
    )


def on_device(
    tokens,
    positions,
    w_query,
    w_key,
    w_value,
    w_out,
    gain_attn,
    w_gate,
    w_up,
    w_down,
    gain_mlp,
    cotangent,
):
    low, wide = jnp.bfloat16, jnp.float32
    groups = lax.axis_size("seq")
    shards = lax.axis_size("fsdp")
    place = lax.axis_index("seq")
    shard = lax.axis_index("fsdp")
    tok_rows, width = tokens.shape[1:]
    shard_rows = w_query.shape[0]
    heads_dev = HEADS // groups
    kv_copies = groups // KV_HEADS
    seq_len = tok_rows * groups
    q_cols = heads_dev * HEAD_DIM
    out_cols = width // groups
    ff = w_gate.shape[1]
    ff_dev = ff // groups
    scale = HEAD_DIM ** (-0.5)

    def z_gather(part):
        return lax.all_gather(part, "fsdp", axis=0, tiled=True)

    def z_scatter(part):
        return lax.psum_scatter(part, "fsdp", scatter_dimension=0, tiled=True)

    def columns(weight, start, count):
        return lax.dynamic_slice_in_dim(weight, start, count, 1)

    place_arg = place.reshape(1).astype(jnp.int32)
    kv_head = place // kv_copies
    attn_own = jnp.concatenate(
        [
            columns(w_query, place * q_cols, q_cols),
            columns(w_key, kv_head * HEAD_DIM, HEAD_DIM),
            columns(w_value, kv_head * HEAD_DIM, HEAD_DIM),
            columns(w_out, place * out_cols, out_cols),
        ],
        axis=1,
    )
    attn_full = z_gather(attn_own)
    attn_full, out_part = attn_full[:, :-out_cols], attn_full[:, -out_cols:]
    mlp_own = jnp.concatenate(
        [columns_of(w_gate, place, groups, shards), columns_of(w_up, place, groups, shards)], axis=1
    )
    mlp_full = z_gather(mlp_own)
    down_rows = w_down.shape[0] // groups
    down_full = z_gather(lax.dynamic_slice_in_dim(w_down, place * down_rows, down_rows, 0))
    sure = positions[0, 0] >= 0
    own = tokens[0]
    gains_own = jnp.stack([gain_attn, gain_mlp]).astype(wide)

    halves = (slice(seq_len // 2, None), slice(0, seq_len // 2))

    def by_halves(product):
        def half(at):
            return product(at).astype(low).reshape(groups // 2, tok_rows, width)

        return scatter_chain(lambda: half(halves[0]), lambda: half(halves[1]))

    def inputs_stage(own, positions, gains_own):
        gains = lax.dynamic_update_slice(
            jnp.zeros((2, width), wide), gains_own, (0, shard * shard_rows)
        )
        gains, where, stream = together(
            ring_chain(gains), gather_chain(positions), gather_chain(own)
        )
        where, stream = where.reshape(seq_len), stream.reshape(seq_len, width).astype(wide)
        cosine, sine = rope_tables(where, HEAD_DIM)
        cosine, sine = cosine.reshape(groups, tok_rows, 128), sine.reshape(groups, tok_rows, 128)
        inverse_all = lax.rsqrt(jnp.mean(stream * stream, axis=-1, keepdims=True) + EPS)
        normed_in = (stream * inverse_all * gains[0]).astype(low)
        return gains, cosine, sine, normed_in

    gains, cosine, sine, normed_in = stage(sure, inputs_stage, own, positions, gains_own)
    gain_in, gain_mid = gains

    def attention_stage(own, cotangent, normed_in, attn_full, out_part, cosine, sine, gain_mid):
        def attend(_):
            qkv = jnp.dot(normed_in, attn_full, preferred_element_type=wide)
            return (
                yield attention(
                    qkv.reshape(groups, tok_rows, -1), cosine, sine, place_arg, heads_dev
                )
            )

        def exchange(attended):
            pairs = yield from exchange_chain(*attended[0])
            return join_columns(pairs, place_arg), attended[1:]

        def project(results):
            attended_tok, kept = results
            while not out_box:
                yield ()
            out_full = join_weight(*out_box[0], place_arg)
            middle = own.astype(wide) + jnp.dot(attended_tok, out_full, preferred_element_type=wide)
            inverse_mid = lax.rsqrt(jnp.mean(middle * middle, axis=-1, keepdims=True) + EPS)
            normed_mid = yield from gather_chain((middle * inverse_mid * gain_mid).astype(low))
            return attended_tok, out_full, middle, normed_mid.reshape(seq_len, width), kept

        out_box = []

        def weight():
            out_box.append((yield from halves_chain(out_part)))

        _, results, (_, dy) = together(
            weight(),
            in_turn(attend, exchange, project),
            in_turn(lambda _: held(cotangent, 1), lambda later: pair_chain(gather_chain(later))),
        )
        return *results, dy.reshape(seq_len, width)

    def pair_chain(chain):
        return None, (yield from chain)

    attended_tok, out_full, middle, normed_mid, kept, dy = stage(
        sure, attention_stage, own, cotangent[0], normed_in, attn_full, out_part, cosine, sine, gain_mid
    )

    def hidden_stage(normed_mid, mlp_full, dy, attended_tok):
        def products():
            mlp_pre, hidden = yield hidden_units(normed_mid, mlp_full)
            down_grad = yield dot(hidden, dy, ((0,), (0,))).astype(low)
            return mlp_pre, hidden, down_grad

        results, attended_all = together(products(), gather_chain(attended_tok))
        return attended_all.reshape(seq_len, -1), *results

    attended_all, mlp_pre, hidden, down_grad = stage(
        sure, hidden_stage, normed_mid, mlp_full, dy, attended_tok
    )
    down_sum = z_scatter(down_grad)
    grad_mlp = hidden_back(after(dy, down_grad), down_full, mlp_pre)

    def middle_stage(grad_mlp, mlp_full, normed_mid, middle, dy_own, gain_mid, out_full):
        inverse_mid = lax.rsqrt(jnp.mean(middle * middle, axis=-1, keepdims=True) + EPS)
        unit_mid = middle * inverse_mid
        grad_normed_mid, results = together(
            by_halves(lambda at: dot(grad_mlp[at], mlp_full, ((1,), (1,)))),
            work(None, None, lambda: row_products((normed_mid, grad_mlp))),
        )
        grad_middle = norm_back(grad_normed_mid * gain_mid, unit_mid, inverse_mid)
        grad_middle = grad_middle + dy_own.astype(wide)
        grad_proj = grad_middle.astype(low)
        grad_attended = dot(grad_proj, out_full, ((1,), (1,))).astype(low)
        grad_even, grad_odd = split_columns((grad_attended, grad_proj), place_arg, groups)
        return grad_middle, grad_even, grad_odd, results[-1]

    grad_middle, grad_even, grad_odd, mlp_grad = stage(
        sure, middle_stage, grad_mlp, mlp_full, normed_mid, middle, cotangent[0], gain_mid, out_full
    )
    mlp_sum = z_scatter(mlp_grad)

    def back_stage(
        grad_even, grad_odd, attended_all, normed_in, cosine, sine, kept, down_sum, own, attn_full,
        gain_in, grad_middle, hidden, down_full, middle,
    ):
        wide_out, rotated, tops, sums = kept

        def back(pairs):
            grad_qkv, grad_proj_cols = yield attention_back(
                pairs, rotated, wide_out, tops, sums, cosine, sine, place_arg
            )
            grad_qkv = grad_qkv.reshape(seq_len, -1)
            terms = yield row_products(
                (normed_in, grad_qkv), (attended_all, grad_proj_cols.reshape(seq_len, out_cols))
            )
            grad_normed_in = yield from by_halves(
                lambda at: dot(grad_qkv[at], attn_full, ((1,), (1,)))
            )
            return grad_normed_in, terms

        (grad_normed_in, attn_terms), down_halves, down_term = together(
            in_turn(lambda _: exchange_chain(grad_even, grad_odd), back),
            in_turn(lambda _: held(down_sum, 2), halves_chain),
            in_turn(
                lambda _: held(hidden, 2),
                lambda later: by_halves(
                    lambda at: jnp.dot(later[at], down_full, preferred_element_type=wide)
                ),
            ),
        )
        stream_own = own.astype(wide)
        inverse_in = lax.rsqrt(jnp.mean(stream_own * stream_own, axis=-1, keepdims=True) + EPS)
        unit_in = stream_own * inverse_in
        grad_stream = norm_back(grad_normed_in * gain_in, unit_in, inverse_in) + grad_middle
        return grad_stream, attn_terms, (middle + down_term).astype(low), *down_halves

    grad_stream, attn_terms, layer_out, down_even, down_odd = stage(
        sure, back_stage, grad_even, grad_odd, attended_all, normed_in, cosine, sine, kept,
        after(down_sum, grad_even), own, attn_full, gain_in, grad_middle, hidden, down_full, middle,
    )

    attn_sum = z_scatter(attn_terms)

    def output_stage(down_even, down_odd, mlp_sum):
        (grad_down,), mine = together(
            work(lambda: put_rows(down_even, down_odd, place_arg)), near_chain(mlp_sum)
        )
        return grad_down, mine

    grad_down, mine = stage(sure, output_stage, down_even, down_odd, after(mlp_sum, attn_terms))

    def last_stage(mine, mlp_sum, mlp_own, attn_sum, attn_own):
        def columns_put():
            even, odd = yield from core_chain(mine)
            gate = yield put_columns(even, odd, place_arg, shards, 0)
            up = yield put_columns(even, odd, place_arg, shards, 1)
            return gate, up

        def sums_chain():
            pairs = ((attn_sum[:, :-out_cols], attn_own[:, :-out_cols]), (mlp_sum, mlp_own))
            sums = [jnp.sum(a.astype(wide) * b.astype(wide), axis=1) for a, b in pairs]
            sums, mask = jnp.stack(sums), 1
            while mask < groups:
                sums = sums + (yield swap(sums, mask))
                mask *= 2
            return sums

        puts, attn_halves, sums = together(columns_put(), halves_chain(attn_sum), sums_chain())
        return *puts, sums, *put_attention(*attn_halves, place_arg, q_cols, out_cols)

    grad_gate, grad_up, row_sums, grad_query, grad_key, grad_value, grad_out = stage(
        sure, last_stage, mine, mlp_sum, mlp_own, after(attn_sum, grad_down), attn_own
    )
    return (
        layer_out[None],
        grad_stream[None],
        grad_query,
        grad_key,
        grad_value,
        grad_out,
        row_sums[0] / gain_attn.astype(wide),
        grad_gate,
        grad_up,
        grad_down,
        row_sums[1] / gain_mlp.astype(wide),
    )


def solution(mesh):
    placed = (
        P("fsdp", "seq", None),
        P("fsdp", "seq"),
        P("fsdp", None),
        P("fsdp", None),
        P("fsdp", None),
        P("fsdp", None),
        P("fsdp"),
        P("fsdp", None),
        P("fsdp", None),
        P("fsdp", None),
        P("fsdp"),
        P("fsdp", "seq", None),
    )
    return jax.shard_map(
        on_device,
        mesh=mesh,
        in_specs=placed,
        out_specs=(
            P("fsdp", "seq", None),
            P("fsdp", "seq", None),
            P("fsdp", None),
            P("fsdp", None),
            P("fsdp", None),
            P("fsdp", None),
            P("fsdp"),
            P("fsdp", None),
            P("fsdp", None),
            P("fsdp", None),
            P("fsdp"),
        ),
        check_vma=False,
    )
```

```python
import math

import jax
import jax.numpy as jnp
from jax import lax
from jax.experimental import pallas as pl
from jax.experimental.pallas import tpu as pltpu
from jax.sharding import PartitionSpec as P

HEADS = 32
KV_HEADS = 4
HEAD_DIM = 64


EPS = 1e-05
ROPE_BASE = 10000.0


def rope_tables(positions, head_size):
    half_dim = head_size // 2
    lane = jnp.arange(128)
    freqs = jnp.exp(
        (lane % half_dim).astype(jnp.float32) * (-2.0 * math.log(ROPE_BASE) / head_size)
    )
    angles = positions.astype(jnp.float32)[..., None] * freqs
    sign = jnp.where(lane % head_size < half_dim, -1.0, 1.0)
    return jnp.cos(angles), jnp.sin(angles) * sign


def norm_back(grad_normed, normed, inverse):
    return inverse * (grad_normed - normed * jnp.mean(grad_normed * normed, axis=-1, keepdims=True))


def dot(left, right, dims):
    return lax.dot_general(left, right, ((dims[0], dims[1]), ((), ())), preferred_element_type=jnp.float32)


def swap(value, mask):
    return lax.ppermute(value, "seq", [(i, i ^ mask) for i in range(lax.axis_size("seq"))])


def place_pieces(pieces, places, shape):
    cols = shape[2]
    tile = 512 if cols % 512 == 0 else cols

    def kernel(*refs):
        for piece, (slot, row), ref in zip(pieces, places, refs):
            refs[-1][slot, row : row + piece.shape[0]] = ref[...]

    return pl.pallas_call(
        kernel,
        grid=(cols // tile,),
        out_shape=jax.ShapeDtypeStruct(shape, pieces[0].dtype),
        in_specs=[pl.BlockSpec((piece.shape[0], tile), lambda i: (0, i)) for piece in pieces],
        out_specs=pl.BlockSpec(shape[:2] + (tile,), lambda i: (0, 0, i)),
        compiler_params=pltpu.CompilerParams(vmem_limit_bytes=48 * 2**20),
        cost_estimate=pl.CostEstimate(flops=0, bytes_accessed=math.prod(shape) * 4, transcendentals=0),
    )(*pieces)


def after(value, *earlier):
    return lax.optimization_barrier((value, *earlier))[0]


def together(*chains):
    results, values, live = [None] * len(chains), [None] * len(chains), list(range(len(chains)))
    while live:
        sent = {}
        for i in live:
            try:
                sent[i] = chains[i].send(values[i])
            except StopIteration as stop:
                results[i] = stop.value
        live = list(sent)
        for i, value in lax.optimization_barrier(sent).items():
            values[i] = value
    return results


def work(*parts):
    results = []
    for part in parts:
        results.append((yield () if part is None else part()))
    return results


def held(value, steps):
    for _ in range(steps):
        value = yield value
    return value


def in_turn(*makers):
    result = None
    for maker in makers:
        result = yield from maker(result)
    return result


def near_chain(part):
    n = lax.axis_size("seq")
    if n == 8 and part.shape[0] % 16 == 0:
        half = part.shape[0] // 32 * 16
        by_x, by_y = yield swap(part, 2), swap(part, 4)
        far = yield swap(by_x[:half], 4), swap(by_y[half:], 2)
        places = ((0, 0), (1, 0), (2, 0), (3, 0), (3, half))
        return place_pieces((part, by_x, by_y, *far), places, (4,) + part.shape)
    mine, mask = part[None], 2
    while mask < n:
        mine = jnp.concatenate([mine, (yield swap(mine, mask))])
        mask *= 2
    return mine


def core_chain(mine):
    return (yield mine, swap(mine, 1))


def halves_chain(part):
    return in_turn(lambda _: near_chain(part), core_chain)


def gather_chain(part):
    mine, other = yield from halves_chain(part)
    if part.shape[0] % 16:
        return jnp.concatenate([mine, other])
    half, rows, cols = mine.shape
    tile = 512 if cols % 512 == 0 else cols

    def kernel(mine_ref, other_ref, out_ref):
        out_ref[:half] = mine_ref[...]
        out_ref[half:] = other_ref[...]

    return pl.pallas_call(
        kernel,
        grid=(cols // tile,),
        out_shape=jax.ShapeDtypeStruct((2 * half, rows, cols), part.dtype),
        in_specs=[pl.BlockSpec((half, rows, tile), lambda i: (0, 0, i))] * 2,
        out_specs=pl.BlockSpec((2 * half, rows, tile), lambda i: (0, 0, i)),
        cost_estimate=pl.CostEstimate(flops=0, bytes_accessed=mine.size * 8, transcendentals=0),
    )(mine, other)


def ring_chain(value):
    n = lax.axis_size("fsdp")
    moving = value
    for _ in range(n - 1):
        moving = yield lax.ppermute(moving, "fsdp", [(i, (i + 1) % n) for i in range(n)])
        value = value + moving
    return value


def scatter_chain(make_odd, make_even):
    n = lax.axis_size("seq")

    def add(own, other):
        return own.astype(jnp.float32) + other.astype(jnp.float32)

    low = jnp.bfloat16
    odd = make_odd()
    even, other = yield make_even(), swap(odd, 1)
    mine = add(even, other)
    if n == 8:
        half = even.shape[1] // 2
        far = mine[3].astype(low)
        from_x, from_y = yield swap(far[:half], 2), swap(far[half:], 4)
        to_y = jnp.concatenate([add(mine[2][:half], from_x), mine[2][half:]]).astype(low)
        to_x = jnp.concatenate([mine[1][:half], add(mine[1][half:], from_y)]).astype(low)
        by_x, by_y = yield swap(to_x, 2), swap(to_y, 4)
        return add(mine[0], by_x) + by_y.astype(jnp.float32)
    mask = n // 2
    while mask > 1:
        count = mine.shape[0] // 2
        mine = add(mine[:count], (yield swap(mine[count:].astype(low), mask)))
        mask //= 2
    return mine[0]


def ordered(place, even, odd, body):
    core = place & 1
    pl.when(core == 0)(lambda: body(even, odd))
    pl.when(core == 1)(lambda: body(odd, even))


def put_columns(even, odd, place, pieces, part, parts, earlier=()):
    half, rows, cols = even.shape
    n, w = 2 * half, cols // (2 * pieces)
    tile = 64
    steps = rows // parts // tile

    def kernel(place_ref, even_ref, odd_ref, *refs):
        chip = place_ref[0] // 2

        def body(first, other):
            blocks = [(other if t % 2 else first)[(t // 2) ^ chip] for t in range(n)]
            for target, start in zip(refs[-2:], (0, cols // 2)):
                for f in range(pieces):
                    at = start + f * w
                    row = jnp.concatenate([block[:, at : at + w] for block in blocks], axis=1)
                    target[:, f * n * w : (f + 1) * n * w] = row.astype(jnp.float32)

        ordered(place_ref[0], even_ref, odd_ref, body)

    spec = pl.BlockSpec((half, tile, cols), lambda i: (0, i + part * steps, 0))
    whole = jax.ShapeDtypeStruct((rows, pieces * n * w), jnp.float32)
    return pl.pallas_call(
        kernel,
        grid=(steps,),
        out_shape=(whole, whole),
        in_specs=[pl.BlockSpec(memory_space=pltpu.SMEM), spec, spec]
        + [pl.BlockSpec(memory_space=pl.ANY)] * len(earlier),
        out_specs=[pl.BlockSpec((tile, pieces * n * w), lambda i: (i + part * steps, 0))] * 2,
        input_output_aliases={3 + i: i for i in range(len(earlier))},
        compiler_params=pltpu.CompilerParams(vmem_limit_bytes=48 * 2**20),
        cost_estimate=pl.CostEstimate(flops=0, bytes_accessed=even.size * 6, transcendentals=0),
    )(place, even, odd, *earlier)


def put_rows(even, odd, place):
    half, rows, cols = even.shape
    tile = 256

    def kernel(place_ref, even_ref, odd_ref, out_ref):
        chip = place_ref[0] // 2

        def body(first, second):
            for t in range(2 * half):
                block = (second if t % 2 else first)[(t // 2) ^ chip]
                out_ref[t * rows : (t + 1) * rows, :] = block.astype(jnp.float32)

        ordered(place_ref[0], even_ref, odd_ref, body)

    spec = pl.BlockSpec((half, rows, tile), lambda i: (0, 0, i))
    return pl.pallas_call(
        kernel,
        grid=(cols // tile,),
        out_shape=jax.ShapeDtypeStruct((2 * half * rows, cols), jnp.float32),
        in_specs=[pl.BlockSpec(memory_space=pltpu.SMEM), spec, spec],
        out_specs=pl.BlockSpec((2 * half * rows, tile), lambda i: (0, i)),
        compiler_params=pltpu.CompilerParams(vmem_limit_bytes=48 * 2**20),
        cost_estimate=pl.CostEstimate(flops=0, bytes_accessed=even.size * 12, transcendentals=0),
    )(place, even, odd)


def put_attention(even, odd, place, q_cols, out_cols):
    half, rows, cols = even.shape
    n, tile = 2 * half, 64
    copies = n // KV_HEADS
    sizes = (n * q_cols, KV_HEADS * HEAD_DIM, KV_HEADS * HEAD_DIM, n * out_cols)

    def kernel(place_ref, even_ref, odd_ref, query_ref, key_ref, value_ref, out_ref):
        chip = place_ref[0] // 2

        def body(first, second):
            blocks = [
                (second if t % 2 else first)[(t // 2) ^ chip].astype(jnp.float32) for t in range(n)
            ]
            for t, block in enumerate(blocks):
                query_ref[:, t * q_cols : (t + 1) * q_cols] = block[:, :q_cols]
                out_ref[:, t * out_cols : (t + 1) * out_cols] = block[:, cols - out_cols :]
            sums = [
                sum(block[:, q_cols : q_cols + 2 * HEAD_DIM] for block in blocks[h * copies : (h + 1) * copies])
                for h in range(KV_HEADS)
            ]
            key_ref[...] = jnp.concatenate([part[:, :HEAD_DIM] for part in sums], axis=1)
            value_ref[...] = jnp.concatenate([part[:, HEAD_DIM:] for part in sums], axis=1)

        ordered(place_ref[0], even_ref, odd_ref, body)

    spec = pl.BlockSpec((half, tile, cols), lambda i: (0, i, 0))
    return pl.pallas_call(
        kernel,
        grid=(rows // tile,),
        out_shape=[jax.ShapeDtypeStruct((rows, size), jnp.float32) for size in sizes],
        in_specs=[pl.BlockSpec(memory_space=pltpu.SMEM), spec, spec],
        out_specs=[pl.BlockSpec((tile, size), lambda i: (i, 0)) for size in sizes],
        compiler_params=pltpu.CompilerParams(vmem_limit_bytes=48 * 2**20),
        cost_estimate=pl.CostEstimate(flops=0, bytes_accessed=even.size * 12, transcendentals=0),
    )(place, even, odd)


def slot_of(mask, n):
    return (mask >> 1) + (mask & 1) * (n // 2)


def split_columns(parts, place, n):
    rows = parts[0].shape[0]
    sizes = [part.shape[1] // n for part in parts]
    half, cols = n // 2, sum(sizes)

    def kernel(place_ref, *refs):
        for core, ref in enumerate(refs[-2:]):
            for k in range(half):
                block, at = place_ref[0] ^ (2 * k + core), 0
                for size, part_ref in zip(sizes, refs):
                    start = pl.multiple_of(block * size, size)
                    ref[k, :, at : at + size] = part_ref[:, pl.ds(start, size)]
                    at += size

    vmem = pl.BlockSpec(memory_space=pltpu.VMEM)
    return pl.pallas_call(
        kernel,
        out_shape=[jax.ShapeDtypeStruct((half, rows, cols), parts[0].dtype)] * 2,
        in_specs=[pl.BlockSpec(memory_space=pltpu.SMEM)] + [vmem] * len(parts),
        out_specs=[vmem] * 2,
    )(place, *parts)


def exchange_chain(even, odd):
    half, rows, cols = even.shape
    other = yield swap(odd, 1)

    def kernel(even_ref, other_ref, *refs):
        for k, ref in enumerate(refs):
            ref[0] = even_ref[k]
            ref[1] = other_ref[k]

    vmem = pl.BlockSpec(memory_space=pltpu.VMEM)
    pairs = pl.pallas_call(
        kernel,
        out_shape=[jax.ShapeDtypeStruct((2, rows, cols), even.dtype)] * half,
        in_specs=[vmem] * 2,
        out_specs=[vmem] * half,
    )(even, other)
    return (yield [pair if k == 0 else swap(pair, 2 * k) for k, pair in enumerate(pairs)])


def join_columns(pairs, place):
    n, (_, rows, cols) = 2 * len(pairs), pairs[0].shape

    def kernel(place_ref, *refs):
        for k, ref in enumerate(refs[:-1]):
            for core in range(2):
                start = pl.multiple_of((place_ref[0] ^ (2 * k + core)) * cols, cols)
                refs[-1][:, pl.ds(start, cols)] = ref[core]

    vmem = pl.BlockSpec(memory_space=pltpu.VMEM)
    return pl.pallas_call(
        kernel,
        out_shape=jax.ShapeDtypeStruct((rows, n * cols), pairs[0].dtype),
        in_specs=[pl.BlockSpec(memory_space=pltpu.SMEM)] + [vmem] * len(pairs),
        out_specs=vmem,
    )(place, *pairs)


def join_weight(even, odd, place):
    half, rows, cols = even.shape
    n, tile = 2 * half, 512

    def kernel(place_ref, even_ref, odd_ref, out_ref):
        for ref, core in ((even_ref, 0), (odd_ref, 1)):
            for k in range(half):
                start = pl.multiple_of((place_ref[0] ^ (2 * k + core)) * cols, cols)
                out_ref[:, pl.ds(start, cols)] = ref[k]

    spec = pl.BlockSpec((half, tile, cols), lambda i: (0, i, 0))
    return pl.pallas_call(
        kernel,
        grid=(rows // tile,),
        out_shape=jax.ShapeDtypeStruct((rows, n * cols), even.dtype),
        in_specs=[pl.BlockSpec(memory_space=pltpu.SMEM), spec, spec],
        out_specs=pl.BlockSpec((tile, n * cols), lambda i: (i, 0)),
        compiler_params=pltpu.CompilerParams(vmem_limit_bytes=48 * 2**20),
        cost_estimate=pl.CostEstimate(flops=0, bytes_accessed=even.size * 8, transcendentals=0),
    )(place, even, odd)


def lanes(shape):
    return lax.broadcasted_iota(jnp.int32, shape, 1)


def halves_swapped(value):
    first = lanes(value.shape) % HEAD_DIM < HEAD_DIM // 2
    size = value.shape[1]
    left, right = pltpu.roll(value, size - HEAD_DIM // 2, 1), pltpu.roll(value, HEAD_DIM // 2, 1)
    return jnp.where(first, left, right)


def turned(value, cosine, sine):
    parts = [
        value[:, i : i + 128] * cosine + halves_swapped(value[:, i : i + 128]) * sine
        for i in range(0, value.shape[1], 128)
    ]
    return jnp.concatenate(parts, axis=1)


def key_copies(key_value):
    first = lanes(key_value.shape) < HEAD_DIM
    turned_over = pltpu.roll(key_value, HEAD_DIM, 1)
    keys = jnp.where(first, key_value, turned_over)
    values = jnp.where(first, turned_over, key_value)
    return keys, values, first


def only(value, head):
    first = lanes(value.shape) < HEAD_DIM
    return jnp.where(first if head == 0 else ~first, value, jnp.zeros_like(value))


def matmul(left, right, dims):
    return lax.dot_general(left, right, (dims, ((), ())), preferred_element_type=jnp.float32)


ROWS_OF = ((1,), (1,))
PLAIN = ((1,), (0,))
COLUMNS_OF = ((0,), (0,))
MASKED = -1e30


def attention(qkv, cosine, sine, place, heads_dev):
    n, rows, cols = qkv.shape
    length, q_cols = n * rows, heads_dev * HEAD_DIM
    block = 256
    low, wide = jnp.bfloat16, jnp.float32

    def kernel(place_ref, qkv_ref, cos_ref, sin_ref, *refs):
        even_ref, odd_ref, out_ref, rot_ref, top_ref, sum_ref = refs
        for t in range(n):
            slot = slot_of(place_ref[0] ^ t, n)
            value = qkv_ref[slot]
            moved = turned(value[:, : q_cols + 128], cos_ref[slot], sin_ref[slot])
            key_value = jnp.where(
                lanes((rows, 128)) < HEAD_DIM, moved[:, q_cols:], value[:, q_cols:]
            )
            at = slice(t * rows, (t + 1) * rows)
            rot_ref[at, :q_cols] = moved[:, :q_cols].astype(low)
            rot_ref[at, q_cols:] = key_value.astype(low)
        for i in range(length // block):
            span = (i + 1) * block
            key_value = rot_ref[:span, q_cols:]
            keys, values, _ = key_copies(key_value)
            held = [only(values, 0), only(values, 1)]
            shape = (block, span)
            seen = lax.broadcasted_iota(jnp.int32, shape, 1) <= i * block + (
                lax.broadcasted_iota(jnp.int32, shape, 0)
            )
            at = slice(i * block, (i + 1) * block)
            for pair in range(q_cols // 128):
                query = rot_ref[at, pair * 128 : (pair + 1) * 128] * jnp.asarray(0.125, low)
                total = None
                for head in range(2):
                    scores = matmul(only(query, head), keys, ROWS_OF)
                    scores = jnp.where(seen, scores, MASKED)
                    top = jnp.max(scores, axis=1, keepdims=True)
                    unnormed = jnp.exp(scores - top)
                    row_sum = jnp.sum(unnormed, axis=1, keepdims=True)
                    part = matmul(unnormed.astype(low), held[head], PLAIN) / row_sum
                    top_ref[2 * pair + head, at, :] = top
                    sum_ref[2 * pair + head, at, :] = row_sum
                    total = part if total is None else total + part
                out_ref[at, pair * 128 : (pair + 1) * 128] = total
        for core, ref in ((0, even_ref), (1, odd_ref)):
            for k in range(n // 2):
                start = pl.multiple_of((place_ref[0] ^ (2 * k + core)) * rows, rows)
                ref[k] = out_ref[pl.ds(start, rows), :].astype(low)

    vmem = pl.BlockSpec(memory_space=pltpu.VMEM)
    results = pl.pallas_call(
        kernel,
        out_shape=[jax.ShapeDtypeStruct((n // 2, rows, q_cols), low)] * 2
        + [
            jax.ShapeDtypeStruct((length, q_cols), wide),
            jax.ShapeDtypeStruct((length, q_cols + 2 * HEAD_DIM), low),
            jax.ShapeDtypeStruct((heads_dev, length, 1), wide),
            jax.ShapeDtypeStruct((heads_dev, length, 1), wide),
        ],
        in_specs=[pl.BlockSpec(memory_space=pltpu.SMEM)] + [vmem] * 3,
        out_specs=[vmem] * 6,
        compiler_params=pltpu.CompilerParams(vmem_limit_bytes=48 * 2**20),
        cost_estimate=pl.CostEstimate(
            flops=2 * length * length * 128 * heads_dev,
            bytes_accessed=qkv.size * 8,
            transcendentals=length * length * heads_dev // 2,
        ),
    )(place, qkv, cosine, sine)
    return results[:2], *results[2:]


def attention_back(grads, rotated, out, tops, sums, cosine, sine, place):
    n, (_, rows, all_cols) = 2 * len(grads), grads[0].shape
    length, cols = rotated.shape
    q_cols = cols - 2 * HEAD_DIM
    heads_dev = q_cols // HEAD_DIM
    block = 256
    low, wide = jnp.bfloat16, jnp.float32

    def kernel(place_ref, rot_ref, out_ref, top_ref, sum_ref, cos_ref, sin_ref, *refs):
        grad_refs = refs[: n // 2]
        result_ref, others_ref, grad_ref, dq_ref, dk_ref, dv_ref = refs[n // 2 :]
        for k, ref in enumerate(grad_refs):
            for core in range(2):
                start = pl.multiple_of((place_ref[0] ^ (2 * k + core)) * rows, rows)
                grad_ref[pl.ds(start, rows), :] = ref[core, :, :q_cols]
                others_ref[core * (n // 2) + k] = ref[core, :, q_cols:]
        dk_ref[...] = jnp.zeros_like(dk_ref)
        dv_ref[...] = jnp.zeros_like(dv_ref)
        for i in range(length // block):
            span = (i + 1) * block
            keys, values, _ = key_copies(rot_ref[:span, q_cols:])
            held = [only(keys, 0), only(keys, 1)]
            shape = (block, span)
            seen = lax.broadcasted_iota(jnp.int32, shape, 1) <= i * block + (
                lax.broadcasted_iota(jnp.int32, shape, 0)
            )
            at = slice(i * block, (i + 1) * block)
            dk = dv = None
            for pair in range(q_cols // 128):
                pair_at = slice(pair * 128, (pair + 1) * 128)
                query = rot_ref[at, pair_at] * jnp.asarray(0.125, low)
                grad = grad_ref[at, pair_at].astype(wide)
                product = grad * out_ref[at, pair_at]
                dq = None
                for head in range(2):
                    row_sum = sum_ref[2 * pair + head, at, :]
                    own_query = only(query, head)
                    own_grad = only((grad / row_sum).astype(low), head)
                    scores = jnp.where(seen, matmul(own_query, keys, ROWS_OF), MASKED)
                    unnormed = jnp.exp(scores - top_ref[2 * pair + head, at, :])
                    shift = jnp.sum(only(product, head), axis=1, keepdims=True) / row_sum
                    grad_probs = matmul(own_grad, values, ROWS_OF)
                    grad_scores = (unnormed * (grad_probs - shift)).astype(low)
                    dq_part = matmul(grad_scores, held[head], PLAIN)
                    dk_part = matmul(grad_scores, own_query, COLUMNS_OF)
                    dv_part = matmul(unnormed.astype(low), own_grad, COLUMNS_OF)
                    dq = dq_part if dq is None else dq + dq_part
                    dk = dk_part if dk is None else dk + dk_part
                    dv = dv_part if dv is None else dv + dv_part
                dq_ref[at, pair_at] = dq * 0.125
            dk_ref[:span, :] += dk
            dv_ref[:span, :] += dv
        for t in range(n):
            slot = slot_of(place_ref[0] ^ t, n)
            at = slice(t * rows, (t + 1) * rows)
            dk, dv = dk_ref[at, :], dv_ref[at, :]
            first = lanes(dk.shape) < HEAD_DIM
            dk, dv = dk + pltpu.roll(dk, HEAD_DIM, 1), dv + pltpu.roll(dv, HEAD_DIM, 1)
            moved = turned(
                jnp.concatenate([dq_ref[at, :], dk], axis=1), cos_ref[slot], -sin_ref[slot]
            )
            result_ref[slot, :, :q_cols] = moved[:, :q_cols].astype(low)
            result_ref[slot, :, q_cols:] = jnp.where(first, moved[:, q_cols:], dv).astype(low)

    vmem = pl.BlockSpec(memory_space=pltpu.VMEM)
    return pl.pallas_call(
        kernel,
        out_shape=[
            jax.ShapeDtypeStruct((n, rows, cols), low),
            jax.ShapeDtypeStruct((n, rows, all_cols - q_cols), low),
        ],
        in_specs=[pl.BlockSpec(memory_space=pltpu.SMEM)] + [vmem] * (6 + n // 2),
        out_specs=[vmem] * 2,
        scratch_shapes=[
            pltpu.VMEM((length, q_cols), low),
            pltpu.VMEM((length, q_cols), wide),
            pltpu.VMEM((length, 128), wide),
            pltpu.VMEM((length, 128), wide),
        ],
        compiler_params=pltpu.CompilerParams(vmem_limit_bytes=48 * 2**20),
        cost_estimate=pl.CostEstimate(
            flops=5 * length * length * 128 * heads_dev,
            bytes_accessed=rotated.size * 8,
            transcendentals=length * length * heads_dev // 2,
        ),
    )(place, rotated, out, tops, sums, cosine, sine, *grads)


def silu_parts(gate):
    sigmoid_gate = 1.0 / (1.0 + jnp.exp(-gate))
    return sigmoid_gate, gate * sigmoid_gate


def hidden_units(normed, weights):
    rows, width = normed.shape
    cols = weights.shape[1]
    tile, ff_dev = 256, cols // 2

    def kernel(normed_ref, weights_ref, pre_ref, hidden_ref):
        pre = matmul(normed_ref[...], weights_ref[...], PLAIN)
        pre_ref[...] = pre
        hidden_ref[...] = (silu_parts(pre[:, :ff_dev])[1] * pre[:, ff_dev:]).astype(jnp.bfloat16)

    return pl.pallas_call(
        kernel,
        grid=(rows // tile,),
        out_shape=[
            jax.ShapeDtypeStruct((rows, cols), jnp.float32),
            jax.ShapeDtypeStruct((rows, ff_dev), jnp.bfloat16),
        ],
        in_specs=[
            pl.BlockSpec((tile, width), lambda i: (i, 0)),
            pl.BlockSpec((width, cols), lambda i: (0, 0)),
        ],
        out_specs=[
            pl.BlockSpec((tile, cols), lambda i: (i, 0)),
            pl.BlockSpec((tile, ff_dev), lambda i: (i, 0)),
        ],
        compiler_params=pltpu.CompilerParams(vmem_limit_bytes=48 * 2**20),
        cost_estimate=pl.CostEstimate(
            flops=2 * rows * width * cols, bytes_accessed=rows * cols * 8, transcendentals=rows * ff_dev
        ),
    )(normed, weights)


def hidden_back(dy, down, pre):
    rows, width = dy.shape
    ff_dev = down.shape[0]
    tile = 256

    def kernel(dy_ref, down_ref, pre_ref, out_ref):
        grad_hidden = matmul(dy_ref[...], down_ref[...], ROWS_OF)
        gate, upper = pre_ref[:, :ff_dev], pre_ref[:, ff_dev:]
        sigmoid_gate, activated = silu_parts(gate)
        grad_gate = grad_hidden * upper * (sigmoid_gate * (1.0 + gate * (1.0 - sigmoid_gate)))
        both = jnp.concatenate([grad_gate, grad_hidden * activated], axis=1)
        out_ref[...] = both.astype(jnp.bfloat16)

    return pl.pallas_call(
        kernel,
        grid=(rows // tile,),
        out_shape=jax.ShapeDtypeStruct((rows, 2 * ff_dev), jnp.bfloat16),
        in_specs=[
            pl.BlockSpec((tile, width), lambda i: (i, 0)),
            pl.BlockSpec((ff_dev, width), lambda i: (0, 0)),
            pl.BlockSpec((tile, 2 * ff_dev), lambda i: (i, 0)),
        ],
        out_specs=pl.BlockSpec((tile, 2 * ff_dev), lambda i: (i, 0)),
        compiler_params=pltpu.CompilerParams(vmem_limit_bytes=48 * 2**20),
        cost_estimate=pl.CostEstimate(
            flops=2 * rows * width * ff_dev, bytes_accessed=rows * ff_dev * 16, transcendentals=rows * ff_dev
        ),
    )(dy, down, pre)


def row_products(*pairs):
    rows, width = pairs[0][0].shape
    sizes = [right.shape[1] for _, right in pairs]
    tile = 512

    def kernel(*refs):
        at = 0
        for i, size in enumerate(sizes):
            product = matmul(refs[2 * i][...], refs[2 * i + 1][...], COLUMNS_OF)
            refs[-1][:, at : at + size] = product.astype(jnp.bfloat16)
            at += size

    return pl.pallas_call(
        kernel,
        grid=(width // tile,),
        out_shape=jax.ShapeDtypeStruct((width, sum(sizes)), jnp.bfloat16),
        in_specs=[
            spec
            for size in sizes
            for spec in (
                pl.BlockSpec((rows, tile), lambda i: (0, i)),
                pl.BlockSpec((rows, size), lambda i: (0, 0)),
            )
        ],
        out_specs=pl.BlockSpec((tile, sum(sizes)), lambda i: (i, 0)),
        compiler_params=pltpu.CompilerParams(vmem_limit_bytes=48 * 2**20),
        cost_estimate=pl.CostEstimate(
            flops=2 * rows * width * sum(sizes), bytes_accessed=rows * width * 4, transcendentals=0
        ),
    )(*[array for pair in pairs for array in pair])


def stage(sure, body, *args):
    shapes = jax.eval_shape(body, *args)

    def nothing(*_):
        return jax.tree.map(lambda leaf: jnp.zeros(leaf.shape, leaf.dtype), shapes)

    return lax.cond(sure, body, nothing, *args)


def columns_of(weight, place, groups, shards):
    width = weight.shape[1] // (groups * shards)
    return jnp.concatenate(
        [
            lax.dynamic_slice_in_dim(weight, (f * groups + place) * width, width, 1)
            for f in range(shards)
        ],
        axis=1,
    )


def on_device(
    tokens,
    positions,
    w_query,
    w_key,
    w_value,
    w_out,
    gain_attn,
    w_gate,
    w_up,
    w_down,
    gain_mlp,
    cotangent,
):
    low, wide = jnp.bfloat16, jnp.float32
    groups = lax.axis_size("seq")
    shards = lax.axis_size("fsdp")
    place = lax.axis_index("seq")
    shard = lax.axis_index("fsdp")
    tok_rows, width = tokens.shape[1:]
    shard_rows = w_query.shape[0]
    heads_dev = HEADS // groups
    kv_copies = groups // KV_HEADS
    seq_len = tok_rows * groups
    q_cols = heads_dev * HEAD_DIM
    out_cols = width // groups
    ff = w_gate.shape[1]
    ff_dev = ff // groups
    scale = HEAD_DIM ** (-0.5)

    def z_gather(part):
        return lax.all_gather(part, "fsdp", axis=0, tiled=True)

    def z_scatter(part):
        return lax.psum_scatter(part, "fsdp", scatter_dimension=0, tiled=True)

    def columns(weight, start, count):
        return lax.dynamic_slice_in_dim(weight, start, count, 1)

    place_arg = place.reshape(1).astype(jnp.int32)
    kv_head = place // kv_copies
    attn_own = jnp.concatenate(
        [
            columns(w_query, place * q_cols, q_cols),
            columns(w_key, kv_head * HEAD_DIM, HEAD_DIM),
            columns(w_value, kv_head * HEAD_DIM, HEAD_DIM),
            columns(w_out, place * out_cols, out_cols),
        ],
        axis=1,
    )
    attn_full = z_gather(attn_own)
    attn_full, out_part = attn_full[:, :-out_cols], attn_full[:, -out_cols:]
    mlp_own = jnp.concatenate(
        [columns_of(w_gate, place, groups, shards), columns_of(w_up, place, groups, shards)], axis=1
    )
    mlp_full = z_gather(mlp_own)
    down_rows = w_down.shape[0] // groups
    down_full = z_gather(lax.dynamic_slice_in_dim(w_down, place * down_rows, down_rows, 0))
    sure = positions[0, 0] >= 0
    own = tokens[0]
    gains_own = jnp.stack([gain_attn, gain_mlp]).astype(wide)

    halves = (slice(seq_len // 2, None), slice(0, seq_len // 2))

    def by_halves(product):
        def half(at):
            return product(at).astype(low).reshape(groups // 2, tok_rows, width)

        return scatter_chain(lambda: half(halves[0]), lambda: half(halves[1]))

    def inputs_stage(own, positions, gains_own):
        gains = lax.dynamic_update_slice(
            jnp.zeros((2, width), wide), gains_own, (0, shard * shard_rows)
        )
        gains, where, stream = together(
            ring_chain(gains), gather_chain(positions), gather_chain(own)
        )
        where, stream = where.reshape(seq_len), stream.reshape(seq_len, width).astype(wide)
        cosine, sine = rope_tables(where, HEAD_DIM)
        cosine, sine = cosine.reshape(groups, tok_rows, 128), sine.reshape(groups, tok_rows, 128)
        inverse_all = lax.rsqrt(jnp.mean(stream * stream, axis=-1, keepdims=True) + EPS)
        normed_in = (stream * inverse_all * gains[0]).astype(low)
        return gains, cosine, sine, normed_in

    gains, cosine, sine, normed_in = stage(sure, inputs_stage, own, positions, gains_own)
    gain_in, gain_mid = gains

    def attention_stage(own, cotangent, normed_in, attn_full, out_part, cosine, sine, gain_mid):
        def attend(_):
            qkv = jnp.dot(normed_in, attn_full, preferred_element_type=wide)
            return (
                yield attention(
                    qkv.reshape(groups, tok_rows, -1), cosine, sine, place_arg, heads_dev
                )
            )

        def exchange(attended):
            pairs = yield from exchange_chain(*attended[0])
            return join_columns(pairs, place_arg), attended[1:]

        def project(results):
            attended_tok, kept = results
            while not out_box:
                yield ()
            out_full = join_weight(*out_box[0], place_arg)
            middle = own.astype(wide) + jnp.dot(attended_tok, out_full, preferred_element_type=wide)
            inverse_mid = lax.rsqrt(jnp.mean(middle * middle, axis=-1, keepdims=True) + EPS)
            normed_mid = yield from gather_chain((middle * inverse_mid * gain_mid).astype(low))
            return attended_tok, out_full, middle, normed_mid.reshape(seq_len, width), kept

        out_box = []

        def weight():
            out_box.append((yield from halves_chain(out_part)))

        _, results, (_, dy) = together(
            weight(),
            in_turn(attend, exchange, project),
            in_turn(lambda _: held(cotangent, 1), lambda later: pair_chain(gather_chain(later))),
        )
        return *results, dy.reshape(seq_len, width)

    def pair_chain(chain):
        return None, (yield from chain)

    attended_tok, out_full, middle, normed_mid, kept, dy = stage(
        sure, attention_stage, own, cotangent[0], normed_in, attn_full, out_part, cosine, sine, gain_mid
    )

    def hidden_stage(normed_mid, mlp_full, dy, attended_tok):
        def products():
            mlp_pre, hidden = yield hidden_units(normed_mid, mlp_full)
            down_grad = yield dot(hidden, dy, ((0,), (0,))).astype(low)
            return mlp_pre, hidden, down_grad

        results, attended_all = together(products(), gather_chain(attended_tok))
        return attended_all.reshape(seq_len, -1), *results

    attended_all, mlp_pre, hidden, down_grad = stage(
        sure, hidden_stage, normed_mid, mlp_full, dy, attended_tok
    )
    down_sum = z_scatter(down_grad)
    grad_mlp = hidden_back(after(dy, down_grad), down_full, mlp_pre)

    def middle_stage(grad_mlp, mlp_full, normed_mid, middle, dy_own, gain_mid, out_full):
        inverse_mid = lax.rsqrt(jnp.mean(middle * middle, axis=-1, keepdims=True) + EPS)
        unit_mid = middle * inverse_mid
        grad_normed_mid, results = together(
            by_halves(lambda at: dot(grad_mlp[at], mlp_full, ((1,), (1,)))),
            work(None, None, lambda: row_products((normed_mid, grad_mlp))),
        )
        grad_middle = norm_back(grad_normed_mid * gain_mid, unit_mid, inverse_mid)
        grad_middle = grad_middle + dy_own.astype(wide)
        grad_proj = grad_middle.astype(low)
        grad_attended = dot(grad_proj, out_full, ((1,), (1,))).astype(low)
        grad_even, grad_odd = split_columns((grad_attended, grad_proj), place_arg, groups)
        return grad_middle, grad_even, grad_odd, results[-1]

    grad_middle, grad_even, grad_odd, mlp_grad = stage(
        sure, middle_stage, grad_mlp, mlp_full, normed_mid, middle, cotangent[0], gain_mid, out_full
    )
    mlp_sum = z_scatter(mlp_grad)

    def back_stage(
        grad_even, grad_odd, attended_all, normed_in, cosine, sine, kept, down_sum, own, attn_full,
        gain_in, grad_middle, hidden, down_full, middle,
    ):
        wide_out, rotated, tops, sums = kept

        def back(pairs):
            grad_qkv, grad_proj_cols = yield attention_back(
                pairs, rotated, wide_out, tops, sums, cosine, sine, place_arg
            )
            grad_qkv = grad_qkv.reshape(seq_len, -1)
            terms = yield row_products(
                (normed_in, grad_qkv), (attended_all, grad_proj_cols.reshape(seq_len, out_cols))
            )
            grad_normed_in = yield from by_halves(
                lambda at: dot(grad_qkv[at], attn_full, ((1,), (1,)))
            )
            return grad_normed_in, terms

        (grad_normed_in, attn_terms), down_halves, down_term = together(
            in_turn(lambda _: exchange_chain(grad_even, grad_odd), back),
            in_turn(lambda _: held(down_sum, 2), halves_chain),
            in_turn(
                lambda _: held(hidden, 2),
                lambda later: by_halves(
                    lambda at: jnp.dot(later[at], down_full, preferred_element_type=wide)
                ),
            ),
        )
        stream_own = own.astype(wide)
        inverse_in = lax.rsqrt(jnp.mean(stream_own * stream_own, axis=-1, keepdims=True) + EPS)
        unit_in = stream_own * inverse_in
        grad_stream = norm_back(grad_normed_in * gain_in, unit_in, inverse_in) + grad_middle
        return grad_stream, attn_terms, (middle + down_term).astype(low), *down_halves

    grad_stream, attn_terms, layer_out, down_even, down_odd = stage(
        sure, back_stage, grad_even, grad_odd, attended_all, normed_in, cosine, sine, kept,
        after(down_sum, grad_even), own, attn_full, gain_in, grad_middle, hidden, down_full, middle,
    )

    attn_sum = z_scatter(attn_terms)

    def output_stage(down_even, down_odd, mlp_sum):
        (grad_down,), mine = together(
            work(lambda: put_rows(down_even, down_odd, place_arg)), near_chain(mlp_sum)
        )
        return grad_down, mine

    grad_down, mine = stage(sure, output_stage, down_even, down_odd, after(mlp_sum, attn_terms))

    def last_stage(mine, mlp_sum, mlp_own, attn_sum, attn_own):
        def columns_put():
            halves_all, filled = (mine, swap(mine, 1)), ()
            for part in range(4):
                filled = put_columns(*halves_all, place_arg, shards, part, 4, filled)
                if part:
                    filled = yield filled
            return filled

        def sums_chain():
            pairs = ((attn_sum[:, :-out_cols], attn_own[:, :-out_cols]), (mlp_sum, mlp_own))
            sums = [jnp.sum(a.astype(wide) * b.astype(wide), axis=1) for a, b in pairs]
            sums, mask = jnp.stack(sums), 1
            while mask < groups:
                sums = sums + (yield swap(sums, mask))
                mask *= 2
            return sums

        puts, attn_halves, sums = together(columns_put(), halves_chain(attn_sum), sums_chain())
        return *puts, sums, *put_attention(*attn_halves, place_arg, q_cols, out_cols)

    grad_gate, grad_up, row_sums, grad_query, grad_key, grad_value, grad_out = stage(
        sure, last_stage, mine, mlp_sum, mlp_own, after(attn_sum, grad_down), attn_own
    )
    return (
        layer_out[None],
        grad_stream[None],
        grad_query,
        grad_key,
        grad_value,
        grad_out,
        row_sums[0] / gain_attn.astype(wide),
        grad_gate,
        grad_up,
        grad_down,
        row_sums[1] / gain_mlp.astype(wide),
    )


def solution(mesh):
    placed = (
        P("fsdp", "seq", None),
        P("fsdp", "seq"),
        P("fsdp", None),
        P("fsdp", None),
        P("fsdp", None),
        P("fsdp", None),
        P("fsdp"),
        P("fsdp", None),
        P("fsdp", None),
        P("fsdp", None),
        P("fsdp"),
        P("fsdp", "seq", None),
    )
    return jax.shard_map(
        on_device,
        mesh=mesh,
        in_specs=placed,
        out_specs=(
            P("fsdp", "seq", None),
            P("fsdp", "seq", None),
            P("fsdp", None),
            P("fsdp", None),
            P("fsdp", None),
            P("fsdp", None),
            P("fsdp"),
            P("fsdp", None),
            P("fsdp", None),
            P("fsdp", None),
            P("fsdp"),
        ),
        check_vma=False,
    )
```

```python
import math

import jax
import jax.numpy as jnp
from jax import lax
from jax.experimental import pallas as pl
from jax.experimental.pallas import tpu as pltpu
from jax.sharding import PartitionSpec as P

HEADS = 32
KV_HEADS = 4
HEAD_DIM = 64


EPS = 1e-05
ROPE_BASE = 10000.0


def rope_tables(positions, head_size):
    half_dim = head_size // 2
    lane = jnp.arange(128)
    freqs = jnp.exp(
        (lane % half_dim).astype(jnp.float32) * (-2.0 * math.log(ROPE_BASE) / head_size)
    )
    angles = positions.astype(jnp.float32)[..., None] * freqs
    sign = jnp.where(lane % head_size < half_dim, -1.0, 1.0)
    return jnp.cos(angles), jnp.sin(angles) * sign


def norm_back(grad_normed, normed, inverse):
    return inverse * (grad_normed - normed * jnp.mean(grad_normed * normed, axis=-1, keepdims=True))


def dot(left, right, dims):
    return lax.dot_general(left, right, ((dims[0], dims[1]), ((), ())), preferred_element_type=jnp.float32)


def swap(value, mask):
    return lax.ppermute(value, "seq", [(i, i ^ mask) for i in range(lax.axis_size("seq"))])


def place_pieces(pieces, places, shape):
    cols = shape[2]
    tile = 512 if cols % 512 == 0 else cols

    def kernel(*refs):
        for piece, (slot, row), ref in zip(pieces, places, refs):
            refs[-1][slot, row : row + piece.shape[0]] = ref[...]

    return pl.pallas_call(
        kernel,
        grid=(cols // tile,),
        out_shape=jax.ShapeDtypeStruct(shape, pieces[0].dtype),
        in_specs=[pl.BlockSpec((piece.shape[0], tile), lambda i: (0, i)) for piece in pieces],
        out_specs=pl.BlockSpec(shape[:2] + (tile,), lambda i: (0, 0, i)),
        compiler_params=pltpu.CompilerParams(vmem_limit_bytes=48 * 2**20),
        cost_estimate=pl.CostEstimate(flops=0, bytes_accessed=math.prod(shape) * 4, transcendentals=0),
    )(*pieces)


def after(value, *earlier):
    return lax.optimization_barrier((value, *earlier))[0]


def together(*chains):
    results, values, live = [None] * len(chains), [None] * len(chains), list(range(len(chains)))
    while live:
        sent = {}
        for i in live:
            try:
                sent[i] = chains[i].send(values[i])
            except StopIteration as stop:
                results[i] = stop.value
        live = list(sent)
        for i, value in lax.optimization_barrier(sent).items():
            values[i] = value
    return results


def work(*parts):
    results = []
    for part in parts:
        results.append((yield () if part is None else part()))
    return results


def held(value, steps):
    for _ in range(steps):
        value = yield value
    return value


def in_turn(*makers):
    result = None
    for maker in makers:
        result = yield from maker(result)
    return result


def near_chain(part):
    n = lax.axis_size("seq")
    if n == 8 and part.shape[0] % 16 == 0:
        half = part.shape[0] // 32 * 16
        by_x, by_y = yield swap(part, 2), swap(part, 4)
        far = yield swap(by_x[:half], 4), swap(by_y[half:], 2)
        places = ((0, 0), (1, 0), (2, 0), (3, 0), (3, half))
        return place_pieces((part, by_x, by_y, *far), places, (4,) + part.shape)
    mine, mask = part[None], 2
    while mask < n:
        mine = jnp.concatenate([mine, (yield swap(mine, mask))])
        mask *= 2
    return mine


def core_chain(mine):
    return (yield mine, swap(mine, 1))


def halves_chain(part):
    return in_turn(lambda _: near_chain(part), core_chain)


def gather_chain(part):
    mine, other = yield from halves_chain(part)
    if part.shape[0] % 16:
        return jnp.concatenate([mine, other])
    half, rows, cols = mine.shape
    tile = 512 if cols % 512 == 0 else cols

    def kernel(mine_ref, other_ref, out_ref):
        out_ref[:half] = mine_ref[...]
        out_ref[half:] = other_ref[...]

    return pl.pallas_call(
        kernel,
        grid=(cols // tile,),
        out_shape=jax.ShapeDtypeStruct((2 * half, rows, cols), part.dtype),
        in_specs=[pl.BlockSpec((half, rows, tile), lambda i: (0, 0, i))] * 2,
        out_specs=pl.BlockSpec((2 * half, rows, tile), lambda i: (0, 0, i)),
        cost_estimate=pl.CostEstimate(flops=0, bytes_accessed=mine.size * 8, transcendentals=0),
    )(mine, other)


def ring_chain(value):
    n = lax.axis_size("fsdp")
    moving = value
    for _ in range(n - 1):
        moving = yield lax.ppermute(moving, "fsdp", [(i, (i + 1) % n) for i in range(n)])
        value = value + moving
    return value


def scatter_chain(make_odd, make_even):
    n = lax.axis_size("seq")

    def add(own, other):
        return own.astype(jnp.float32) + other.astype(jnp.float32)

    low = jnp.bfloat16
    odd = make_odd()
    even, other = yield make_even(), swap(odd, 1)
    mine = add(even, other)
    if n == 8:
        half = even.shape[1] // 2
        far = mine[3].astype(low)
        from_x, from_y = yield swap(far[:half], 2), swap(far[half:], 4)
        to_y = jnp.concatenate([add(mine[2][:half], from_x), mine[2][half:]]).astype(low)
        to_x = jnp.concatenate([mine[1][:half], add(mine[1][half:], from_y)]).astype(low)
        by_x, by_y = yield swap(to_x, 2), swap(to_y, 4)
        return add(mine[0], by_x) + by_y.astype(jnp.float32)
    mask = n // 2
    while mask > 1:
        count = mine.shape[0] // 2
        mine = add(mine[:count], (yield swap(mine[count:].astype(low), mask)))
        mask //= 2
    return mine[0]


def ordered(place, even, odd, body):
    core = place & 1
    pl.when(core == 0)(lambda: body(even, odd))
    pl.when(core == 1)(lambda: body(odd, even))


def put_columns(even, odd, place, pieces, part, parts, earlier=()):
    half, rows, cols = even.shape
    n, w = 2 * half, cols // (2 * pieces)
    tile = 64
    steps = rows // parts // tile

    def kernel(place_ref, even_ref, odd_ref, *refs):
        chip = place_ref[0] // 2

        def body(first, other):
            blocks = [(other if t % 2 else first)[(t // 2) ^ chip] for t in range(n)]
            for target, start in zip(refs[-2:], (0, cols // 2)):
                for f in range(pieces):
                    at = start + f * w
                    row = jnp.concatenate([block[:, at : at + w] for block in blocks], axis=1)
                    target[:, f * n * w : (f + 1) * n * w] = row.astype(jnp.float32)

        ordered(place_ref[0], even_ref, odd_ref, body)

    spec = pl.BlockSpec((half, tile, cols), lambda i: (0, i + part * steps, 0))
    whole = jax.ShapeDtypeStruct((rows, pieces * n * w), jnp.float32)
    return pl.pallas_call(
        kernel,
        grid=(steps,),
        out_shape=(whole, whole),
        in_specs=[pl.BlockSpec(memory_space=pltpu.SMEM), spec, spec]
        + [pl.BlockSpec(memory_space=pl.ANY)] * len(earlier),
        out_specs=[pl.BlockSpec((tile, pieces * n * w), lambda i: (i + part * steps, 0))] * 2,
        input_output_aliases={3 + i: i for i in range(len(earlier))},
        compiler_params=pltpu.CompilerParams(vmem_limit_bytes=48 * 2**20),
        cost_estimate=pl.CostEstimate(flops=0, bytes_accessed=even.size * 6, transcendentals=0),
    )(place, even, odd, *earlier)


def put_rows(even, odd, place):
    half, rows, cols = even.shape
    tile = 256

    def kernel(place_ref, even_ref, odd_ref, out_ref):
        chip = place_ref[0] // 2

        def body(first, second):
            for t in range(2 * half):
                block = (second if t % 2 else first)[(t // 2) ^ chip]
                out_ref[t * rows : (t + 1) * rows, :] = block.astype(jnp.float32)

        ordered(place_ref[0], even_ref, odd_ref, body)

    spec = pl.BlockSpec((half, rows, tile), lambda i: (0, 0, i))
    return pl.pallas_call(
        kernel,
        grid=(cols // tile,),
        out_shape=jax.ShapeDtypeStruct((2 * half * rows, cols), jnp.float32),
        in_specs=[pl.BlockSpec(memory_space=pltpu.SMEM), spec, spec],
        out_specs=pl.BlockSpec((2 * half * rows, tile), lambda i: (0, i)),
        compiler_params=pltpu.CompilerParams(vmem_limit_bytes=48 * 2**20),
        cost_estimate=pl.CostEstimate(flops=0, bytes_accessed=even.size * 12, transcendentals=0),
    )(place, even, odd)


def put_attention(even, odd, place, q_cols, out_cols):
    half, rows, cols = even.shape
    n, tile = 2 * half, 64
    copies = n // KV_HEADS
    sizes = (n * q_cols, KV_HEADS * HEAD_DIM, KV_HEADS * HEAD_DIM, n * out_cols)

    def kernel(place_ref, even_ref, odd_ref, query_ref, key_ref, value_ref, out_ref):
        chip = place_ref[0] // 2

        def body(first, second):
            blocks = [
                (second if t % 2 else first)[(t // 2) ^ chip].astype(jnp.float32) for t in range(n)
            ]
            for t, block in enumerate(blocks):
                query_ref[:, t * q_cols : (t + 1) * q_cols] = block[:, :q_cols]
                out_ref[:, t * out_cols : (t + 1) * out_cols] = block[:, cols - out_cols :]
            sums = [
                sum(block[:, q_cols : q_cols + 2 * HEAD_DIM] for block in blocks[h * copies : (h + 1) * copies])
                for h in range(KV_HEADS)
            ]
            key_ref[...] = jnp.concatenate([part[:, :HEAD_DIM] for part in sums], axis=1)
            value_ref[...] = jnp.concatenate([part[:, HEAD_DIM:] for part in sums], axis=1)

        ordered(place_ref[0], even_ref, odd_ref, body)

    spec = pl.BlockSpec((half, tile, cols), lambda i: (0, i, 0))
    return pl.pallas_call(
        kernel,
        grid=(rows // tile,),
        out_shape=[jax.ShapeDtypeStruct((rows, size), jnp.float32) for size in sizes],
        in_specs=[pl.BlockSpec(memory_space=pltpu.SMEM), spec, spec],
        out_specs=[pl.BlockSpec((tile, size), lambda i: (i, 0)) for size in sizes],
        compiler_params=pltpu.CompilerParams(vmem_limit_bytes=48 * 2**20),
        cost_estimate=pl.CostEstimate(flops=0, bytes_accessed=even.size * 12, transcendentals=0),
    )(place, even, odd)


def slot_of(mask, n):
    return (mask >> 1) + (mask & 1) * (n // 2)


def split_columns(parts, place, n):
    rows = parts[0].shape[0]
    sizes = [part.shape[1] // n for part in parts]
    half, cols = n // 2, sum(sizes)

    def kernel(place_ref, *refs):
        for core, ref in enumerate(refs[-2:]):
            for k in range(half):
                block, at = place_ref[0] ^ (2 * k + core), 0
                for size, part_ref in zip(sizes, refs):
                    start = pl.multiple_of(block * size, size)
                    ref[k, :, at : at + size] = part_ref[:, pl.ds(start, size)]
                    at += size

    vmem = pl.BlockSpec(memory_space=pltpu.VMEM)
    return pl.pallas_call(
        kernel,
        out_shape=[jax.ShapeDtypeStruct((half, rows, cols), parts[0].dtype)] * 2,
        in_specs=[pl.BlockSpec(memory_space=pltpu.SMEM)] + [vmem] * len(parts),
        out_specs=[vmem] * 2,
    )(place, *parts)


def exchange_chain(even, odd):
    half, rows, cols = even.shape
    other = yield swap(odd, 1)

    def kernel(even_ref, other_ref, *refs):
        for k, ref in enumerate(refs):
            ref[0] = even_ref[k]
            ref[1] = other_ref[k]

    vmem = pl.BlockSpec(memory_space=pltpu.VMEM)
    pairs = pl.pallas_call(
        kernel,
        out_shape=[jax.ShapeDtypeStruct((2, rows, cols), even.dtype)] * half,
        in_specs=[vmem] * 2,
        out_specs=[vmem] * half,
    )(even, other)
    return (yield [pair if k == 0 else swap(pair, 2 * k) for k, pair in enumerate(pairs)])


def join_columns(pairs, place):
    n, (_, rows, cols) = 2 * len(pairs), pairs[0].shape

    def kernel(place_ref, *refs):
        for k, ref in enumerate(refs[:-1]):
            for core in range(2):
                start = pl.multiple_of((place_ref[0] ^ (2 * k + core)) * cols, cols)
                refs[-1][:, pl.ds(start, cols)] = ref[core]

    vmem = pl.BlockSpec(memory_space=pltpu.VMEM)
    return pl.pallas_call(
        kernel,
        out_shape=jax.ShapeDtypeStruct((rows, n * cols), pairs[0].dtype),
        in_specs=[pl.BlockSpec(memory_space=pltpu.SMEM)] + [vmem] * len(pairs),
        out_specs=vmem,
    )(place, *pairs)


def join_weight(even, odd, place):
    half, rows, cols = even.shape
    n, tile = 2 * half, 512

    def kernel(place_ref, even_ref, odd_ref, out_ref):
        for ref, core in ((even_ref, 0), (odd_ref, 1)):
            for k in range(half):
                start = pl.multiple_of((place_ref[0] ^ (2 * k + core)) * cols, cols)
                out_ref[:, pl.ds(start, cols)] = ref[k]

    spec = pl.BlockSpec((half, tile, cols), lambda i: (0, i, 0))
    return pl.pallas_call(
        kernel,
        grid=(rows // tile,),
        out_shape=jax.ShapeDtypeStruct((rows, n * cols), even.dtype),
        in_specs=[pl.BlockSpec(memory_space=pltpu.SMEM), spec, spec],
        out_specs=pl.BlockSpec((tile, n * cols), lambda i: (i, 0)),
        compiler_params=pltpu.CompilerParams(vmem_limit_bytes=48 * 2**20),
        cost_estimate=pl.CostEstimate(flops=0, bytes_accessed=even.size * 8, transcendentals=0),
    )(place, even, odd)


def lanes(shape):
    return lax.broadcasted_iota(jnp.int32, shape, 1)


def halves_swapped(value):
    first = lanes(value.shape) % HEAD_DIM < HEAD_DIM // 2
    size = value.shape[1]
    left, right = pltpu.roll(value, size - HEAD_DIM // 2, 1), pltpu.roll(value, HEAD_DIM // 2, 1)
    return jnp.where(first, left, right)


def turned(value, cosine, sine):
    parts = [
        value[:, i : i + 128] * cosine + halves_swapped(value[:, i : i + 128]) * sine
        for i in range(0, value.shape[1], 128)
    ]
    return jnp.concatenate(parts, axis=1)


def key_copies(key_value):
    first = lanes(key_value.shape) < HEAD_DIM
    turned_over = pltpu.roll(key_value, HEAD_DIM, 1)
    keys = jnp.where(first, key_value, turned_over)
    values = jnp.where(first, turned_over, key_value)
    return keys, values, first


def only(value, head):
    first = lanes(value.shape) < HEAD_DIM
    return jnp.where(first if head == 0 else ~first, value, jnp.zeros_like(value))


def matmul(left, right, dims):
    return lax.dot_general(left, right, (dims, ((), ())), preferred_element_type=jnp.float32)


ROWS_OF = ((1,), (1,))
PLAIN = ((1,), (0,))
COLUMNS_OF = ((0,), (0,))
MASKED = -1e30


def attention(qkv, cosine, sine, place, heads_dev):
    n, rows, cols = qkv.shape
    length, q_cols = n * rows, heads_dev * HEAD_DIM
    block = 256
    low, wide = jnp.bfloat16, jnp.float32

    def kernel(place_ref, qkv_ref, cos_ref, sin_ref, *refs):
        even_ref, odd_ref, out_ref, rot_ref, top_ref, sum_ref = refs
        for t in range(n):
            slot = slot_of(place_ref[0] ^ t, n)
            value = qkv_ref[slot]
            moved = turned(value[:, : q_cols + 128], cos_ref[slot], sin_ref[slot])
            key_value = jnp.where(
                lanes((rows, 128)) < HEAD_DIM, moved[:, q_cols:], value[:, q_cols:]
            )
            at = slice(t * rows, (t + 1) * rows)
            rot_ref[at, :q_cols] = moved[:, :q_cols].astype(low)
            rot_ref[at, q_cols:] = key_value.astype(low)
        for i in range(length // block):
            span = (i + 1) * block
            key_value = rot_ref[:span, q_cols:]
            keys, values, _ = key_copies(key_value)
            held = [only(values, 0), only(values, 1)]
            shape = (block, span)
            seen = lax.broadcasted_iota(jnp.int32, shape, 1) <= i * block + (
                lax.broadcasted_iota(jnp.int32, shape, 0)
            )
            at = slice(i * block, (i + 1) * block)
            for pair in range(q_cols // 128):
                query = rot_ref[at, pair * 128 : (pair + 1) * 128] * jnp.asarray(0.125, low)
                total = None
                for head in range(2):
                    scores = matmul(only(query, head), keys, ROWS_OF)
                    scores = jnp.where(seen, scores, MASKED)
                    top = jnp.max(scores, axis=1, keepdims=True)
                    unnormed = jnp.exp(scores - top)
                    row_sum = jnp.sum(unnormed, axis=1, keepdims=True)
                    part = matmul(unnormed.astype(low), held[head], PLAIN) / row_sum
                    top_ref[2 * pair + head, at, :] = top
                    sum_ref[2 * pair + head, at, :] = row_sum
                    total = part if total is None else total + part
                out_ref[at, pair * 128 : (pair + 1) * 128] = total
        for core, ref in ((0, even_ref), (1, odd_ref)):
            for k in range(n // 2):
                start = pl.multiple_of((place_ref[0] ^ (2 * k + core)) * rows, rows)
                ref[k] = out_ref[pl.ds(start, rows), :].astype(low)

    vmem = pl.BlockSpec(memory_space=pltpu.VMEM)
    results = pl.pallas_call(
        kernel,
        out_shape=[jax.ShapeDtypeStruct((n // 2, rows, q_cols), low)] * 2
        + [
            jax.ShapeDtypeStruct((length, q_cols), wide),
            jax.ShapeDtypeStruct((length, q_cols + 2 * HEAD_DIM), low),
            jax.ShapeDtypeStruct((heads_dev, length, 1), wide),
            jax.ShapeDtypeStruct((heads_dev, length, 1), wide),
        ],
        in_specs=[pl.BlockSpec(memory_space=pltpu.SMEM)] + [vmem] * 3,
        out_specs=[vmem] * 6,
        compiler_params=pltpu.CompilerParams(vmem_limit_bytes=48 * 2**20),
        cost_estimate=pl.CostEstimate(
            flops=2 * length * length * 128 * heads_dev,
            bytes_accessed=qkv.size * 8,
            transcendentals=length * length * heads_dev // 2,
        ),
    )(place, qkv, cosine, sine)
    return results[:2], *results[2:]


def attention_back(grads, rotated, out, tops, sums, cosine, sine, place):
    n, (_, rows, all_cols) = 2 * len(grads), grads[0].shape
    length, cols = rotated.shape
    q_cols = cols - 2 * HEAD_DIM
    heads_dev = q_cols // HEAD_DIM
    block = 256
    low, wide = jnp.bfloat16, jnp.float32

    def kernel(place_ref, rot_ref, out_ref, top_ref, sum_ref, cos_ref, sin_ref, *refs):
        grad_refs = refs[: n // 2]
        result_ref, others_ref, grad_ref, dq_ref, dk_ref, dv_ref = refs[n // 2 :]
        for k, ref in enumerate(grad_refs):
            for core in range(2):
                start = pl.multiple_of((place_ref[0] ^ (2 * k + core)) * rows, rows)
                grad_ref[pl.ds(start, rows), :] = ref[core, :, :q_cols]
                others_ref[core * (n // 2) + k] = ref[core, :, q_cols:]
        dk_ref[...] = jnp.zeros_like(dk_ref)
        dv_ref[...] = jnp.zeros_like(dv_ref)
        for i in range(length // block):
            span = (i + 1) * block
            keys, values, _ = key_copies(rot_ref[:span, q_cols:])
            held = [only(keys, 0), only(keys, 1)]
            shape = (block, span)
            seen = lax.broadcasted_iota(jnp.int32, shape, 1) <= i * block + (
                lax.broadcasted_iota(jnp.int32, shape, 0)
            )
            at = slice(i * block, (i + 1) * block)
            dk = dv = None
            for pair in range(q_cols // 128):
                pair_at = slice(pair * 128, (pair + 1) * 128)
                query = rot_ref[at, pair_at] * jnp.asarray(0.125, low)
                grad = grad_ref[at, pair_at].astype(wide)
                product = grad * out_ref[at, pair_at]
                dq = None
                for head in range(2):
                    row_sum = sum_ref[2 * pair + head, at, :]
                    own_query = only(query, head)
                    own_grad = only((grad / row_sum).astype(low), head)
                    scores = jnp.where(seen, matmul(own_query, keys, ROWS_OF), MASKED)
                    unnormed = jnp.exp(scores - top_ref[2 * pair + head, at, :])
                    shift = jnp.sum(only(product, head), axis=1, keepdims=True) / row_sum
                    grad_probs = matmul(own_grad, values, ROWS_OF)
                    grad_scores = (unnormed * (grad_probs - shift)).astype(low)
                    dq_part = matmul(grad_scores, held[head], PLAIN)
                    dk_part = matmul(grad_scores, own_query, COLUMNS_OF)
                    dv_part = matmul(unnormed.astype(low), own_grad, COLUMNS_OF)
                    dq = dq_part if dq is None else dq + dq_part
                    dk = dk_part if dk is None else dk + dk_part
                    dv = dv_part if dv is None else dv + dv_part
                dq_ref[at, pair_at] = dq * 0.125
            dk_ref[:span, :] += dk
            dv_ref[:span, :] += dv
        for t in range(n):
            slot = slot_of(place_ref[0] ^ t, n)
            at = slice(t * rows, (t + 1) * rows)
            dk, dv = dk_ref[at, :], dv_ref[at, :]
            first = lanes(dk.shape) < HEAD_DIM
            dk, dv = dk + pltpu.roll(dk, HEAD_DIM, 1), dv + pltpu.roll(dv, HEAD_DIM, 1)
            moved = turned(
                jnp.concatenate([dq_ref[at, :], dk], axis=1), cos_ref[slot], -sin_ref[slot]
            )
            result_ref[slot, :, :q_cols] = moved[:, :q_cols].astype(low)
            result_ref[slot, :, q_cols:] = jnp.where(first, moved[:, q_cols:], dv).astype(low)

    vmem = pl.BlockSpec(memory_space=pltpu.VMEM)
    return pl.pallas_call(
        kernel,
        out_shape=[
            jax.ShapeDtypeStruct((n, rows, cols), low),
            jax.ShapeDtypeStruct((n, rows, all_cols - q_cols), low),
        ],
        in_specs=[pl.BlockSpec(memory_space=pltpu.SMEM)] + [vmem] * (6 + n // 2),
        out_specs=[vmem] * 2,
        scratch_shapes=[
            pltpu.VMEM((length, q_cols), low),
            pltpu.VMEM((length, q_cols), wide),
            pltpu.VMEM((length, 128), wide),
            pltpu.VMEM((length, 128), wide),
        ],
        compiler_params=pltpu.CompilerParams(vmem_limit_bytes=48 * 2**20),
        cost_estimate=pl.CostEstimate(
            flops=5 * length * length * 128 * heads_dev,
            bytes_accessed=rotated.size * 8,
            transcendentals=length * length * heads_dev // 2,
        ),
    )(place, rotated, out, tops, sums, cosine, sine, *grads)


def silu_parts(gate):
    sigmoid_gate = 1.0 / (1.0 + jnp.exp(-gate))
    return sigmoid_gate, gate * sigmoid_gate


def hidden_units(normed, weights):
    rows, width = normed.shape
    cols = weights.shape[1]
    tile, ff_dev = 256, cols // 2

    def kernel(normed_ref, weights_ref, pre_ref, hidden_ref):
        pre = matmul(normed_ref[...], weights_ref[...], PLAIN)
        pre_ref[...] = pre
        hidden_ref[...] = (silu_parts(pre[:, :ff_dev])[1] * pre[:, ff_dev:]).astype(jnp.bfloat16)

    return pl.pallas_call(
        kernel,
        grid=(rows // tile,),
        out_shape=[
            jax.ShapeDtypeStruct((rows, cols), jnp.float32),
            jax.ShapeDtypeStruct((rows, ff_dev), jnp.bfloat16),
        ],
        in_specs=[
            pl.BlockSpec((tile, width), lambda i: (i, 0)),
            pl.BlockSpec((width, cols), lambda i: (0, 0)),
        ],
        out_specs=[
            pl.BlockSpec((tile, cols), lambda i: (i, 0)),
            pl.BlockSpec((tile, ff_dev), lambda i: (i, 0)),
        ],
        compiler_params=pltpu.CompilerParams(vmem_limit_bytes=48 * 2**20),
        cost_estimate=pl.CostEstimate(
            flops=2 * rows * width * cols, bytes_accessed=rows * cols * 8, transcendentals=rows * ff_dev
        ),
    )(normed, weights)


def hidden_back(dy, down, pre):
    rows, width = dy.shape
    ff_dev = down.shape[0]
    tile = 256

    def kernel(dy_ref, down_ref, pre_ref, out_ref):
        grad_hidden = matmul(dy_ref[...], down_ref[...], ROWS_OF)
        gate, upper = pre_ref[:, :ff_dev], pre_ref[:, ff_dev:]
        sigmoid_gate, activated = silu_parts(gate)
        grad_gate = grad_hidden * upper * (sigmoid_gate * (1.0 + gate * (1.0 - sigmoid_gate)))
        both = jnp.concatenate([grad_gate, grad_hidden * activated], axis=1)
        out_ref[...] = both.astype(jnp.bfloat16)

    return pl.pallas_call(
        kernel,
        grid=(rows // tile,),
        out_shape=jax.ShapeDtypeStruct((rows, 2 * ff_dev), jnp.bfloat16),
        in_specs=[
            pl.BlockSpec((tile, width), lambda i: (i, 0)),
            pl.BlockSpec((ff_dev, width), lambda i: (0, 0)),
            pl.BlockSpec((tile, 2 * ff_dev), lambda i: (i, 0)),
        ],
        out_specs=pl.BlockSpec((tile, 2 * ff_dev), lambda i: (i, 0)),
        compiler_params=pltpu.CompilerParams(vmem_limit_bytes=48 * 2**20),
        cost_estimate=pl.CostEstimate(
            flops=2 * rows * width * ff_dev, bytes_accessed=rows * ff_dev * 16, transcendentals=rows * ff_dev
        ),
    )(dy, down, pre)


def row_products(*pairs):
    rows, width = pairs[0][0].shape
    sizes = [right.shape[1] for _, right in pairs]
    tile = 512

    def kernel(*refs):
        at = 0
        for i, size in enumerate(sizes):
            product = matmul(refs[2 * i][...], refs[2 * i + 1][...], COLUMNS_OF)
            refs[-1][:, at : at + size] = product.astype(jnp.bfloat16)
            at += size

    return pl.pallas_call(
        kernel,
        grid=(width // tile,),
        out_shape=jax.ShapeDtypeStruct((width, sum(sizes)), jnp.bfloat16),
        in_specs=[
            spec
            for size in sizes
            for spec in (
                pl.BlockSpec((rows, tile), lambda i: (0, i)),
                pl.BlockSpec((rows, size), lambda i: (0, 0)),
            )
        ],
        out_specs=pl.BlockSpec((tile, sum(sizes)), lambda i: (i, 0)),
        compiler_params=pltpu.CompilerParams(vmem_limit_bytes=48 * 2**20),
        cost_estimate=pl.CostEstimate(
            flops=2 * rows * width * sum(sizes), bytes_accessed=rows * width * 4, transcendentals=0
        ),
    )(*[array for pair in pairs for array in pair])


def stage(sure, body, *args):
    shapes = jax.eval_shape(body, *args)

    def nothing(*_):
        return jax.tree.map(lambda leaf: jnp.zeros(leaf.shape, leaf.dtype), shapes)

    return lax.cond(sure, body, nothing, *args)


def own_columns(place, w_query, w_key, w_value, w_out, n):
    rows, q_cols, out_cols = w_query.shape[0], w_query.shape[1] // n, w_out.shape[1] // n
    cols = q_cols + 2 * HEAD_DIM + out_cols

    def kernel(place_ref, query_ref, key_ref, value_ref, out_ref, result_ref):
        result_ref[:, :q_cols] = query_ref[...]
        result_ref[:, cols - out_cols :] = out_ref[...]
        for head in range(KV_HEADS):
            at = slice(head * HEAD_DIM, (head + 1) * HEAD_DIM)

            @pl.when(place_ref[0] // (n // KV_HEADS) == head)
            def _(at=at):
                both = jnp.concatenate([key_ref[:, at], value_ref[:, at]], axis=1)
                result_ref[:, q_cols : q_cols + 2 * HEAD_DIM] = both

    tile = rows // 2
    return pl.pallas_call(
        kernel,
        grid_spec=pltpu.PrefetchScalarGridSpec(
            num_scalar_prefetch=1,
            grid=(2,),
            in_specs=[
                pl.BlockSpec((tile, q_cols), lambda i, place_ref: (i, place_ref[0])),
                pl.BlockSpec((tile, w_key.shape[1]), lambda i, place_ref: (i, 0)),
                pl.BlockSpec((tile, w_value.shape[1]), lambda i, place_ref: (i, 0)),
                pl.BlockSpec((tile, out_cols), lambda i, place_ref: (i, place_ref[0])),
            ],
            out_specs=pl.BlockSpec((tile, cols), lambda i, place_ref: (i, 0)),
        ),
        out_shape=jax.ShapeDtypeStruct((rows, cols), w_query.dtype),
        cost_estimate=pl.CostEstimate(flops=0, bytes_accessed=rows * cols * 6, transcendentals=0),
    )(place, w_query, w_key, w_value, w_out)


def columns_of(weight, place, groups, shards):
    width = weight.shape[1] // (groups * shards)
    return jnp.concatenate(
        [
            lax.dynamic_slice_in_dim(weight, (f * groups + place) * width, width, 1)
            for f in range(shards)
        ],
        axis=1,
    )


def on_device(
    tokens,
    positions,
    w_query,
    w_key,
    w_value,
    w_out,
    gain_attn,
    w_gate,
    w_up,
    w_down,
    gain_mlp,
    cotangent,
):
    low, wide = jnp.bfloat16, jnp.float32
    groups = lax.axis_size("seq")
    shards = lax.axis_size("fsdp")
    place = lax.axis_index("seq")
    shard = lax.axis_index("fsdp")
    tok_rows, width = tokens.shape[1:]
    shard_rows = w_query.shape[0]
    heads_dev = HEADS // groups
    seq_len = tok_rows * groups
    q_cols = heads_dev * HEAD_DIM
    out_cols = width // groups

    def z_gather(part):
        return lax.all_gather(part, "fsdp", axis=0, tiled=True)

    def z_scatter(part):
        return lax.psum_scatter(part, "fsdp", scatter_dimension=0, tiled=True)

    def columns(weight, start, count):
        return lax.dynamic_slice_in_dim(weight, start, count, 1)

    place_arg = place.reshape(1).astype(jnp.int32)
    attn_own = own_columns(place_arg, w_query, w_key, w_value, w_out, groups)
    attn_full = z_gather(attn_own)
    attn_full, out_part = attn_full[:, :-out_cols], attn_full[:, -out_cols:]
    mlp_own = jnp.concatenate(
        [columns_of(w_gate, place, groups, shards), columns_of(w_up, place, groups, shards)], axis=1
    )
    mlp_full = z_gather(mlp_own)
    down_rows = w_down.shape[0] // groups
    down_full = z_gather(lax.dynamic_slice_in_dim(w_down, place * down_rows, down_rows, 0))
    sure = positions[0, 0] >= 0
    own = tokens[0]
    gains_own = jnp.stack([gain_attn, gain_mlp]).astype(wide)

    halves = (slice(seq_len // 2, None), slice(0, seq_len // 2))

    def half_of(product, at):
        return product(at).astype(low).reshape(groups // 2, tok_rows, width)

    def by_halves(product):
        return scatter_chain(
            lambda: half_of(product, halves[0]), lambda: half_of(product, halves[1])
        )

    def inputs_stage(own, positions, gains_own):
        gains = lax.dynamic_update_slice(
            jnp.zeros((2, width), wide), gains_own, (0, shard * shard_rows)
        )
        gains, where, stream = together(
            ring_chain(gains), gather_chain(positions), gather_chain(own)
        )
        where, stream = where.reshape(seq_len), stream.reshape(seq_len, width).astype(wide)
        cosine, sine = rope_tables(where, HEAD_DIM)
        cosine, sine = cosine.reshape(groups, tok_rows, 128), sine.reshape(groups, tok_rows, 128)
        inverse_all = lax.rsqrt(jnp.mean(stream * stream, axis=-1, keepdims=True) + EPS)
        normed_in = (stream * inverse_all * gains[0]).astype(low)
        return gains, cosine, sine, normed_in

    gains, cosine, sine, normed_in = stage(sure, inputs_stage, own, positions, gains_own)
    gain_in, gain_mid = gains

    def attention_stage(own, cotangent, normed_in, attn_full, out_part, cosine, sine, gain_mid):
        def attend(_):
            qkv = jnp.dot(normed_in, attn_full, preferred_element_type=wide)
            return (
                yield attention(
                    qkv.reshape(groups, tok_rows, -1), cosine, sine, place_arg, heads_dev
                )
            )

        def exchange(attended):
            pairs = yield from exchange_chain(*attended[0])
            return join_columns(pairs, place_arg), attended[1:]

        def project(results):
            attended_tok, kept = results
            while not out_box:
                yield ()
            out_full = join_weight(*out_box[0], place_arg)
            middle = own.astype(wide) + jnp.dot(attended_tok, out_full, preferred_element_type=wide)
            inverse_mid = lax.rsqrt(jnp.mean(middle * middle, axis=-1, keepdims=True) + EPS)
            normed_mid = yield from gather_chain((middle * inverse_mid * gain_mid).astype(low))
            return attended_tok, out_full, middle, normed_mid.reshape(seq_len, width), kept

        out_box = []

        def weight():
            out_box.append((yield from halves_chain(out_part)))

        _, results, (_, dy) = together(
            weight(),
            in_turn(attend, exchange, project),
            in_turn(lambda _: held(cotangent, 1), lambda later: pair_chain(gather_chain(later))),
        )
        return *results, dy.reshape(seq_len, width)

    def pair_chain(chain):
        return None, (yield from chain)

    attended_tok, out_full, middle, normed_mid, kept, dy = stage(
        sure, attention_stage, own, cotangent[0], normed_in, attn_full, out_part, cosine, sine, gain_mid
    )

    def hidden_stage(normed_mid, mlp_full, dy, attended_tok):
        def products():
            mlp_pre, hidden = yield hidden_units(normed_mid, mlp_full)
            down_grad = yield dot(hidden, dy, ((0,), (0,))).astype(low)
            return mlp_pre, hidden, down_grad

        results, attended_all = together(products(), gather_chain(attended_tok))
        return attended_all.reshape(seq_len, -1), *results

    attended_all, mlp_pre, hidden, down_grad = stage(
        sure, hidden_stage, normed_mid, mlp_full, dy, attended_tok
    )
    down_sum = z_scatter(down_grad)
    grad_mlp = hidden_back(after(dy, down_grad), down_full, mlp_pre)

    def middle_stage(grad_mlp, mlp_full, normed_mid, middle, dy_own, gain_mid, out_full):
        inverse_mid = lax.rsqrt(jnp.mean(middle * middle, axis=-1, keepdims=True) + EPS)
        unit_mid = middle * inverse_mid
        grad_normed_mid, results = together(
            by_halves(lambda at: dot(grad_mlp[at], mlp_full, ((1,), (1,)))),
            work(None, None, lambda: row_products((normed_mid, grad_mlp))),
        )
        grad_middle = norm_back(grad_normed_mid * gain_mid, unit_mid, inverse_mid)
        grad_middle = grad_middle + dy_own.astype(wide)
        grad_proj = grad_middle.astype(low)
        grad_attended = dot(grad_proj, out_full, ((1,), (1,))).astype(low)
        grad_even, grad_odd = split_columns((grad_attended, grad_proj), place_arg, groups)
        return grad_middle, grad_even, grad_odd, results[-1]

    grad_middle, grad_even, grad_odd, mlp_grad = stage(
        sure, middle_stage, grad_mlp, mlp_full, normed_mid, middle, cotangent[0], gain_mid, out_full
    )
    mlp_sum = z_scatter(mlp_grad)

    def back_stage(
        grad_even, grad_odd, attended_all, normed_in, cosine, sine, kept, down_sum, own, attn_full,
        gain_in, grad_middle, hidden, down_full, middle,
    ):
        wide_out, rotated, tops, sums = kept

        def back(pairs):
            grad_qkv, grad_proj_cols = yield attention_back(
                pairs, rotated, wide_out, tops, sums, cosine, sine, place_arg
            )
            grad_qkv = grad_qkv.reshape(seq_len, -1)
            terms = yield row_products(
                (normed_in, grad_qkv), (attended_all, grad_proj_cols.reshape(seq_len, out_cols))
            )
            grad_normed_in = yield from by_halves(
                lambda at: dot(grad_qkv[at], attn_full, ((1,), (1,)))
            )
            return grad_normed_in, terms

        def down_terms():
            later = yield from held(hidden, 1)

            def product(at):
                return jnp.dot(later[at], down_full, preferred_element_type=wide)

            odd, even = yield [half_of(product, at) for at in halves]
            return (yield from scatter_chain(lambda: odd, lambda: even))

        (grad_normed_in, attn_terms), down_halves, down_term = together(
            in_turn(lambda _: exchange_chain(grad_even, grad_odd), back),
            in_turn(lambda _: held(down_sum, 2), halves_chain),
            down_terms(),
        )
        stream_own = own.astype(wide)
        inverse_in = lax.rsqrt(jnp.mean(stream_own * stream_own, axis=-1, keepdims=True) + EPS)
        unit_in = stream_own * inverse_in
        grad_stream = norm_back(grad_normed_in * gain_in, unit_in, inverse_in) + grad_middle
        return grad_stream, attn_terms, (middle + down_term).astype(low), *down_halves

    grad_stream, attn_terms, layer_out, down_even, down_odd = stage(
        sure, back_stage, grad_even, grad_odd, attended_all, normed_in, cosine, sine, kept,
        after(down_sum, grad_even), own, attn_full, gain_in, grad_middle, hidden, down_full, middle,
    )

    attn_sum = z_scatter(attn_terms)

    def output_stage(down_even, down_odd, mlp_sum):
        (grad_down,), mine = together(
            work(lambda: put_rows(down_even, down_odd, place_arg)), near_chain(mlp_sum)
        )
        return grad_down, mine

    grad_down, mine = stage(sure, output_stage, down_even, down_odd, after(mlp_sum, attn_terms))

    def last_stage(mine, mlp_sum, mlp_own, attn_sum, attn_own):
        def columns_put():
            halves_all, filled = (mine, swap(mine, 1)), ()
            for part in range(4):
                filled = put_columns(*halves_all, place_arg, shards, part, 4, filled)
                if part:
                    filled = yield filled
            return filled

        def sums_chain():
            pairs = ((attn_sum[:, :-out_cols], attn_own[:, :-out_cols]), (mlp_sum, mlp_own))
            sums = [jnp.sum(a.astype(wide) * b.astype(wide), axis=1) for a, b in pairs]
            sums, mask = jnp.stack(sums), 1
            while mask < groups:
                sums = sums + (yield swap(sums, mask))
                mask *= 2
            return sums

        puts, attn_halves, sums = together(columns_put(), halves_chain(attn_sum), sums_chain())
        return *puts, sums, *put_attention(*attn_halves, place_arg, q_cols, out_cols)

    grad_gate, grad_up, row_sums, grad_query, grad_key, grad_value, grad_out = stage(
        sure, last_stage, mine, mlp_sum, mlp_own, after(attn_sum, grad_down), attn_own
    )
    return (
        layer_out[None],
        grad_stream[None],
        grad_query,
        grad_key,
        grad_value,
        grad_out,
        row_sums[0] / gain_attn.astype(wide),
        grad_gate,
        grad_up,
        grad_down,
        row_sums[1] / gain_mlp.astype(wide),
    )


def solution(mesh):
    placed = (
        P("fsdp", "seq", None),
        P("fsdp", "seq"),
        P("fsdp", None),
        P("fsdp", None),
        P("fsdp", None),
        P("fsdp", None),
        P("fsdp"),
        P("fsdp", None),
        P("fsdp", None),
        P("fsdp", None),
        P("fsdp"),
        P("fsdp", "seq", None),
    )
    return jax.shard_map(
        on_device,
        mesh=mesh,
        in_specs=placed,
        out_specs=(
            P("fsdp", "seq", None),
            P("fsdp", "seq", None),
            P("fsdp", None),
            P("fsdp", None),
            P("fsdp", None),
            P("fsdp", None),
            P("fsdp"),
            P("fsdp", None),
            P("fsdp", None),
            P("fsdp", None),
            P("fsdp"),
        ),
        check_vma=False,
    )
```

```python
import math

import jax
import jax.numpy as jnp
from jax import lax
from jax.experimental import pallas as pl
from jax.experimental.pallas import tpu as pltpu
from jax.sharding import PartitionSpec as P

HEADS = 32
KV_HEADS = 4
HEAD_DIM = 64


EPS = 1e-05
ROPE_BASE = 10000.0


def rope_tables(positions, head_size):
    half_dim = head_size // 2
    lane = jnp.arange(128)
    freqs = jnp.exp(
        (lane % half_dim).astype(jnp.float32) * (-2.0 * math.log(ROPE_BASE) / head_size)
    )
    angles = positions.astype(jnp.float32)[..., None] * freqs
    sign = jnp.where(lane % head_size < half_dim, -1.0, 1.0)
    return jnp.cos(angles), jnp.sin(angles) * sign


def norm_back(grad_normed, normed, inverse):
    return inverse * (grad_normed - normed * jnp.mean(grad_normed * normed, axis=-1, keepdims=True))


def dot(left, right, dims):
    return lax.dot_general(left, right, ((dims[0], dims[1]), ((), ())), preferred_element_type=jnp.float32)


def swap(value, mask):
    return lax.ppermute(value, "seq", [(i, i ^ mask) for i in range(lax.axis_size("seq"))])


def place_pieces(pieces, places, shape):
    cols = shape[2]
    tile = 512 if cols % 512 == 0 else cols

    def kernel(*refs):
        for piece, (slot, row), ref in zip(pieces, places, refs):
            refs[-1][slot, row : row + piece.shape[0]] = ref[...]

    return pl.pallas_call(
        kernel,
        grid=(cols // tile,),
        out_shape=jax.ShapeDtypeStruct(shape, pieces[0].dtype),
        in_specs=[pl.BlockSpec((piece.shape[0], tile), lambda i: (0, i)) for piece in pieces],
        out_specs=pl.BlockSpec(shape[:2] + (tile,), lambda i: (0, 0, i)),
        compiler_params=pltpu.CompilerParams(vmem_limit_bytes=48 * 2**20),
        cost_estimate=pl.CostEstimate(flops=0, bytes_accessed=math.prod(shape) * 4, transcendentals=0),
    )(*pieces)


def after(value, *earlier):
    return lax.optimization_barrier((value, *earlier))[0]


def together(*chains):
    results, values, live = [None] * len(chains), [None] * len(chains), list(range(len(chains)))
    while live:
        sent = {}
        for i in live:
            try:
                sent[i] = chains[i].send(values[i])
            except StopIteration as stop:
                results[i] = stop.value
        live = list(sent)
        for i, value in lax.optimization_barrier(sent).items():
            values[i] = value
    return results


def work(*parts):
    results = []
    for part in parts:
        results.append((yield () if part is None else part()))
    return results


def held(value, steps):
    for _ in range(steps):
        value = yield value
    return value


def in_turn(*makers):
    result = None
    for maker in makers:
        result = yield from maker(result)
    return result


def near_chain(part):
    n = lax.axis_size("seq")
    if n == 8 and part.shape[0] % 16 == 0:
        half = part.shape[0] // 32 * 16
        by_x, by_y = yield swap(part, 2), swap(part, 4)
        far = yield swap(by_x[:half], 4), swap(by_y[half:], 2)
        places = ((0, 0), (1, 0), (2, 0), (3, 0), (3, half))
        return place_pieces((part, by_x, by_y, *far), places, (4,) + part.shape)
    mine, mask = part[None], 2
    while mask < n:
        mine = jnp.concatenate([mine, (yield swap(mine, mask))])
        mask *= 2
    return mine


def core_chain(mine):
    return (yield mine, swap(mine, 1))


def halves_chain(part):
    return in_turn(lambda _: near_chain(part), core_chain)


def pieces_chain(part):
    if lax.axis_size("seq") == 8 and part.shape[0] % 32 == 0:
        half = part.shape[0] // 2
        by_x, by_y = yield swap(part, 2), swap(part, 4)
        near = part, by_x, by_y
        far, other = yield (
            (swap(by_x[:half], 4), swap(by_y[half:], 2)),
            tuple(swap(piece, 1) for piece in near),
        )
        other_far = yield tuple(swap(piece, 1) for piece in far)
        places = ((0, 0), (1, 0), (2, 0), (3, 0), (3, half))
        return (*near, *far), (*other, *other_far), places
    mine, other = yield from halves_chain(part)
    return tuple(mine), tuple(other), tuple((k, 0) for k in range(mine.shape[0]))


def gather_chain(part):
    mine, other = yield from halves_chain(part)
    if part.shape[0] % 16:
        return jnp.concatenate([mine, other])
    half, rows, cols = mine.shape
    tile = 512 if cols % 512 == 0 else cols

    def kernel(mine_ref, other_ref, out_ref):
        out_ref[:half] = mine_ref[...]
        out_ref[half:] = other_ref[...]

    return pl.pallas_call(
        kernel,
        grid=(cols // tile,),
        out_shape=jax.ShapeDtypeStruct((2 * half, rows, cols), part.dtype),
        in_specs=[pl.BlockSpec((half, rows, tile), lambda i: (0, 0, i))] * 2,
        out_specs=pl.BlockSpec((2 * half, rows, tile), lambda i: (0, 0, i)),
        cost_estimate=pl.CostEstimate(flops=0, bytes_accessed=mine.size * 8, transcendentals=0),
    )(mine, other)


def ring_chain(value):
    n = lax.axis_size("fsdp")
    moving = value
    for _ in range(n - 1):
        moving = yield lax.ppermute(moving, "fsdp", [(i, (i + 1) % n) for i in range(n)])
        value = value + moving
    return value


def scatter_chain(make_odd, make_even):
    n = lax.axis_size("seq")

    def add(own, other):
        return own.astype(jnp.float32) + other.astype(jnp.float32)

    low = jnp.bfloat16
    odd = make_odd()
    even, other = yield make_even(), swap(odd, 1)
    mine = add(even, other)
    if n == 8:
        half = even.shape[1] // 2
        far = mine[3].astype(low)
        from_x, from_y = yield swap(far[:half], 2), swap(far[half:], 4)
        to_y = jnp.concatenate([add(mine[2][:half], from_x), mine[2][half:]]).astype(low)
        to_x = jnp.concatenate([mine[1][:half], add(mine[1][half:], from_y)]).astype(low)
        by_x, by_y = yield swap(to_x, 2), swap(to_y, 4)
        return add(mine[0], by_x) + by_y.astype(jnp.float32)
    mask = n // 2
    while mask > 1:
        count = mine.shape[0] // 2
        mine = add(mine[:count], (yield swap(mine[count:].astype(low), mask)))
        mask //= 2
    return mine[0]


def ordered(place, even, odd, body):
    core = place & 1
    pl.when(core == 0)(lambda: body(even, odd))
    pl.when(core == 1)(lambda: body(odd, even))


def put_columns(even, odd, place, pieces, part, parts, earlier=()):
    half, rows, cols = even.shape
    n, w = 2 * half, cols // (2 * pieces)
    tile = 64
    steps = rows // parts // tile

    def kernel(place_ref, even_ref, odd_ref, *refs):
        chip = place_ref[0] // 2

        def body(first, other):
            blocks = [(other if t % 2 else first)[(t // 2) ^ chip] for t in range(n)]
            for target, start in zip(refs[-2:], (0, cols // 2)):
                for f in range(pieces):
                    at = start + f * w
                    row = jnp.concatenate([block[:, at : at + w] for block in blocks], axis=1)
                    target[:, f * n * w : (f + 1) * n * w] = row.astype(jnp.float32)

        ordered(place_ref[0], even_ref, odd_ref, body)

    spec = pl.BlockSpec((half, tile, cols), lambda i: (0, i + part * steps, 0))
    whole = jax.ShapeDtypeStruct((rows, pieces * n * w), jnp.float32)
    return pl.pallas_call(
        kernel,
        grid=(steps,),
        out_shape=(whole, whole),
        in_specs=[pl.BlockSpec(memory_space=pltpu.SMEM), spec, spec]
        + [pl.BlockSpec(memory_space=pl.ANY)] * len(earlier),
        out_specs=[pl.BlockSpec((tile, pieces * n * w), lambda i: (i + part * steps, 0))] * 2,
        input_output_aliases={3 + i: i for i in range(len(earlier))},
        compiler_params=pltpu.CompilerParams(vmem_limit_bytes=48 * 2**20),
        cost_estimate=pl.CostEstimate(flops=0, bytes_accessed=even.size * 6, transcendentals=0),
    )(place, even, odd, *earlier)


def put_rows(even, odd, place):
    half, rows, cols = even.shape
    tile = 256

    def kernel(place_ref, even_ref, odd_ref, out_ref):
        chip = place_ref[0] // 2

        def body(first, second):
            for t in range(2 * half):
                block = (second if t % 2 else first)[(t // 2) ^ chip]
                out_ref[t * rows : (t + 1) * rows, :] = block.astype(jnp.float32)

        ordered(place_ref[0], even_ref, odd_ref, body)

    spec = pl.BlockSpec((half, rows, tile), lambda i: (0, 0, i))
    return pl.pallas_call(
        kernel,
        grid=(cols // tile,),
        out_shape=jax.ShapeDtypeStruct((2 * half * rows, cols), jnp.float32),
        in_specs=[pl.BlockSpec(memory_space=pltpu.SMEM), spec, spec],
        out_specs=pl.BlockSpec((2 * half * rows, tile), lambda i: (0, i)),
        compiler_params=pltpu.CompilerParams(vmem_limit_bytes=48 * 2**20),
        cost_estimate=pl.CostEstimate(flops=0, bytes_accessed=even.size * 12, transcendentals=0),
    )(place, even, odd)


def put_attention(even, odd, places, place, q_cols, out_cols):
    half = max(slot for slot, _ in places) + 1
    rows, cols = even[0].shape
    n, tile = 2 * half, 64
    copies = n // KV_HEADS
    sizes = (n * q_cols, KV_HEADS * HEAD_DIM, KV_HEADS * HEAD_DIM, n * out_cols)

    def kernel(place_ref, *refs):
        count, step = len(places), pl.program_id(0)
        query_ref, key_ref, value_ref, out_ref, even_ref, odd_ref = refs[2 * count :]
        for held_ref, piece_refs in ((even_ref, refs[:count]), (odd_ref, refs[count : 2 * count])):
            for (slot, row), piece, ref in zip(places, even, piece_refs):
                first, steps = row // tile, piece.shape[0] // tile

                @pl.when((step >= first) & (step < first + steps))
                def _(held_ref=held_ref, slot=slot, ref=ref):
                    held_ref[slot] = ref[...]

        chip = place_ref[0] // 2

        def body(first, second):
            blocks = [
                (second if t % 2 else first)[(t // 2) ^ chip].astype(jnp.float32) for t in range(n)
            ]
            for t, block in enumerate(blocks):
                query_ref[:, t * q_cols : (t + 1) * q_cols] = block[:, :q_cols]
                out_ref[:, t * out_cols : (t + 1) * out_cols] = block[:, cols - out_cols :]
            sums = [
                sum(block[:, q_cols : q_cols + 2 * HEAD_DIM] for block in blocks[h * copies : (h + 1) * copies])
                for h in range(KV_HEADS)
            ]
            key_ref[...] = jnp.concatenate([part[:, :HEAD_DIM] for part in sums], axis=1)
            value_ref[...] = jnp.concatenate([part[:, HEAD_DIM:] for part in sums], axis=1)

        ordered(place_ref[0], even_ref, odd_ref, body)

    def spec(row, piece):
        first, last = row // tile, piece.shape[0] // tile - 1
        return pl.BlockSpec((tile, cols), lambda i: (jnp.clip(i - first, 0, last), 0))

    specs = [spec(row, piece) for (_, row), piece in zip(places, even)]
    return pl.pallas_call(
        kernel,
        grid=(rows // tile,),
        out_shape=[jax.ShapeDtypeStruct((rows, size), jnp.float32) for size in sizes],
        in_specs=[pl.BlockSpec(memory_space=pltpu.SMEM)] + specs * 2,
        out_specs=[pl.BlockSpec((tile, size), lambda i: (i, 0)) for size in sizes],
        scratch_shapes=[pltpu.VMEM((half, tile, cols), even[0].dtype)] * 2,
        compiler_params=pltpu.CompilerParams(vmem_limit_bytes=48 * 2**20),
        cost_estimate=pl.CostEstimate(flops=0, bytes_accessed=half * rows * cols * 12, transcendentals=0),
    )(place, *even, *odd)


def slot_of(mask, n):
    return (mask >> 1) + (mask & 1) * (n // 2)


def split_columns(parts, place, n):
    rows = parts[0].shape[0]
    sizes = [part.shape[1] // n for part in parts]
    half, cols = n // 2, sum(sizes)

    def kernel(place_ref, *refs):
        for core, ref in enumerate(refs[-2:]):
            for k in range(half):
                block, at = place_ref[0] ^ (2 * k + core), 0
                for size, part_ref in zip(sizes, refs):
                    start = pl.multiple_of(block * size, size)
                    ref[k, :, at : at + size] = part_ref[:, pl.ds(start, size)]
                    at += size

    vmem = pl.BlockSpec(memory_space=pltpu.VMEM)
    return pl.pallas_call(
        kernel,
        out_shape=[jax.ShapeDtypeStruct((half, rows, cols), parts[0].dtype)] * 2,
        in_specs=[pl.BlockSpec(memory_space=pltpu.SMEM)] + [vmem] * len(parts),
        out_specs=[vmem] * 2,
    )(place, *parts)


def exchange_chain(even, odd):
    half, rows, cols = even.shape
    other = yield swap(odd, 1)

    def kernel(even_ref, other_ref, *refs):
        for k, ref in enumerate(refs):
            ref[0] = even_ref[k]
            ref[1] = other_ref[k]

    vmem = pl.BlockSpec(memory_space=pltpu.VMEM)
    pairs = pl.pallas_call(
        kernel,
        out_shape=[jax.ShapeDtypeStruct((2, rows, cols), even.dtype)] * half,
        in_specs=[vmem] * 2,
        out_specs=[vmem] * half,
    )(even, other)
    return (yield [pair if k == 0 else swap(pair, 2 * k) for k, pair in enumerate(pairs)])


def join_columns(pairs, place):
    n, (_, rows, cols) = 2 * len(pairs), pairs[0].shape

    def kernel(place_ref, *refs):
        for k, ref in enumerate(refs[:-1]):
            for core in range(2):
                start = pl.multiple_of((place_ref[0] ^ (2 * k + core)) * cols, cols)
                refs[-1][:, pl.ds(start, cols)] = ref[core]

    vmem = pl.BlockSpec(memory_space=pltpu.VMEM)
    return pl.pallas_call(
        kernel,
        out_shape=jax.ShapeDtypeStruct((rows, n * cols), pairs[0].dtype),
        in_specs=[pl.BlockSpec(memory_space=pltpu.SMEM)] + [vmem] * len(pairs),
        out_specs=vmem,
    )(place, *pairs)


def join_weight(even, odd, place):
    half, rows, cols = even.shape
    n, tile = 2 * half, 512

    def kernel(place_ref, even_ref, odd_ref, out_ref):
        for ref, core in ((even_ref, 0), (odd_ref, 1)):
            for k in range(half):
                start = pl.multiple_of((place_ref[0] ^ (2 * k + core)) * cols, cols)
                out_ref[:, pl.ds(start, cols)] = ref[k]

    spec = pl.BlockSpec((half, tile, cols), lambda i: (0, i, 0))
    return pl.pallas_call(
        kernel,
        grid=(rows // tile,),
        out_shape=jax.ShapeDtypeStruct((rows, n * cols), even.dtype),
        in_specs=[pl.BlockSpec(memory_space=pltpu.SMEM), spec, spec],
        out_specs=pl.BlockSpec((tile, n * cols), lambda i: (i, 0)),
        compiler_params=pltpu.CompilerParams(vmem_limit_bytes=48 * 2**20),
        cost_estimate=pl.CostEstimate(flops=0, bytes_accessed=even.size * 8, transcendentals=0),
    )(place, even, odd)


def lanes(shape):
    return lax.broadcasted_iota(jnp.int32, shape, 1)


def halves_swapped(value):
    first = lanes(value.shape) % HEAD_DIM < HEAD_DIM // 2
    size = value.shape[1]
    left, right = pltpu.roll(value, size - HEAD_DIM // 2, 1), pltpu.roll(value, HEAD_DIM // 2, 1)
    return jnp.where(first, left, right)


def turned(value, cosine, sine):
    parts = [
        value[:, i : i + 128] * cosine + halves_swapped(value[:, i : i + 128]) * sine
        for i in range(0, value.shape[1], 128)
    ]
    return jnp.concatenate(parts, axis=1)


def key_copies(key_value):
    first = lanes(key_value.shape) < HEAD_DIM
    turned_over = pltpu.roll(key_value, HEAD_DIM, 1)
    keys = jnp.where(first, key_value, turned_over)
    values = jnp.where(first, turned_over, key_value)
    return keys, values, first


def only(value, head):
    first = lanes(value.shape) < HEAD_DIM
    return jnp.where(first if head == 0 else ~first, value, jnp.zeros_like(value))


def matmul(left, right, dims):
    return lax.dot_general(left, right, (dims, ((), ())), preferred_element_type=jnp.float32)


ROWS_OF = ((1,), (1,))
PLAIN = ((1,), (0,))
COLUMNS_OF = ((0,), (0,))
MASKED = -1e30


def attention(qkv, cosine, sine, place, heads_dev):
    n, rows, cols = qkv.shape
    length, q_cols = n * rows, heads_dev * HEAD_DIM
    block = 256
    low, wide = jnp.bfloat16, jnp.float32

    def kernel(place_ref, qkv_ref, cos_ref, sin_ref, *refs):
        even_ref, odd_ref, out_ref, rot_ref, top_ref, sum_ref = refs
        for t in range(n):
            slot = slot_of(place_ref[0] ^ t, n)
            value = qkv_ref[slot]
            moved = turned(value[:, : q_cols + 128], cos_ref[slot], sin_ref[slot])
            key_value = jnp.where(
                lanes((rows, 128)) < HEAD_DIM, moved[:, q_cols:], value[:, q_cols:]
            )
            at = slice(t * rows, (t + 1) * rows)
            rot_ref[at, :q_cols] = moved[:, :q_cols].astype(low)
            rot_ref[at, q_cols:] = key_value.astype(low)
        for i in range(length // block):
            span = (i + 1) * block
            key_value = rot_ref[:span, q_cols:]
            keys, values, _ = key_copies(key_value)
            held = [only(values, 0), only(values, 1)]
            shape = (block, span)
            seen = lax.broadcasted_iota(jnp.int32, shape, 1) <= i * block + (
                lax.broadcasted_iota(jnp.int32, shape, 0)
            )
            at = slice(i * block, (i + 1) * block)
            for pair in range(q_cols // 128):
                query = rot_ref[at, pair * 128 : (pair + 1) * 128] * jnp.asarray(0.125, low)
                total = None
                for head in range(2):
                    scores = matmul(only(query, head), keys, ROWS_OF)
                    scores = jnp.where(seen, scores, MASKED)
                    top = jnp.max(scores, axis=1, keepdims=True)
                    unnormed = jnp.exp(scores - top)
                    row_sum = jnp.sum(unnormed, axis=1, keepdims=True)
                    part = matmul(unnormed.astype(low), held[head], PLAIN) / row_sum
                    top_ref[2 * pair + head, at, :] = top
                    sum_ref[2 * pair + head, at, :] = row_sum
                    total = part if total is None else total + part
                out_ref[at, pair * 128 : (pair + 1) * 128] = total
        for core, ref in ((0, even_ref), (1, odd_ref)):
            for k in range(n // 2):
                start = pl.multiple_of((place_ref[0] ^ (2 * k + core)) * rows, rows)
                ref[k] = out_ref[pl.ds(start, rows), :].astype(low)

    vmem = pl.BlockSpec(memory_space=pltpu.VMEM)
    results = pl.pallas_call(
        kernel,
        out_shape=[jax.ShapeDtypeStruct((n // 2, rows, q_cols), low)] * 2
        + [
            jax.ShapeDtypeStruct((length, q_cols), wide),
            jax.ShapeDtypeStruct((length, q_cols + 2 * HEAD_DIM), low),
            jax.ShapeDtypeStruct((heads_dev, length, 1), wide),
            jax.ShapeDtypeStruct((heads_dev, length, 1), wide),
        ],
        in_specs=[pl.BlockSpec(memory_space=pltpu.SMEM)] + [vmem] * 3,
        out_specs=[vmem] * 6,
        compiler_params=pltpu.CompilerParams(vmem_limit_bytes=48 * 2**20),
        cost_estimate=pl.CostEstimate(
            flops=2 * length * length * 128 * heads_dev,
            bytes_accessed=qkv.size * 8,
            transcendentals=length * length * heads_dev // 2,
        ),
    )(place, qkv, cosine, sine)
    return results[:2], *results[2:]


def attention_back(grads, rotated, out, tops, sums, cosine, sine, place):
    n, (_, rows, all_cols) = 2 * len(grads), grads[0].shape
    length, cols = rotated.shape
    q_cols = cols - 2 * HEAD_DIM
    heads_dev = q_cols // HEAD_DIM
    block = 256
    low, wide = jnp.bfloat16, jnp.float32

    def kernel(place_ref, rot_ref, out_ref, top_ref, sum_ref, cos_ref, sin_ref, *refs):
        grad_refs = refs[: n // 2]
        result_ref, others_ref, grad_ref, dq_ref, dk_ref, dv_ref = refs[n // 2 :]
        for k, ref in enumerate(grad_refs):
            for core in range(2):
                start = pl.multiple_of((place_ref[0] ^ (2 * k + core)) * rows, rows)
                grad_ref[pl.ds(start, rows), :] = ref[core, :, :q_cols]
                others_ref[core * (n // 2) + k] = ref[core, :, q_cols:]
        dk_ref[...] = jnp.zeros_like(dk_ref)
        dv_ref[...] = jnp.zeros_like(dv_ref)
        for i in range(length // block):
            span = (i + 1) * block
            keys, values, _ = key_copies(rot_ref[:span, q_cols:])
            held = [only(keys, 0), only(keys, 1)]
            shape = (block, span)
            seen = lax.broadcasted_iota(jnp.int32, shape, 1) <= i * block + (
                lax.broadcasted_iota(jnp.int32, shape, 0)
            )
            at = slice(i * block, (i + 1) * block)
            dk = dv = None
            for pair in range(q_cols // 128):
                pair_at = slice(pair * 128, (pair + 1) * 128)
                query = rot_ref[at, pair_at] * jnp.asarray(0.125, low)
                grad = grad_ref[at, pair_at].astype(wide)
                product = grad * out_ref[at, pair_at]
                dq = None
                for head in range(2):
                    row_sum = sum_ref[2 * pair + head, at, :]
                    own_query = only(query, head)
                    own_grad = only((grad / row_sum).astype(low), head)
                    scores = jnp.where(seen, matmul(own_query, keys, ROWS_OF), MASKED)
                    unnormed = jnp.exp(scores - top_ref[2 * pair + head, at, :])
                    shift = jnp.sum(only(product, head), axis=1, keepdims=True) / row_sum
                    grad_probs = matmul(own_grad, values, ROWS_OF)
                    grad_scores = (unnormed * (grad_probs - shift)).astype(low)
                    dq_part = matmul(grad_scores, held[head], PLAIN)
                    dk_part = matmul(grad_scores, own_query, COLUMNS_OF)
                    dv_part = matmul(unnormed.astype(low), own_grad, COLUMNS_OF)
                    dq = dq_part if dq is None else dq + dq_part
                    dk = dk_part if dk is None else dk + dk_part
                    dv = dv_part if dv is None else dv + dv_part
                dq_ref[at, pair_at] = dq * 0.125
            dk_ref[:span, :] += dk
            dv_ref[:span, :] += dv
        for t in range(n):
            slot = slot_of(place_ref[0] ^ t, n)
            at = slice(t * rows, (t + 1) * rows)
            dk, dv = dk_ref[at, :], dv_ref[at, :]
            first = lanes(dk.shape) < HEAD_DIM
            dk, dv = dk + pltpu.roll(dk, HEAD_DIM, 1), dv + pltpu.roll(dv, HEAD_DIM, 1)
            moved = turned(
                jnp.concatenate([dq_ref[at, :], dk], axis=1), cos_ref[slot], -sin_ref[slot]
            )
            result_ref[slot, :, :q_cols] = moved[:, :q_cols].astype(low)
            result_ref[slot, :, q_cols:] = jnp.where(first, moved[:, q_cols:], dv).astype(low)

    vmem = pl.BlockSpec(memory_space=pltpu.VMEM)
    return pl.pallas_call(
        kernel,
        out_shape=[
            jax.ShapeDtypeStruct((n, rows, cols), low),
            jax.ShapeDtypeStruct((n, rows, all_cols - q_cols), low),
        ],
        in_specs=[pl.BlockSpec(memory_space=pltpu.SMEM)] + [vmem] * (6 + n // 2),
        out_specs=[vmem] * 2,
        scratch_shapes=[
            pltpu.VMEM((length, q_cols), low),
            pltpu.VMEM((length, q_cols), wide),
            pltpu.VMEM((length, 128), wide),
            pltpu.VMEM((length, 128), wide),
        ],
        compiler_params=pltpu.CompilerParams(vmem_limit_bytes=48 * 2**20),
        cost_estimate=pl.CostEstimate(
            flops=5 * length * length * 128 * heads_dev,
            bytes_accessed=rotated.size * 8,
            transcendentals=length * length * heads_dev // 2,
        ),
    )(place, rotated, out, tops, sums, cosine, sine, *grads)


def silu_parts(gate):
    sigmoid_gate = 1.0 / (1.0 + jnp.exp(-gate))
    return sigmoid_gate, gate * sigmoid_gate


def hidden_units(normed, weights):
    rows, width = normed.shape
    cols = weights.shape[1]
    tile, ff_dev = 256, cols // 2

    def kernel(normed_ref, weights_ref, pre_ref, hidden_ref):
        pre = matmul(normed_ref[...], weights_ref[...], PLAIN)
        pre_ref[...] = pre
        hidden_ref[...] = (silu_parts(pre[:, :ff_dev])[1] * pre[:, ff_dev:]).astype(jnp.bfloat16)

    return pl.pallas_call(
        kernel,
        grid=(rows // tile,),
        out_shape=[
            jax.ShapeDtypeStruct((rows, cols), jnp.float32),
            jax.ShapeDtypeStruct((rows, ff_dev), jnp.bfloat16),
        ],
        in_specs=[
            pl.BlockSpec((tile, width), lambda i: (i, 0)),
            pl.BlockSpec((width, cols), lambda i: (0, 0)),
        ],
        out_specs=[
            pl.BlockSpec((tile, cols), lambda i: (i, 0)),
            pl.BlockSpec((tile, ff_dev), lambda i: (i, 0)),
        ],
        compiler_params=pltpu.CompilerParams(vmem_limit_bytes=48 * 2**20),
        cost_estimate=pl.CostEstimate(
            flops=2 * rows * width * cols, bytes_accessed=rows * cols * 8, transcendentals=rows * ff_dev
        ),
    )(normed, weights)


def hidden_back(dy, down, pre):
    rows, width = dy.shape
    ff_dev = down.shape[0]
    tile = 256

    def kernel(dy_ref, down_ref, pre_ref, out_ref):
        grad_hidden = matmul(dy_ref[...], down_ref[...], ROWS_OF)
        gate, upper = pre_ref[:, :ff_dev], pre_ref[:, ff_dev:]
        sigmoid_gate, activated = silu_parts(gate)
        grad_gate = grad_hidden * upper * (sigmoid_gate * (1.0 + gate * (1.0 - sigmoid_gate)))
        both = jnp.concatenate([grad_gate, grad_hidden * activated], axis=1)
        out_ref[...] = both.astype(jnp.bfloat16)

    return pl.pallas_call(
        kernel,
        grid=(rows // tile,),
        out_shape=jax.ShapeDtypeStruct((rows, 2 * ff_dev), jnp.bfloat16),
        in_specs=[
            pl.BlockSpec((tile, width), lambda i: (i, 0)),
            pl.BlockSpec((ff_dev, width), lambda i: (0, 0)),
            pl.BlockSpec((tile, 2 * ff_dev), lambda i: (i, 0)),
        ],
        out_specs=pl.BlockSpec((tile, 2 * ff_dev), lambda i: (i, 0)),
        compiler_params=pltpu.CompilerParams(vmem_limit_bytes=48 * 2**20),
        cost_estimate=pl.CostEstimate(
            flops=2 * rows * width * ff_dev, bytes_accessed=rows * ff_dev * 16, transcendentals=rows * ff_dev
        ),
    )(dy, down, pre)


def row_products(*pairs):
    rows, width = pairs[0][0].shape
    sizes = [right.shape[1] for _, right in pairs]
    tile = 512

    def kernel(*refs):
        at = 0
        for i, size in enumerate(sizes):
            product = matmul(refs[2 * i][...], refs[2 * i + 1][...], COLUMNS_OF)
            refs[-1][:, at : at + size] = product.astype(jnp.bfloat16)
            at += size

    return pl.pallas_call(
        kernel,
        grid=(width // tile,),
        out_shape=jax.ShapeDtypeStruct((width, sum(sizes)), jnp.bfloat16),
        in_specs=[
            spec
            for size in sizes
            for spec in (
                pl.BlockSpec((rows, tile), lambda i: (0, i)),
                pl.BlockSpec((rows, size), lambda i: (0, 0)),
            )
        ],
        out_specs=pl.BlockSpec((tile, sum(sizes)), lambda i: (i, 0)),
        compiler_params=pltpu.CompilerParams(vmem_limit_bytes=48 * 2**20),
        cost_estimate=pl.CostEstimate(
            flops=2 * rows * width * sum(sizes), bytes_accessed=rows * width * 4, transcendentals=0
        ),
    )(*[array for pair in pairs for array in pair])


def stage(sure, body, *args):
    shapes = jax.eval_shape(body, *args)

    def nothing(*_):
        return jax.tree.map(lambda leaf: jnp.zeros(leaf.shape, leaf.dtype), shapes)

    return lax.cond(sure, body, nothing, *args)


def own_columns(place, w_query, w_key, w_value, w_out, n):
    rows, q_cols, out_cols = w_query.shape[0], w_query.shape[1] // n, w_out.shape[1] // n
    cols = q_cols + 2 * HEAD_DIM + out_cols

    def kernel(place_ref, query_ref, key_ref, value_ref, out_ref, result_ref):
        result_ref[:, :q_cols] = query_ref[...]
        result_ref[:, cols - out_cols :] = out_ref[...]
        for head in range(KV_HEADS):
            at = slice(head * HEAD_DIM, (head + 1) * HEAD_DIM)

            @pl.when(place_ref[0] // (n // KV_HEADS) == head)
            def _(at=at):
                both = jnp.concatenate([key_ref[:, at], value_ref[:, at]], axis=1)
                result_ref[:, q_cols : q_cols + 2 * HEAD_DIM] = both

    tile = rows // 2
    return pl.pallas_call(
        kernel,
        grid_spec=pltpu.PrefetchScalarGridSpec(
            num_scalar_prefetch=1,
            grid=(2,),
            in_specs=[
                pl.BlockSpec((tile, q_cols), lambda i, place_ref: (i, place_ref[0])),
                pl.BlockSpec((tile, w_key.shape[1]), lambda i, place_ref: (i, 0)),
                pl.BlockSpec((tile, w_value.shape[1]), lambda i, place_ref: (i, 0)),
                pl.BlockSpec((tile, out_cols), lambda i, place_ref: (i, place_ref[0])),
            ],
            out_specs=pl.BlockSpec((tile, cols), lambda i, place_ref: (i, 0)),
        ),
        out_shape=jax.ShapeDtypeStruct((rows, cols), w_query.dtype),
        cost_estimate=pl.CostEstimate(flops=0, bytes_accessed=rows * cols * 6, transcendentals=0),
    )(place, w_query, w_key, w_value, w_out)


def columns_of(weight, place, groups, shards):
    width = weight.shape[1] // (groups * shards)
    return jnp.concatenate(
        [
            lax.dynamic_slice_in_dim(weight, (f * groups + place) * width, width, 1)
            for f in range(shards)
        ],
        axis=1,
    )


def on_device(
    tokens,
    positions,
    w_query,
    w_key,
    w_value,
    w_out,
    gain_attn,
    w_gate,
    w_up,
    w_down,
    gain_mlp,
    cotangent,
):
    low, wide = jnp.bfloat16, jnp.float32
    groups = lax.axis_size("seq")
    shards = lax.axis_size("fsdp")
    place = lax.axis_index("seq")
    shard = lax.axis_index("fsdp")
    tok_rows, width = tokens.shape[1:]
    shard_rows = w_query.shape[0]
    heads_dev = HEADS // groups
    seq_len = tok_rows * groups
    q_cols = heads_dev * HEAD_DIM
    out_cols = width // groups

    def z_gather(part):
        return lax.all_gather(part, "fsdp", axis=0, tiled=True)

    def z_scatter(part):
        return lax.psum_scatter(part, "fsdp", scatter_dimension=0, tiled=True)

    def columns(weight, start, count):
        return lax.dynamic_slice_in_dim(weight, start, count, 1)

    place_arg = place.reshape(1).astype(jnp.int32)
    attn_own = own_columns(place_arg, w_query, w_key, w_value, w_out, groups)
    attn_full = z_gather(attn_own)
    attn_full, out_part = attn_full[:, :-out_cols], attn_full[:, -out_cols:]
    mlp_own = jnp.concatenate(
        [columns_of(w_gate, place, groups, shards), columns_of(w_up, place, groups, shards)], axis=1
    )
    mlp_full = z_gather(mlp_own)
    down_rows = w_down.shape[0] // groups
    down_full = z_gather(lax.dynamic_slice_in_dim(w_down, place * down_rows, down_rows, 0))
    sure = positions[0, 0] >= 0
    own = tokens[0]
    gains_own = jnp.stack([gain_attn, gain_mlp]).astype(wide)

    halves = (slice(seq_len // 2, None), slice(0, seq_len // 2))

    def half_of(product, at):
        return product(at).astype(low).reshape(groups // 2, tok_rows, width)

    def by_halves(product):
        return scatter_chain(
            lambda: half_of(product, halves[0]), lambda: half_of(product, halves[1])
        )

    def inputs_stage(own, positions, gains_own):
        gains = lax.dynamic_update_slice(
            jnp.zeros((2, width), wide), gains_own, (0, shard * shard_rows)
        )
        gains, where, stream = together(
            ring_chain(gains), gather_chain(positions), gather_chain(own)
        )
        where, stream = where.reshape(seq_len), stream.reshape(seq_len, width).astype(wide)
        cosine, sine = rope_tables(where, HEAD_DIM)
        cosine, sine = cosine.reshape(groups, tok_rows, 128), sine.reshape(groups, tok_rows, 128)
        inverse_all = lax.rsqrt(jnp.mean(stream * stream, axis=-1, keepdims=True) + EPS)
        normed_in = (stream * inverse_all * gains[0]).astype(low)
        return gains, cosine, sine, normed_in

    gains, cosine, sine, normed_in = stage(sure, inputs_stage, own, positions, gains_own)
    gain_in, gain_mid = gains

    def attention_stage(own, cotangent, normed_in, attn_full, out_part, cosine, sine, gain_mid):
        def attend(_):
            qkv = jnp.dot(normed_in, attn_full, preferred_element_type=wide)
            return (
                yield attention(
                    qkv.reshape(groups, tok_rows, -1), cosine, sine, place_arg, heads_dev
                )
            )

        def exchange(attended):
            pairs = yield from exchange_chain(*attended[0])
            return join_columns(pairs, place_arg), attended[1:]

        def project(results):
            attended_tok, kept = results
            while not out_box:
                yield ()
            out_full = join_weight(*out_box[0], place_arg)
            middle = own.astype(wide) + jnp.dot(attended_tok, out_full, preferred_element_type=wide)
            inverse_mid = lax.rsqrt(jnp.mean(middle * middle, axis=-1, keepdims=True) + EPS)
            normed_mid = yield from gather_chain((middle * inverse_mid * gain_mid).astype(low))
            return attended_tok, out_full, middle, normed_mid.reshape(seq_len, width), kept

        out_box = []

        def weight():
            out_box.append((yield from halves_chain(out_part)))

        _, results, (_, dy) = together(
            weight(),
            in_turn(attend, exchange, project),
            in_turn(lambda _: held(cotangent, 1), lambda later: pair_chain(gather_chain(later))),
        )
        return *results, dy.reshape(seq_len, width)

    def pair_chain(chain):
        return None, (yield from chain)

    attended_tok, out_full, middle, normed_mid, kept, dy = stage(
        sure, attention_stage, own, cotangent[0], normed_in, attn_full, out_part, cosine, sine, gain_mid
    )

    def hidden_stage(normed_mid, mlp_full, dy, attended_tok):
        def products():
            mlp_pre, hidden = yield hidden_units(normed_mid, mlp_full)
            down_grad = yield dot(hidden, dy, ((0,), (0,))).astype(low)
            return mlp_pre, hidden, down_grad

        results, attended_all = together(products(), gather_chain(attended_tok))
        return attended_all.reshape(seq_len, -1), *results

    attended_all, mlp_pre, hidden, down_grad = stage(
        sure, hidden_stage, normed_mid, mlp_full, dy, attended_tok
    )
    down_sum = z_scatter(down_grad)
    grad_mlp = hidden_back(after(dy, down_grad), down_full, mlp_pre)

    def middle_stage(grad_mlp, mlp_full, normed_mid, middle, dy_own, gain_mid, out_full):
        inverse_mid = lax.rsqrt(jnp.mean(middle * middle, axis=-1, keepdims=True) + EPS)
        unit_mid = middle * inverse_mid
        grad_normed_mid, results = together(
            by_halves(lambda at: dot(grad_mlp[at], mlp_full, ((1,), (1,)))),
            work(None, None, lambda: row_products((normed_mid, grad_mlp))),
        )
        grad_middle = norm_back(grad_normed_mid * gain_mid, unit_mid, inverse_mid)
        grad_middle = grad_middle + dy_own.astype(wide)
        grad_proj = grad_middle.astype(low)
        grad_attended = dot(grad_proj, out_full, ((1,), (1,))).astype(low)
        grad_even, grad_odd = split_columns((grad_attended, grad_proj), place_arg, groups)
        return grad_middle, grad_even, grad_odd, results[-1]

    grad_middle, grad_even, grad_odd, mlp_grad = stage(
        sure, middle_stage, grad_mlp, mlp_full, normed_mid, middle, cotangent[0], gain_mid, out_full
    )
    mlp_sum = z_scatter(mlp_grad)

    def back_stage(
        grad_even, grad_odd, attended_all, normed_in, cosine, sine, kept, down_sum, own, attn_full,
        gain_in, grad_middle, hidden, down_full, middle,
    ):
        wide_out, rotated, tops, sums = kept

        def back(pairs):
            grad_qkv, grad_proj_cols = yield attention_back(
                pairs, rotated, wide_out, tops, sums, cosine, sine, place_arg
            )
            grad_qkv = grad_qkv.reshape(seq_len, -1)
            terms = yield row_products(
                (normed_in, grad_qkv), (attended_all, grad_proj_cols.reshape(seq_len, out_cols))
            )
            grad_normed_in = yield from by_halves(
                lambda at: dot(grad_qkv[at], attn_full, ((1,), (1,)))
            )
            return grad_normed_in, terms

        def down_terms():
            later = yield from held(hidden, 1)

            def product(at):
                return jnp.dot(later[at], down_full, preferred_element_type=wide)

            odd, even = yield [half_of(product, at) for at in halves]
            return (yield from scatter_chain(lambda: odd, lambda: even))

        (grad_normed_in, attn_terms), down_halves, down_term = together(
            in_turn(lambda _: exchange_chain(grad_even, grad_odd), back),
            in_turn(lambda _: held(down_sum, 2), halves_chain),
            down_terms(),
        )
        stream_own = own.astype(wide)
        inverse_in = lax.rsqrt(jnp.mean(stream_own * stream_own, axis=-1, keepdims=True) + EPS)
        unit_in = stream_own * inverse_in
        grad_stream = norm_back(grad_normed_in * gain_in, unit_in, inverse_in) + grad_middle
        return grad_stream, attn_terms, (middle + down_term).astype(low), *down_halves

    grad_stream, attn_terms, layer_out, down_even, down_odd = stage(
        sure, back_stage, grad_even, grad_odd, attended_all, normed_in, cosine, sine, kept,
        after(down_sum, grad_even), own, attn_full, gain_in, grad_middle, hidden, down_full, middle,
    )

    attn_sum = z_scatter(attn_terms)

    def output_stage(down_even, down_odd, mlp_sum):
        (grad_down,), mine = together(
            work(lambda: put_rows(down_even, down_odd, place_arg)), near_chain(mlp_sum)
        )
        return grad_down, mine

    grad_down, mine = stage(sure, output_stage, down_even, down_odd, after(mlp_sum, attn_terms))

    def last_stage(mine, mlp_sum, mlp_own, attn_sum, attn_own):
        def columns_put():
            halves_all, filled = (mine, swap(mine, 1)), ()
            for part in range(4):
                filled = put_columns(*halves_all, place_arg, shards, part, 4, filled)
                if part:
                    filled = yield filled
            return filled

        def sums_chain():
            pairs = ((attn_sum[:, :-out_cols], attn_own[:, :-out_cols]), (mlp_sum, mlp_own))
            sums = [jnp.sum(a.astype(wide) * b.astype(wide), axis=1) for a, b in pairs]
            sums, mask = jnp.stack(sums), 1
            while mask < groups:
                sums = sums + (yield swap(sums, mask))
                mask *= 2
            return sums

        puts, attn_pieces, sums = together(columns_put(), pieces_chain(attn_sum), sums_chain())
        return *puts, sums, *put_attention(*attn_pieces, place_arg, q_cols, out_cols)

    grad_gate, grad_up, row_sums, grad_query, grad_key, grad_value, grad_out = stage(
        sure, last_stage, mine, mlp_sum, mlp_own, after(attn_sum, grad_down), attn_own
    )
    return (
        layer_out[None],
        grad_stream[None],
        grad_query,
        grad_key,
        grad_value,
        grad_out,
        row_sums[0] / gain_attn.astype(wide),
        grad_gate,
        grad_up,
        grad_down,
        row_sums[1] / gain_mlp.astype(wide),
    )


def solution(mesh):
    placed = (
        P("fsdp", "seq", None),
        P("fsdp", "seq"),
        P("fsdp", None),
        P("fsdp", None),
        P("fsdp", None),
        P("fsdp", None),
        P("fsdp"),
        P("fsdp", None),
        P("fsdp", None),
        P("fsdp", None),
        P("fsdp"),
        P("fsdp", "seq", None),
    )
    return jax.shard_map(
        on_device,
        mesh=mesh,
        in_specs=placed,
        out_specs=(
            P("fsdp", "seq", None),
            P("fsdp", "seq", None),
            P("fsdp", None),
            P("fsdp", None),
            P("fsdp", None),
            P("fsdp", None),
            P("fsdp"),
            P("fsdp", None),
            P("fsdp", None),
            P("fsdp", None),
            P("fsdp"),
        ),
        check_vma=False,
    )
```
